32 devices in a mesh: space: 2 (over y), vel: 16 (over z, x, core).
Axes of the slice: x: 2, y: 2, z: 4, core: 2. Of those that a mesh axis runs over, the one named last changes fastest.
Arguments:
- dist: float32 [256, 32768], P('space', 'vel'), as said below
- wall_temp: float32 [256], P('space'), may hold values from 0.6 to 1.5
- neighbours: int32 [6, 256], P(None, 'space'), may hold values from 0 to 255, as said below
- wall_mask: int32 [6, 256], P(None, 'space'), may hold values from 0 to 1, as said below
- face_rows: int32 [2, 2, 64], P('space'), may hold values from 0 to 127, as said below
Outputs:
- dist_out: float32 [256, 32768], P('space', 'vel')
The draws below stay inside these ranges and needn't reach their ends.
Inputs may be any that keep to these rules, and one draw needn't show every extreme that they name: `dist`: strictly positive. Each block b holds the 2 x-planes b * 2 to (b + 1) * 2 - 1 of a periodic grid of 4 x 8 x 8 cells, its cells in some order; neighbours[k, c] is the cell across face k, periodic along x, and the cell itself across the channel's four side walls. `wall_mask`: all faces on the channel's four sides are walls, and x faces of solid screen elements, on both cells that share them. face_rows[b, 0, j] and face_rows[b, 1, j] are rows within block b, counted from 0, of its cells on its lowest and highest x-plane at the same position j across the channel, so the cell at face_rows[b, 1, j] has as +x neighbour the cell at face_rows[(b + 1) mod 2, 0, j] of the next block.
All inputs are finite; a program needn't handle non-finite values.
Results may differ from the reference program's by a relative error of at most 0.0003.
Values sent between devices are 32-bit elements; how exact they have to be, the bound alone decides.
No kernel may reach another device: no remote copies, remote signals or barrier semaphores. Data moves between devices by JAX's collectives and lax.ppermute only.
A program may use at most 64 MiB of HBM per device.

```python
import math
import jax
import jax.numpy as jnp
from jax import lax

NV = 32
VEL = 32768
CXL = 2
GY = 8
GZ = 8
STEPS = 1
FACE = 64
CELL_DEV = 128
BLOCKS = 2
MESH_SITE_COUNT = 256


LIMIT = 4.5


def cell_layout(key):
    layout_key = jax.random.fold_in(key, 7101)
    fresh_stochastic_seeds = jax.random.split(layout_key, BLOCKS)
    orders = jax.vmap(lambda subkey: jax.random.permutation(subkey, CELL_DEV))(fresh_stochastic_seeds).astype(jnp.int32)
    inverse = jnp.argsort(orders, axis=1, stable=True).astype(jnp.int32)
    return (orders, inverse)


def grid_position(orders):
    block_id = jnp.arange(BLOCKS, dtype=jnp.int32)[:, None]
    plane = orders // FACE
    along_y = orders // GZ % GY
    along_z = orders % GZ
    along_x = block_id * CXL + plane
    return (along_x, along_y, along_z)


def draw_neighbours(key, part):
    orders, inverse = cell_layout(key)
    along_x, along_y, along_z = grid_position(orders)
    total_x = BLOCKS * CXL

    def global_row(grid_x, grid_y, grid_z):
        grid_x = grid_x % total_x
        owner_block = grid_x // CXL
        position = (grid_x % CXL * GY + jnp.clip(grid_y, 0, GY - 1)) * GZ + jnp.clip(grid_z, 0, GZ - 1)
        return owner_block * CELL_DEV + inverse[owner_block, position]
    itself = global_row(along_x, along_y, along_z)
    lower_x = global_row(along_x - 1, along_y, along_z)
    upper_x = global_row(along_x + 1, along_y, along_z)
    lower_y = jnp.where(along_y > 0, global_row(along_x, along_y - 1, along_z), itself)
    upper_y = jnp.where(along_y < GY - 1, global_row(along_x, along_y + 1, along_z), itself)
    lower_z = jnp.where(along_z > 0, global_row(along_x, along_y, along_z - 1), itself)
    upper_z = jnp.where(along_z < GZ - 1, global_row(along_x, along_y, along_z + 1), itself)
    stacked = jnp.stack([lower_x, upper_x, lower_y, upper_y, lower_z, upper_z], axis=0)
    return stacked.reshape(6, MESH_SITE_COUNT).astype(jnp.int32)


def draw_wall_mask(key, part):
    orders, inverse = cell_layout(key)
    along_x, along_y, along_z = grid_position(orders)
    total_x = BLOCKS * CXL
    screen_key = jax.random.fold_in(key, 7202)
    screen = (jax.random.randint(screen_key, (total_x, GY, GZ), 0, 4) == 0).astype(jnp.int32)
    lower_x = screen[(along_x - 1) % total_x, along_y, along_z]
    upper_x = screen[along_x, along_y, along_z]
    lower_y = (along_y == 0).astype(jnp.int32)
    upper_y = (along_y == GY - 1).astype(jnp.int32)
    lower_z = (along_z == 0).astype(jnp.int32)
    upper_z = (along_z == GZ - 1).astype(jnp.int32)
    stacked = jnp.stack([lower_x, upper_x, lower_y, upper_y, lower_z, upper_z], axis=0)
    return stacked.reshape(6, MESH_SITE_COUNT).astype(jnp.int32)


def draw_face_rows(key, part):
    orders, inverse = cell_layout(key)
    low_face = inverse[:, :FACE]
    high_face = inverse[:, (CXL - 1) * FACE:CXL * FACE]
    return jnp.stack([low_face, high_face], axis=1).astype(jnp.int32)


def draw_dist(key, part):
    fresh_stochastic_seeds = jax.random.split(jax.random.fold_in(key, 7303), 5)
    vel_index = jnp.arange(VEL, dtype=jnp.int32)
    spacing = 2.0 * LIMIT / NV
    vel_x = -LIMIT + ((vel_index // NV % NV).astype(jnp.float32) + 0.5) * spacing
    vel_y = -LIMIT + ((vel_index // (NV * NV)).astype(jnp.float32) + 0.5) * spacing
    vel_z = -LIMIT + ((vel_index % NV).astype(jnp.float32) + 0.5) * spacing
    particle_count_per_volume = jnp.exp(jax.random.uniform(fresh_stochastic_seeds[0], (MESH_SITE_COUNT, 1), minval=math.log(0.5), maxval=math.log(2.0)))
    site_kelvin = jax.random.uniform(fresh_stochastic_seeds[1], (MESH_SITE_COUNT, 1), minval=0.7, maxval=1.4)
    drift = jnp.clip(0.3 * jax.random.normal(fresh_stochastic_seeds[2], (MESH_SITE_COUNT, 3)), -0.9, 0.9)
    startup_disturbance = 0.35 * jnp.clip(jax.random.normal(fresh_stochastic_seeds[3], (MESH_SITE_COUNT, VEL)), -1.0, 1.0)
    rel_x = vel_x[None, :] - drift[:, 0:1]
    rel_y = vel_y[None, :] - drift[:, 1:2]
    rel_z = vel_z[None, :] - drift[:, 2:3]
    peculiar_motion_norm = rel_x * rel_x + rel_y * rel_y + rel_z * rel_z
    drawn_samples = particle_count_per_volume * site_kelvin ** (-1.5) * jnp.exp(-peculiar_motion_norm / (2.0 * site_kelvin)) * (1.0 + startup_disturbance)
    return drawn_samples.astype(jnp.float32)


def block_scale(stream_key, shape, shards, least, high):
    gain, own = 1.0, jax.random.fold_in(stream_key, 6)
    for axis_at, parts in shards:
        heights = jnp.exp(jax.random.uniform(jax.random.fold_in(own, axis_at), (parts,), jnp.float32, least / len(shards), high / len(shards)))
        gain = gain * jnp.repeat(heights, shape[axis_at] // parts).reshape([-1 if axis == axis_at else 1 for axis in range(len(shape))])
    return gain


def setup_inputs(seed: int = 0) -> dict:
    seeds = jax.random.split(jax.random.key(seed), 6)
    dist = draw_dist(jax.random.fold_in(seeds[5], 71), 0)
    wall_temp = jnp.clip(0.6 + 0.9 * jax.random.uniform(seeds[1], (MESH_SITE_COUNT,), jnp.float32) ** block_scale(seeds[1], (MESH_SITE_COUNT,), ((0, 2),), -0.2, 0.2), 0.6, 1.5)
    neighbours = draw_neighbours(jax.random.fold_in(seeds[5], 71), 0)
    wall_mask = draw_wall_mask(jax.random.fold_in(seeds[5], 71), 0)
    face_rows = draw_face_rows(jax.random.fold_in(seeds[5], 71), 0)
    return dict(dist=dist, wall_temp=wall_temp, neighbours=neighbours, wall_mask=wall_mask, face_rows=face_rows)


LIMIT = 4.5
TIME_STEP = 0.05
BASELINE_SHEAR = 0.1
SHEAR_EXPONENT = 0.66
MOMENTUM_RATIO = 2.0 / 3.0


def velocity_table(first_vel, vel_count):
    vel_index = first_vel + jnp.arange(vel_count, dtype=jnp.int32)
    spacing = 2.0 * LIMIT / NV

    def coordinate(slot):
        return -LIMIT + (slot.astype(jnp.float32) + 0.5) * spacing

    vel_x = coordinate((vel_index // NV) % NV)
    vel_y = coordinate(vel_index // (NV * NV))
    vel_z = coordinate(vel_index % NV)
    return vel_x, vel_y, vel_z


def quad_weight():
    spacing = 2.0 * LIMIT / NV
    return spacing ** 3 * (2.0 * math.pi) ** -1.5


def normal_speeds(vel_x, vel_y, vel_z):
    return [-vel_x, vel_x, -vel_y, vel_y, -vel_z, vel_z]


def moment_table(vel_x, vel_y, vel_z, weight):
    speed_sq = vel_x * vel_x + vel_y * vel_y + vel_z * vel_z
    columns = [jnp.ones_like(vel_x), vel_x, vel_y, vel_z, vel_x * vel_x, vel_y * vel_y, vel_z * vel_z,
               vel_x * vel_y, vel_x * vel_z, vel_y * vel_z, vel_x * speed_sq, vel_y * speed_sq, vel_z * speed_sq]
    return weight * jnp.stack(columns, axis=1)


def reflect_table(speeds, weight):
    return weight * jnp.stack([jnp.maximum(normal_speed, 0.0) for normal_speed in speeds], axis=1)


def collide(current, moment_sums, vel_x, vel_y, vel_z):
    particle_count_per_volume = moment_sums[:, 0]
    flow_x = moment_sums[:, 1] / particle_count_per_volume
    flow_y = moment_sums[:, 2] / particle_count_per_volume
    flow_z = moment_sums[:, 3] / particle_count_per_volume
    press_xx = moment_sums[:, 4]
    press_yy = moment_sums[:, 5]
    press_zz = moment_sums[:, 6]
    press_xy = moment_sums[:, 7]
    press_xz = moment_sums[:, 8]
    press_yz = moment_sums[:, 9]
    internal_agitation = press_xx + press_yy + press_zz
    bulk_motion_norm = flow_x * flow_x + flow_y * flow_y + flow_z * flow_z
    site_kelvin = (internal_agitation / particle_count_per_volume - bulk_motion_norm) / 3.0
    heat_x = 0.5 * (moment_sums[:, 10] - 2.0 * (press_xx * flow_x + press_xy * flow_y + press_xz * flow_z)
                    - flow_x * internal_agitation + 2.0 * particle_count_per_volume * flow_x * bulk_motion_norm)
    heat_y = 0.5 * (moment_sums[:, 11] - 2.0 * (press_xy * flow_x + press_yy * flow_y + press_yz * flow_z)
                    - flow_y * internal_agitation + 2.0 * particle_count_per_volume * flow_y * bulk_motion_norm)
    heat_z = 0.5 * (moment_sums[:, 12] - 2.0 * (press_xz * flow_x + press_yz * flow_y + press_zz * flow_z)
                    - flow_z * internal_agitation + 2.0 * particle_count_per_volume * flow_z * bulk_motion_norm)
    rel_x = vel_x[None, :] - flow_x[:, None]
    rel_y = vel_y[None, :] - flow_y[:, None]
    rel_z = vel_z[None, :] - flow_z[:, None]
    peculiar_motion_norm = rel_x * rel_x + rel_y * rel_y + rel_z * rel_z
    kelvin_vertical_array = site_kelvin[:, None]
    maxwellian_target = (particle_count_per_volume * site_kelvin ** -1.5)[:, None] * jnp.exp(-peculiar_motion_norm / (2.0 * kelvin_vertical_array))
    peculiar_conduction = rel_x * heat_x[:, None] + rel_y * heat_y[:, None] + rel_z * heat_z[:, None]
    conduction_scale = (1.0 - MOMENTUM_RATIO) / (5.0 * particle_count_per_volume * site_kelvin ** 2)
    kinetic_bgk_variant = maxwellian_target * (1.0 + conduction_scale[:, None] * peculiar_conduction * (peculiar_motion_norm / kelvin_vertical_array - 5.0))
    collision_rate_inverse_time = particle_count_per_volume * site_kelvin ** (1.0 - SHEAR_EXPONENT) / BASELINE_SHEAR
    return (kinetic_bgk_variant - current) * collision_rate_inverse_time[:, None]


def stream_term(own_rows, extended, index_list, wall_mask, wall_scale, wall_shape, speeds):
    stream_sum = jnp.zeros_like(own_rows)
    for direction in range(6):
        normal_speed = speeds[direction][None, :]
        beside = jnp.take(extended, index_list[direction], axis=0)
        wall_value = wall_scale[:, direction:direction + 1] * wall_shape
        inflow = jnp.where(wall_mask[direction][:, None] == 1, wall_value, beside)
        stream_sum = stream_sum - normal_speed * jnp.where(normal_speed > 0, own_rows, inflow)
    return stream_sum


def reference(dist, wall_temp, neighbours, wall_mask, face_rows):
    vel_x, vel_y, vel_z = velocity_table(0, VEL)
    weight = quad_weight()
    speeds = normal_speeds(vel_x, vel_y, vel_z)
    moments_tab = moment_table(vel_x, vel_y, vel_z, weight)
    reflect_tab = reflect_table(speeds, weight)
    speed_sq = vel_x * vel_x + vel_y * vel_y + vel_z * vel_z
    norm_weight = weight * jnp.maximum(vel_x, 0.0)

    def rate(current):
        def one_block(block_id):
            first_row = block_id * CELL_DEV
            own_rows = lax.dynamic_slice_in_dim(current, first_row, CELL_DEV, 0)
            temps = lax.dynamic_slice_in_dim(wall_temp, first_row, CELL_DEV, 0)
            near = lax.dynamic_slice_in_dim(neighbours, first_row, CELL_DEV, 1)
            walls = lax.dynamic_slice_in_dim(wall_mask, first_row, CELL_DEV, 1)
            before = (block_id - 1) % BLOCKS
            after = (block_id + 1) % BLOCKS
            own_faces = face_rows[block_id]
            index_list = [near[direction] for direction in range(6)]
            index_list[0] = index_list[0].at[own_faces[0]].set(before * CELL_DEV + face_rows[before, 1])
            index_list[1] = index_list[1].at[own_faces[1]].set(after * CELL_DEV + face_rows[after, 0])
            wall_shape = jnp.exp(-speed_sq[None, :] / (2.0 * temps[:, None]))
            wall_norm = jnp.dot(wall_shape, norm_weight, precision=lax.Precision.HIGHEST)
            moment_sums = jnp.dot(own_rows, moments_tab, precision=lax.Precision.HIGHEST)
            outflow = jnp.dot(own_rows, reflect_tab, precision=lax.Precision.HIGHEST)
            wall_scale = outflow / wall_norm[:, None]
            running = stream_term(own_rows, current, index_list, walls, wall_scale, wall_shape, speeds)
            return running + collide(own_rows, moment_sums, vel_x, vel_y, vel_z)

        return lax.map(one_block, jnp.arange(BLOCKS, dtype=jnp.int32)).reshape(MESH_SITE_COUNT, VEL)

    current = dist
    for repeat in range(STEPS):
        slope_one = rate(current)
        middle = current + TIME_STEP * slope_one
        slope_two = rate(middle)
        current = current + (0.5 * TIME_STEP) * (slope_one + slope_two)
    return current
```

```python
import functools
import math

import jax
import jax.numpy as jnp
from jax import lax
from jax.experimental import pallas as pl
from jax.experimental.pallas import tpu as pltpu
from jax.sharding import PartitionSpec as P

NV = 32
LIMIT = 4.5
SPACING = 2.0 * LIMIT / NV
WEIGHT = SPACING**3 * (2.0 * math.pi) ** (-1.5)
TIME_STEP = 0.05
BASELINE_SHEAR = 0.1
SHEAR_EXPONENT = 0.66
MOMENTUM_RATIO = 2.0 / 3.0
PLANE = NV * NV
HALF = PLANE // 2
ROWS = 8
COLUMN_TILE = 256
SUMS = 16
F32 = jnp.float32
BF16 = jnp.bfloat16


def point(slot):
    return -LIMIT + (slot.astype(F32) + 0.5) * SPACING


def lane_table(first, start, width):
    lane = lax.broadcasted_iota(jnp.int32, (1, width), 1) + start
    vel = first + lane
    vel_x = point((lane >> 5) & (NV - 1))
    vel_y = point(vel >> 10)
    vel_z = point(lane & (NV - 1))
    return vel_x, vel_y, vel_z


def first_vel(width):
    return lax.axis_index("vel") * width


def split(value, count):
    pieces = []
    for _ in range(count - 1):
        piece = value.astype(BF16)
        pieces.append(piece)
        value = value - piece.astype(F32)
    pieces.append(value.astype(BF16))
    return pieces


def dot(left, right, dims=((1,), (0,))):
    return lax.dot_general(left, right, (dims, ((), ())), preferred_element_type=F32)


def sums_of(values, vel_x, vel_y, vel_z):
    speed_sq = vel_x * vel_x + vel_y * vel_y + vel_z * vel_z
    table = WEIGHT * jnp.concatenate(
        [
            jnp.ones_like(vel_x),
            vel_x * vel_x,
            vel_y * vel_y,
            vel_z * vel_z,
            vel_x * vel_y,
            vel_x * vel_z,
            vel_y * vel_z,
            vel_x * speed_sq,
            vel_y * speed_sq,
            vel_z * speed_sq,
            jnp.maximum(-vel_x, 0.0),
            jnp.maximum(vel_x, 0.0),
            jnp.maximum(-vel_y, 0.0),
            jnp.maximum(vel_y, 0.0),
            jnp.maximum(-vel_z, 0.0),
            jnp.maximum(vel_z, 0.0),
        ],
        axis=0,
    )
    tables = split(table, 3)
    pieces = split(values, 3)
    stacked = jnp.concatenate(tables, axis=0)
    total = None
    for order, piece in enumerate(pieces):
        part = dot(stacked[: (3 - order) * SUMS], piece, ((1,), (1,)))
        for at in range(3 - order):
            term = part[at * SUMS : (at + 1) * SUMS]
            total = term if total is None else total + term
    return total


def half_slices(width):
    low, high = [], []
    for plane in range(width // PLANE):
        low.append((plane * PLANE, plane * HALF))
        high.append((plane * PLANE + HALF, plane * HALF))
    return low, high


def start_kernel(rows_ref, dist_ref, send_ref, sums_ref):
    cells, width = dist_ref.shape
    count = cells // 2
    low, high = half_slices(width)

    def move(at, _):
        low_row = rows_ref[0, 0, at]
        high_row = rows_ref[0, 1, at]
        for source, target in high:
            send_ref[pl.ds(at, 1), target : target + HALF] = dist_ref[
                pl.ds(high_row, 1), source : source + HALF
            ]
        for source, target in low:
            send_ref[pl.ds(count + at, 1), target : target + HALF] = dist_ref[
                pl.ds(low_row, 1), source : source + HALF
            ]
        return 0

    lax.fori_loop(0, count, move, 0, unroll=4)
    vel_x, vel_y, vel_z = lane_table(first_vel(width), 0, width)
    sums_ref[...] = sums_of(dist_ref[...], vel_x, vel_y, vel_z)


def picks(near_ref, mask_ref, face, cell_start, cells):
    index = near_ref[face : face + 1, :] - cell_start
    hit = lax.broadcasted_iota(jnp.int32, (cells, cells), 0) == index
    open_face = mask_ref[face : face + 1, :] != 1
    return jnp.where(hit & open_face, 1.0, 0.0).astype(F32)


def stream_kernel(near_ref, mask_ref, dist_ref, out_ref):
    stream_body(near_ref, mask_ref, dist_ref, None, out_ref)


def stream_last_kernel(near_ref, mask_ref, dist_ref, middle_ref, out_ref):
    stream_body(near_ref, mask_ref, middle_ref, dist_ref, out_ref)


def stream_body(near_ref, mask_ref, value_ref, dist_ref, out_ref):
    cells, width = value_ref.shape
    first = first_vel(width)
    cell_start = lax.axis_index("space") * cells
    upward = first >= (NV // 2) * PLANE
    faces = [picks(near_ref, mask_ref, face, cell_start, cells) for face in range(6)]
    along_y = jnp.where(upward, faces[2], faces[3])
    chosen = []
    for face in (faces[0], faces[1], along_y, faces[4], faces[5]):
        flipped = face.T.astype(BF16)
        chosen.append(jnp.concatenate([flipped, flipped], axis=1))
    rest = jnp.concatenate(chosen[2:], axis=0)
    for start in range(0, width, COLUMN_TILE):
        side = chosen[0] if start % PLANE >= HALF else chosen[1]
        vel_x, vel_y, vel_z = lane_table(first, start, COLUMN_TILE)
        values = value_ref[:, start : start + COLUMN_TILE]
        pieces = jnp.concatenate(split(values, 2), axis=0)
        moved = dot(jnp.concatenate([side, rest], axis=0), pieces)
        speed_x, speed_y, speed_z = jnp.abs(vel_x), jnp.abs(vel_y), jnp.abs(vel_z)
        from_z = jnp.where(vel_z > 0, moved[2 * cells : 3 * cells], moved[3 * cells :])
        stream = (
            speed_x * moved[:cells]
            + speed_y * moved[cells : 2 * cells]
            + speed_z * from_z
            - (speed_x + speed_y + speed_z) * values
        )
        if dist_ref is None:
            out_ref[:, start : start + COLUMN_TILE] = stream
        else:
            out_ref[:, start : start + COLUMN_TILE] = (
                0.5 * (dist_ref[:, start : start + COLUMN_TILE] + values)
                + (0.5 * TIME_STEP) * stream
            )


def columns_of(sums, wall_temp, mask, upward):
    count = sums[0:1]
    inv_count = 1.0 / count
    flow_x = (sums[11:12] - sums[10:11]) * inv_count
    flow_y = (sums[13:14] - sums[12:13]) * inv_count
    flow_z = (sums[15:16] - sums[14:15]) * inv_count
    p_xx, p_yy, p_zz, p_xy, p_xz, p_yz = (sums[at : at + 1] for at in range(1, 7))
    energy = p_xx + p_yy + p_zz
    flow_sq = flow_x * flow_x + flow_y * flow_y + flow_z * flow_z
    temp = (energy * inv_count - flow_sq) / 3.0
    inv_temp = 1.0 / temp

    def heat(third, flow, press):
        return 0.5 * (
            third
            - 2.0 * (press[0] * flow_x + press[1] * flow_y + press[2] * flow_z)
            - flow * energy
            + 2.0 * count * flow * flow_sq
        )

    scale = ((1.0 - MOMENTUM_RATIO) / 5.0) * inv_count * inv_temp * inv_temp
    heat_x = scale * heat(sums[7:8], flow_x, (p_xx, p_xy, p_xz))
    heat_y = scale * heat(sums[8:9], flow_y, (p_xy, p_yy, p_yz))
    heat_z = scale * heat(sums[9:10], flow_z, (p_xz, p_yz, p_zz))
    peak = count * inv_temp * lax.rsqrt(temp)
    rate = count * jnp.exp((1.0 - SHEAR_EXPONENT) * jnp.log(temp)) * (1.0 / BASELINE_SHEAR)
    axis_point = point(lax.broadcasted_iota(jnp.int32, (NV, 1), 0))
    cooling = -0.5 / wall_temp
    profile = jnp.exp(axis_point * axis_point * cooling)
    mass = jnp.sum(profile, axis=0, keepdims=True)
    flux = jnp.sum(jnp.maximum(axis_point, 0.0) * profile, axis=0, keepdims=True)
    inv_norm = 1.0 / (WEIGHT * flux * mass * mass)
    back = [
        jnp.where(mask[face : face + 1] == 1, sums[10 + face : 11 + face] * inv_norm, 0.0)
        for face in range(6)
    ]
    rows = [
        flow_x,
        flow_y,
        flow_z,
        inv_temp,
        heat_x,
        heat_y,
        heat_z,
        peak,
        rate,
        cooling,
        back[0],
        back[1],
        jnp.where(upward, back[2], back[3]),
        back[4],
        back[5],
    ]
    cells = count.shape[1]
    rows.append(jnp.zeros((128 - len(rows), cells), F32))
    return jnp.concatenate(rows, axis=0).T


def local_rate(columns, values, vel_x, vel_y, vel_z):
    def column(at):
        return columns[:, at : at + 1]

    rel_x = vel_x - column(0)
    rel_y = vel_y - column(1)
    rel_z = vel_z - column(2)
    ratio = (rel_x * rel_x + rel_y * rel_y + rel_z * rel_z) * column(3)
    conduction = rel_x * column(4) + rel_y * column(5) + rel_z * column(6)
    target = column(7) * jnp.exp(-0.5 * ratio) * (1.0 + conduction * (ratio - 5.0))
    speed_sq = vel_x * vel_x + vel_y * vel_y + vel_z * vel_z
    shape = jnp.exp(speed_sq * column(9))
    back = (
        jnp.maximum(vel_x, 0.0) * column(10)
        + jnp.maximum(-vel_x, 0.0) * column(11)
        + jnp.abs(vel_y) * column(12)
        + jnp.maximum(vel_z, 0.0) * column(13)
        + jnp.maximum(-vel_z, 0.0) * column(14)
    )
    return (target - values) * column(8) + shape * back


def middle_kernel(
    rows_ref, temp_ref, mask_ref, sums_ref, dist_ref, stream_ref, out_ref, send_ref, columns_ref
):
    cells, width = dist_ref.shape
    count = cells // 2
    first = first_vel(width)
    low, high = half_slices(width)
    upward = first >= (NV // 2) * PLANE
    columns_ref[...] = columns_of(sums_ref[...], temp_ref[...], mask_ref[...], upward)

    def group(at, _):
        rows = pl.ds(pl.multiple_of(at * ROWS, ROWS), ROWS)
        columns = columns_ref[rows, :]
        vel_x, vel_y, vel_z = lane_table(first, 0, width)
        values = dist_ref[rows, :]
        rate = stream_ref[rows, :] + local_rate(columns, values, vel_x, vel_y, vel_z)
        out_ref[rows, :] = values + TIME_STEP * rate
        return 0

    lax.fori_loop(0, cells // ROWS, group, 0)

    def move(at, _):
        low_row = rows_ref[0, 0, at]
        high_row = rows_ref[0, 1, at]
        for source, target in high:
            send_ref[pl.ds(at, 1), target : target + HALF] = out_ref[
                pl.ds(high_row, 1), source : source + HALF
            ]
        for source, target in low:
            send_ref[pl.ds(count + at, 1), target : target + HALF] = out_ref[
                pl.ds(low_row, 1), source : source + HALF
            ]
        return 0

    lax.fori_loop(0, count, move, 0, unroll=4)


def halo_picks(face_ref, mask_ref, cells):
    count = cells // 2
    mask = jnp.concatenate(
        [mask_ref[...].astype(F32), jnp.zeros((128 - mask_ref.shape[0], cells), F32)], axis=0
    ).T
    row = lax.broadcasted_iota(jnp.int32, (cells, count), 0)
    sides = []
    for face in (1, 0):
        hit = (row == face_ref[0, face : face + 1, :]) & (mask[:, face : face + 1] != 1.0)
        side = jnp.where(hit, 1.0, 0.0).astype(BF16)
        sides.append(jnp.concatenate([side, side], axis=1))
    return sides


def halo_part(halo_refs, side, start, count):
    lanes = slice(start, start + COLUMN_TILE)
    if len(halo_refs) == 1:
        rows = halo_refs[0][(1 - side) * count : (2 - side) * count, lanes]
    else:
        rows = halo_refs[1 - side][:, lanes]
    return jnp.concatenate(split(rows, 2), axis=0)


def join_kernel(face_ref, mask_ref, part_ref, *refs):
    halo_refs, (out_ref, sums_ref) = refs[:-2], refs[-2:]
    cells, width = part_ref.shape
    count = cells // 2
    sides = halo_picks(face_ref, mask_ref, cells)
    first = first_vel(width)
    for side, ranges in enumerate(half_slices(width)):
        for source, target in ranges:
            for step in range(0, HALF, COLUMN_TILE):
                lanes = slice(source + step, source + step + COLUMN_TILE)
                vel_x, _, _ = lane_table(first, source + step, COLUMN_TILE)
                halo = dot(sides[side], halo_part(halo_refs, side, target + step, count))
                out_ref[:, lanes] = part_ref[:, lanes] + (TIME_STEP * jnp.abs(vel_x)) * halo
    vel_x, vel_y, vel_z = lane_table(first, 0, width)
    sums_ref[...] = sums_of(out_ref[...], vel_x, vel_y, vel_z)


def last_kernel(face_ref, temp_ref, mask_ref, sums_ref, middle_ref, part_ref, *refs):
    halo_refs, (out_ref, columns_ref) = refs[:-2], refs[-2:]
    cells, width = part_ref.shape
    count = cells // 2
    first = first_vel(width)
    upward = first >= (NV // 2) * PLANE
    columns_ref[...] = columns_of(sums_ref[...], temp_ref[...], mask_ref[...], upward)

    def group(at, _):
        rows = pl.ds(pl.multiple_of(at * ROWS, ROWS), ROWS)
        columns = columns_ref[rows, :]
        vel_x, vel_y, vel_z = lane_table(first, 0, width)
        rate = local_rate(columns, middle_ref[rows, :], vel_x, vel_y, vel_z)
        out_ref[rows, :] = part_ref[rows, :] + (0.5 * TIME_STEP) * rate
        return 0

    lax.fori_loop(0, cells // ROWS, group, 0)
    sides = halo_picks(face_ref, mask_ref, cells)
    for side, ranges in enumerate(half_slices(width)):
        for source, target in ranges:
            for step in range(0, HALF, COLUMN_TILE):
                lanes = slice(source + step, source + step + COLUMN_TILE)
                vel_x, _, _ = lane_table(first, source + step, COLUMN_TILE)
                halo = dot(sides[side], halo_part(halo_refs, side, target + step, count))
                out_ref[:, lanes] = out_ref[:, lanes] + (0.5 * TIME_STEP * jnp.abs(vel_x)) * halo


def call(kernel, outs, scalars, arrays, scratch=(), flops=0):
    specs = [pl.BlockSpec(memory_space=pltpu.SMEM)] * len(scalars)
    specs += [pl.BlockSpec(memory_space=pltpu.VMEM)] * len(arrays)
    size = sum(math.prod(array.shape) * 4 for array in arrays)
    return pl.pallas_call(
        kernel,
        out_shape=[jax.ShapeDtypeStruct(shape, F32) for shape in outs],
        in_specs=specs,
        out_specs=[pl.BlockSpec(memory_space=pltpu.VMEM)] * len(outs),
        scratch_shapes=list(scratch),
        compiler_params=pltpu.CompilerParams(vmem_limit_bytes=40 * 2**20),
        cost_estimate=pl.CostEstimate(flops=flops, bytes_accessed=size, transcendentals=0),
    )(*scalars, *arrays)


def total(value):
    count = lax.axis_size("vel")
    step = 1
    while step < count:
        value = value + lax.ppermute(value, "vel", [(i, i ^ step) for i in range(count)])
        step *= 2
    return value


def exchange(send):
    count = lax.axis_size("space")
    forward = [(i, (i + 1) % count) for i in range(count)]
    backward = [(target, source) for source, target in forward]
    if count == 2:
        return [lax.ppermute(send, "space", forward)]
    half = send.shape[0] // 2
    return [
        lax.ppermute(send[:half], "space", forward),
        lax.ppermute(send[half:], "space", backward),
    ]


def on_device(dist, wall_temp, neighbours, wall_mask, face_rows):
    cells, width = dist.shape
    temp = wall_temp[None, :]
    whole, sums, send = (cells, width), (SUMS, cells), (cells, width // 2)
    column_scratch = [pltpu.VMEM((cells, 128), F32)]

    sent, own_sums = call(start_kernel, [send, sums], [face_rows], [dist])
    halo = exchange(sent)
    (stream,) = call(stream_kernel, [whole], [], [neighbours, wall_mask, dist])
    sums_one = total(own_sums)
    part, sent = call(
        middle_kernel,
        [whole, send],
        [face_rows],
        [temp, wall_mask, sums_one, dist, stream],
        column_scratch,
    )
    halo_two = exchange(sent)
    middle, own_sums = call(join_kernel, [whole, sums], [], [face_rows, wall_mask, part, *halo])
    (part,) = call(stream_last_kernel, [whole], [], [neighbours, wall_mask, dist, middle])
    sums_two = total(own_sums)
    (result,) = call(
        last_kernel,
        [whole],
        [],
        [face_rows, temp, wall_mask, sums_two, middle, part, *halo_two],
        column_scratch,
    )
    return result


def solution(mesh):
    return jax.shard_map(
        on_device,
        mesh=mesh,
        in_specs=(
            P("space", "vel"),
            P("space"),
            P(None, "space"),
            P(None, "space"),
            P("space", None, None),
        ),
        out_specs=P("space", "vel"),
        check_vma=False,
    )
```

```python
import math

import jax
import jax.numpy as jnp
from jax import lax
from jax.experimental import pallas as pl
from jax.experimental.pallas import tpu as pltpu
from jax.sharding import PartitionSpec as P

NV = 32
LIMIT = 4.5
SPACING = 2.0 * LIMIT / NV
WEIGHT = SPACING**3 * (2.0 * math.pi) ** (-1.5)
TIME_STEP = 0.05
BASELINE_SHEAR = 0.1
SHEAR_EXPONENT = 0.66
MOMENTUM_RATIO = 2.0 / 3.0
PLANE = NV * NV
HALF = PLANE // 2
ROWS = 8
LANES = 128
COLUMN_TILE = 256
SUMS = 16
LOG2E = math.log2(math.e)
F32 = jnp.float32
BF16 = jnp.bfloat16


def point(slot):
    return -LIMIT + (slot.astype(F32) + 0.5) * SPACING


def lane_points(start, width):
    lane = lax.broadcasted_iota(jnp.int32, (1, width), 1) + start
    return point((lane >> 5) & (NV - 1)), point(lane & (NV - 1))


def planes_y(width):
    planes = width // PLANE
    first = lax.axis_index("vel") * planes
    return [point(first + at) for at in range(planes)], first >= NV // 2


def split(value, count):
    pieces = []
    for _ in range(count - 1):
        piece = value.astype(BF16)
        pieces.append(piece)
        value = value - piece.astype(F32)
    pieces.append(value.astype(BF16))
    return pieces


def dot(left, right, dims=((1,), (0,))):
    return lax.dot_general(left, right, (dims, ((), ())), preferred_element_type=F32)


def sum_table():
    lane = lax.broadcasted_iota(jnp.int32, (1, PLANE), 1)
    at_x = (2 * ((lane >> 5) & (NV - 1)) - (NV - 1)).astype(F32)
    at_z = (2 * (lane & (NV - 1)) - (NV - 1)).astype(F32)
    square = at_x * at_x + at_z * at_z
    rows = [
        jnp.ones_like(at_x),
        jnp.maximum(at_x, 0.0),
        jnp.maximum(-at_x, 0.0),
        jnp.maximum(at_z, 0.0),
        jnp.maximum(-at_z, 0.0),
        at_x * at_x,
        at_z * at_z,
        at_x * at_z,
        at_x * square,
        at_z * square,
    ]
    rows.append(jnp.zeros((SUMS - len(rows), PLANE), F32))
    return jnp.concatenate(split(jnp.concatenate(rows, axis=0), 2), axis=0)


def plane_sums(table_ref, value_ref, start, stop):
    width = value_ref.shape[1]
    parts = [value_ref[:, plane + start : plane + stop] for plane in range(0, width, PLANE)]
    values = jnp.concatenate(parts, axis=0)
    table = table_ref[:, start:stop]
    total = None
    for piece in split(values, 3):
        part = dot(table, piece, ((1,), (1,)))
        total = part if total is None else total + part
    return total[:SUMS] + total[SUMS:]


def sums_of(found, width):
    planes, upward = planes_y(width)
    cells = found.shape[1] // len(planes)
    unit = SPACING / 2
    count = up = xx = yy = zz = xy = xz = yz = third_x = third_y = third_z = 0.0
    x_plus = x_minus = z_plus = z_minus = 0.0
    for at, vel_y in enumerate(planes):
        rows = [found[row : row + 1, at * cells : (at + 1) * cells] for row in range(10)]
        ones, plus_x, minus_x, plus_z, minus_z = rows[0], *(unit * row for row in rows[1:5])
        sq_x, sq_z, cross = (unit * unit * row for row in rows[5:8])
        cube_x, cube_z = (unit**3 * row for row in rows[8:10])
        sq_y = vel_y * vel_y
        along_x, along_z = plus_x - minus_x, plus_z - minus_z
        count += ones
        x_plus += plus_x
        x_minus += minus_x
        z_plus += plus_z
        z_minus += minus_z
        up += jnp.abs(vel_y) * ones
        xx += sq_x
        yy += sq_y * ones
        zz += sq_z
        xy += vel_y * along_x
        xz += cross
        yz += vel_y * along_z
        third_x += cube_x + sq_y * along_x
        third_y += vel_y * (sq_x + sq_z + sq_y * ones)
        third_z += cube_z + sq_y * along_z
    y_plus = jnp.where(upward, up, 0.0)
    y_minus = jnp.where(upward, 0.0, up)
    rows = [count, xx, yy, zz, xy, xz, yz, third_x, third_y, third_z]
    rows += [x_minus, x_plus, y_minus, y_plus, z_minus, z_plus]
    return WEIGHT * jnp.concatenate(rows, axis=0)


def half_slices(width):
    low, high = [], []
    for plane in range(width // PLANE):
        low.append((plane * PLANE, plane * HALF))
        high.append((plane * PLANE + HALF, plane * HALF))
    return low, high


def move_rows(rows_ref, value_ref, send_ref, side):
    cells, width = value_ref.shape
    count = cells // 2
    ranges = half_slices(width)[side]

    def move(at, _):
        row = rows_ref[0, side, at]
        for source, target in ranges:
            send_ref[pl.ds((1 - side) * count + at, 1), target : target + HALF] = value_ref[
                pl.ds(row, 1), source : source + HALF
            ]
        return 0

    lax.fori_loop(0, count, move, 0, unroll=8)


def start_kernel(face_ref, dist_ref, own_ref, send_ref, sums_ref, table_ref, rows_ref, row_sem, sems):
    width = dist_ref.shape[1]
    row_copy = pltpu.make_async_copy(face_ref, rows_ref, row_sem)
    row_copy.start()
    copies = []
    for side, ranges in enumerate(half_slices(width)):
        for at, (source, _) in enumerate(ranges):
            lanes = slice(source, source + HALF)
            copy = pltpu.make_async_copy(
                dist_ref.at[:, lanes], own_ref.at[:, lanes], sems.at[side, at]
            )
            copy.start()
            copies.append((side, copy))
    table_ref[...] = sum_table()
    row_copy.wait()
    found = 0.0
    for side in range(2):
        for owner, copy in copies:
            if owner == side:
                copy.wait()
        move_rows(rows_ref, own_ref, send_ref, side)
        found += plane_sums(table_ref, own_ref, side * HALF, (side + 1) * HALF)
    sums_ref[...] = sums_of(found, width)


def picks(near_ref, mask_ref, face, cell_start, cells):
    index = near_ref[face : face + 1, :] - cell_start
    hit = lax.broadcasted_iota(jnp.int32, (cells, cells), 0) == index
    open_face = mask_ref[face : face + 1, :] != 1
    return jnp.where(hit & open_face, 1.0, 0.0).astype(F32)


def along(near_ref, mask_ref, upward):
    cells = near_ref.shape[1]
    cell_start = lax.axis_index("space") * cells
    faces = [picks(near_ref, mask_ref, face, cell_start, cells) for face in range(6)]
    return [faces[0], faces[1], jnp.where(upward, faces[2], faces[3]), faces[4], faces[5]]


def stream_tiles(near_ref, mask_ref, value_ref, store):
    cells, width = value_ref.shape
    planes, upward = planes_y(width)
    chosen = []
    for face in along(near_ref, mask_ref, upward):
        flipped = face.T.astype(BF16)
        chosen.append(jnp.concatenate([flipped, flipped], axis=1))
    rest = jnp.concatenate(chosen[2:], axis=0)
    for start in range(0, width, COLUMN_TILE):
        side = chosen[0] if start % PLANE >= HALF else chosen[1]
        vel_x, vel_z = lane_points(start, COLUMN_TILE)
        values = value_ref[:, start : start + COLUMN_TILE]
        pieces = jnp.concatenate(split(values, 2), axis=0)
        moved = dot(jnp.concatenate([side, rest], axis=0), pieces)
        speed_x, speed_z = jnp.abs(vel_x), jnp.abs(vel_z)
        speed_y = jnp.abs(planes[start // PLANE])
        from_z = jnp.where(vel_z > 0, moved[2 * cells : 3 * cells], moved[3 * cells :])
        stream = (
            speed_x * moved[:cells]
            + speed_y * moved[cells : 2 * cells]
            + speed_z * from_z
            - (speed_x + speed_y + speed_z) * values
        )
        store(slice(start, start + COLUMN_TILE), values, stream)


def stream_kernel(near_ref, mask_ref, value_ref, out_ref):
    def store(lanes, values, stream):
        out_ref[:, lanes] = TIME_STEP * stream

    stream_tiles(near_ref, mask_ref, value_ref, store)


def stream_last_kernel(near_ref, mask_ref, dist_ref, middle_ref, out_ref):
    def store(lanes, values, stream):
        out_ref[:, lanes] = 0.5 * (dist_ref[:, lanes] + values) + (0.5 * TIME_STEP) * stream

    stream_tiles(near_ref, mask_ref, middle_ref, store)


def wall_kernel(face_ref, temp_ref, mask_ref, shape_ref, back_ref, side_ref):
    cells, width = shape_ref.shape
    count = cells // 2
    planes, _ = planes_y(width)
    cooling = (-0.5 * LOG2E) / temp_ref[...]
    axis_point = point(lax.broadcasted_iota(jnp.int32, (NV, 1), 0))
    profile = jnp.exp2(axis_point * axis_point * cooling)
    mass = jnp.sum(profile, axis=0, keepdims=True)
    flux = jnp.sum(jnp.maximum(axis_point, 0.0) * profile, axis=0, keepdims=True)
    inv_norm = 1.0 / (WEIGHT * flux * mass * mass)
    mask = mask_ref[...]
    back_ref[...] = jnp.concatenate(
        [jnp.where(mask == 1, inv_norm, 0.0), jnp.zeros((2, cells), F32)], axis=0
    )
    rows = [mask[:2].astype(F32), cooling, jnp.zeros((LANES - 3, cells), F32)]
    columns = jnp.concatenate(rows, axis=0).T
    row = lax.broadcasted_iota(jnp.int32, (cells, count), 0)
    for side, face in enumerate((1, 0)):
        hit = (row == face_ref[0, face : face + 1, :]) & (columns[:, face : face + 1] != 1.0)
        picked = jnp.where(hit, 1.0, 0.0).astype(BF16)
        side_ref[side * cells : (side + 1) * cells, :] = jnp.concatenate([picked, picked], axis=1)
    cooling = jnp.broadcast_to(columns[:, 2:3], (cells, LANES))
    for start in range(0, PLANE, LANES):
        vel_x, vel_z = lane_points(start, LANES)
        flat = vel_x * vel_x + vel_z * vel_z
        for at, vel_y in enumerate(planes):
            lanes = slice(at * PLANE + start, at * PLANE + start + LANES)
            shape_ref[:, lanes] = jnp.exp2((flat + vel_y * vel_y) * cooling)


def columns_of(sums, back, width, step, keep):
    _, upward = planes_y(width)
    count = sums[0:1]
    inv_count = 1.0 / count
    flow_x = (sums[11:12] - sums[10:11]) * inv_count
    flow_y = (sums[13:14] - sums[12:13]) * inv_count
    flow_z = (sums[15:16] - sums[14:15]) * inv_count
    p_xx, p_yy, p_zz, p_xy, p_xz, p_yz = (sums[at : at + 1] for at in range(1, 7))
    energy = p_xx + p_yy + p_zz
    flow_sq = flow_x * flow_x + flow_y * flow_y + flow_z * flow_z
    temp = (energy * inv_count - flow_sq) / 3.0
    inv_temp = 1.0 / temp

    def heat(third, flow, press):
        return 0.5 * (
            third
            - 2.0 * (press[0] * flow_x + press[1] * flow_y + press[2] * flow_z)
            - flow * energy
            + 2.0 * count * flow * flow_sq
        )

    scale = ((1.0 - MOMENTUM_RATIO) / 5.0) * inv_count * inv_temp * inv_temp * (-2.0 / LOG2E)
    rate = (count * jnp.exp((1.0 - SHEAR_EXPONENT) * jnp.log(temp))) * (step / BASELINE_SHEAR)
    returned = (back[0:6] * step) * sums[10:16]
    rows = [
        flow_x,
        flow_y,
        flow_z,
        (-0.5 * LOG2E) * inv_temp,
        scale * heat(sums[7:8], flow_x, (p_xx, p_xy, p_xz)),
        scale * heat(sums[8:9], flow_y, (p_xy, p_yy, p_yz)),
        scale * heat(sums[9:10], flow_z, (p_xz, p_yz, p_zz)),
        count * inv_temp * lax.rsqrt(temp) * rate,
        keep - rate,
        jnp.where(upward, returned[2:3], returned[3:4]),
        returned[0:2],
        returned[4:6],
    ]
    rows.append(jnp.zeros((LANES - 14, count.shape[1]), F32))
    return jnp.concatenate(rows, axis=0).T


def relax(columns_ref, base_ref, value_ref, shape_ref, out_ref, done=None):
    cells, width = value_ref.shape
    planes, _ = planes_y(width)
    lane = lax.broadcasted_iota(jnp.int32, (ROWS, LANES), 1)
    first_x, vel_z = point((lane >> 5) & (NV - 1)), point(lane & (NV - 1))
    z_plus, z_minus = jnp.maximum(vel_z, 0.0), jnp.maximum(-vel_z, 0.0)

    def group(at, _):
        rows = pl.ds(pl.multiple_of(at * ROWS, ROWS), ROWS)
        columns = columns_ref[rows, :]
        flow_x, flow_y, flow_z, cool, heat_x, heat_y, heat_z, gain, keep, back_y, *back = (
            jnp.broadcast_to(columns[:, column : column + 1], (ROWS, LANES)) for column in range(14)
        )
        rel_z = vel_z - flow_z
        square_z = rel_z * rel_z * cool
        heat_of_z = rel_z * heat_z
        back_z = z_plus * back[2] + z_minus * back[3]
        of_y = []
        for vel_y in planes:
            rel_y = vel_y - flow_y
            of_y.append((rel_y * rel_y * cool, rel_y * heat_y, jnp.abs(vel_y) * back_y))
        for tile in range(PLANE // LANES):
            vel_x = first_x + (tile * (LANES // NV)) * SPACING
            rel_x = vel_x - flow_x
            square_xz = rel_x * rel_x * cool + square_z
            heat_xz = rel_x * heat_x + heat_of_z
            upper = tile * LANES >= HALF
            back_xz = jnp.abs(vel_x) * (back[0] if upper else back[1]) + back_z
            for plane, (square_y, heat_of_y, back_of_y) in enumerate(of_y):
                start = plane * PLANE + tile * LANES
                lanes = slice(start, start + LANES)
                square = square_xz + square_y
                skew = (heat_xz + heat_of_y) * (square + 2.5 * LOG2E) + 1.0
                out_ref[rows, lanes] = (
                    base_ref[rows, lanes]
                    + keep * value_ref[rows, lanes]
                    + gain * jnp.exp2(square) * skew
                    + shape_ref[rows, lanes] * (back_xz + back_of_y)
                )
        return 0

    parts = cells // ROWS // 4
    for part in range(4):
        lax.fori_loop(part * parts, (part + 1) * parts, group, 0)
        if done is not None:
            done(part)


def halo_tile(halo_refs, side, start, count):
    lanes = slice(start, start + COLUMN_TILE)
    if len(halo_refs) == 1:
        rows = halo_refs[0][(1 - side) * count : (2 - side) * count, lanes]
    else:
        rows = halo_refs[1 - side][:, lanes]
    return jnp.concatenate(split(rows, 2), axis=0)


def add_halo(side_ref, halo_refs, base_ref, out_ref, step):
    cells, width = base_ref.shape
    for side, ranges in enumerate(half_slices(width)):
        pick = side_ref[side * cells : (side + 1) * cells, :]
        for source, target in ranges:
            for tile in range(0, HALF, COLUMN_TILE):
                lanes = slice(source + tile, source + tile + COLUMN_TILE)
                vel_x, _ = lane_points(source + tile, COLUMN_TILE)
                halo = dot(pick, halo_tile(halo_refs, side, target + tile, cells // 2))
                out_ref[:, lanes] = base_ref[:, lanes] + (step * jnp.abs(vel_x)) * halo


def middle_kernel(face_ref, sums_ref, table_ref, back_ref, side_ref, own_ref, stream_ref, shape_ref, *refs):
    halo_refs = refs[:-7]
    out_ref, send_ref, next_ref, columns_ref, base_ref, rows_ref, row_sem = refs[-7:]
    width = own_ref.shape[1]
    row_copy = pltpu.make_async_copy(face_ref, rows_ref, row_sem)
    row_copy.start()
    columns_ref[...] = columns_of(sums_ref[...], back_ref[...], width, TIME_STEP, 1.0)
    add_halo(side_ref, halo_refs, stream_ref, base_ref, TIME_STEP)
    relax(columns_ref, base_ref, own_ref, shape_ref, out_ref)
    row_copy.wait()
    for side in range(2):
        move_rows(rows_ref, out_ref, send_ref, side)
    next_ref[...] = sums_of(plane_sums(table_ref, out_ref, 0, PLANE), width)


def last_kernel(sums_ref, back_ref, side_ref, middle_ref, part_ref, shape_ref, *refs):
    halo_refs = refs[:-5]
    out_ref, columns_ref, base_ref, result_ref, sems = refs[-5:]
    cells, width = middle_ref.shape
    step = 0.5 * TIME_STEP
    columns_ref[...] = columns_of(sums_ref[...], back_ref[...], width, step, 0.0)
    add_halo(side_ref, halo_refs, part_ref, base_ref, step)
    copies = []

    def done(part):
        rows = slice(part * cells // 4, (part + 1) * cells // 4)
        copy = pltpu.make_async_copy(result_ref.at[rows], out_ref.at[rows], sems.at[part])
        copy.start()
        copies.append(copy)

    relax(columns_ref, base_ref, middle_ref, shape_ref, result_ref, done)
    for copy in copies:
        copy.wait()


def call(kernel, outs, arrays, scratch=(), far=(), far_outs=False, flops=0):
    specs = [
        pl.BlockSpec(memory_space=pltpu.HBM if at in far else pltpu.VMEM)
        for at in range(len(arrays))
    ]
    out_space = pltpu.HBM if far_outs else pltpu.VMEM
    size = sum(math.prod(array.shape) * 4 for array in arrays)
    return pl.pallas_call(
        kernel,
        out_shape=[jax.ShapeDtypeStruct(shape, dtype) for shape, dtype in outs],
        in_specs=specs,
        out_specs=[pl.BlockSpec(memory_space=out_space)] * len(outs),
        scratch_shapes=list(scratch),
        compiler_params=pltpu.CompilerParams(vmem_limit_bytes=40 * 2**20),
        cost_estimate=pl.CostEstimate(flops=flops, bytes_accessed=size, transcendentals=0),
    )(*arrays)


def total(value):
    count = lax.axis_size("vel")
    step = 1
    while step < count:
        value = value + lax.ppermute(value, "vel", [(i, i ^ step) for i in range(count)])
        step *= 2
    return value


def exchange(send):
    count = lax.axis_size("space")
    forward = [(i, (i + 1) % count) for i in range(count)]
    backward = [(target, source) for source, target in forward]
    if count == 2:
        return [lax.ppermute(send, "space", forward)]
    half = send.shape[0] // 2
    return [
        lax.ppermute(send[:half], "space", forward),
        lax.ppermute(send[half:], "space", backward),
    ]


def on_device(dist, wall_temp, neighbours, wall_mask, face_rows):
    cells, width = dist.shape
    planes = width // PLANE
    whole, sums, send = ((cells, width), F32), ((SUMS, cells), F32), ((cells, width // 2), F32)
    table, back, sides = ((2 * SUMS, PLANE), BF16), ((8, cells), F32), ((2 * cells, cells), BF16)
    rows_scratch = [pltpu.SMEM(face_rows.shape, jnp.int32), pltpu.SemaphoreType.DMA(())]
    work = [pltpu.VMEM((cells, LANES), F32), pltpu.VMEM((cells, width), F32)]

    own, sent, own_sums, tab = call(
        start_kernel,
        [whole, send, sums, table],
        [face_rows, dist],
        rows_scratch + [pltpu.SemaphoreType.DMA((2, planes))],
        far=(0, 1),
    )
    halo = exchange(sent)
    shape, back, side = call(wall_kernel, [whole, back, sides], [face_rows, wall_temp[None, :], wall_mask])
    (stream,) = call(stream_kernel, [whole], [neighbours, wall_mask, own])
    sums_one = total(own_sums)
    middle, sent, own_sums = call(
        middle_kernel,
        [whole, send, sums],
        [face_rows, sums_one, tab, back, side, own, stream, shape, *halo],
        work + rows_scratch,
        far=(0,),
    )
    halo = exchange(sent)
    (part,) = call(stream_last_kernel, [whole], [neighbours, wall_mask, own, middle])
    sums_two = total(own_sums)
    (result,) = call(
        last_kernel,
        [whole],
        [sums_two, back, side, middle, part, shape, *halo],
        work + [pltpu.VMEM((cells, width), F32), pltpu.SemaphoreType.DMA((4,))],
        far_outs=True,
    )
    return result


def solution(mesh):
    return jax.shard_map(
        on_device,
        mesh=mesh,
        in_specs=(
            P("space", "vel"),
            P("space"),
            P(None, "space"),
            P(None, "space"),
            P("space", None, None),
        ),
        out_specs=P("space", "vel"),
        check_vma=False,
    )
```

```python
import functools
import math

import jax
import jax.numpy as jnp
from jax import lax
from jax.experimental import pallas as pl
from jax.experimental.pallas import tpu as pltpu
from jax.sharding import PartitionSpec as P

NV = 32
LIMIT = 4.5
SPACING = 2.0 * LIMIT / NV
WEIGHT = SPACING**3 * (2.0 * math.pi) ** (-1.5)
TIME_STEP = 0.05
BASELINE_SHEAR = 0.1
SHEAR_EXPONENT = 0.66
MOMENTUM_RATIO = 2.0 / 3.0
PLANE = NV * NV
HALF = PLANE // 2
ROWS = 8
LANES = 128
COLUMN_TILE = 256
SUMS = 16
FACES = 6
NOTES = 8
BEND = 2.5 * math.log2(math.e)
LOG2E = math.log2(math.e)
F32 = jnp.float32
BF16 = jnp.bfloat16


def point(slot):
    return -LIMIT + (slot.astype(F32) + 0.5) * SPACING


def lane_points(start, width):
    lane = lax.broadcasted_iota(jnp.int32, (1, width), 1) + start
    return point((lane >> 5) & (NV - 1)), point(lane & (NV - 1))


def planes_y(width):
    planes = width // PLANE
    first = lax.axis_index("vel") * planes
    return [point(first + at) for at in range(planes)], first >= NV // 2


def split(value, count):
    pieces = []
    for _ in range(count - 1):
        piece = value.astype(BF16)
        pieces.append(piece)
        value = value - piece.astype(F32)
    pieces.append(value.astype(BF16))
    return pieces


def dot(left, right, dims=((1,), (0,))):
    return lax.dot_general(left, right, (dims, ((), ())), preferred_element_type=F32)


def exact(left, right, dims=((1,), (0,))):
    rows = left.shape[0]
    found = dot(jnp.concatenate(split(left, 3), axis=0), right, dims)
    return found[:rows] + found[rows : 2 * rows] + found[2 * rows :]


def inward(vel_x, vel_y, vel_z):
    return [
        jnp.maximum(sign * vel, 0.0) for vel in (vel_x, vel_y, vel_z) for sign in (1.0, -1.0)
    ]


def weights(vel_x, vel_y, vel_z):
    speed_sq = vel_x * vel_x + vel_y * vel_y + vel_z * vel_z
    into = inward(vel_x, vel_y, vel_z)
    rows = [
        jnp.ones_like(vel_x),
        vel_x * vel_x,
        vel_y * vel_y,
        vel_z * vel_z,
        vel_x * vel_y,
        vel_x * vel_z,
        vel_y * vel_z,
        vel_x * speed_sq,
        vel_y * speed_sq,
        vel_z * speed_sq,
        into[1],
        into[0],
        into[3],
        into[2],
        into[5],
        into[4],
    ]
    return WEIGHT * jnp.concatenate(rows, axis=0), into


def face_hits(face_ref, cells):
    row = lax.broadcasted_iota(jnp.int32, (cells, face_ref.shape[2]), 0)
    return [jnp.where(row == face_ref[0, side : side + 1, :], 1.0, 0.0) for side in range(2)]


def sums_kernel(face_ref, dist_ref, sums_ref, send_ref):
    cells, width = dist_ref.shape
    planes, _ = planes_y(width)
    total = None
    for start in range(0, width, HALF):
        lanes = slice(start, start + HALF)
        vel_x, vel_z = lane_points(start, HALF)
        vel_y = jnp.full((1, HALF), planes[start // PLANE])
        base, into = weights(vel_x, vel_y, vel_z)
        table = jnp.concatenate([base] + [base * speed for speed in into], axis=0)
        coarse, fine = split(table, 2)
        finest = split(base, 3)[2]
        pieces = split(dist_ref[:, lanes], 3)
        across = ((1,), (1,))
        one = dot(jnp.concatenate([coarse, fine, finest], axis=0), pieces[0], across)
        two = dot(jnp.concatenate([coarse, fine], axis=0), pieces[1], across)
        three = dot(coarse, pieces[2], across)
        rows = table.shape[0]
        part = one[:rows] + one[rows : 2 * rows] + two[:rows] + two[rows:] + three
        part = jnp.concatenate([part[:SUMS] + one[2 * rows :], part[SUMS:]], axis=0)
        total = part if total is None else total + part
    sums_ref[...] = total
    low, high = face_hits(face_ref, cells)
    base, from_low, from_high = total[:SUMS], total[SUMS : 2 * SUMS], total[2 * SUMS : 3 * SUMS]
    upward = exact(jnp.concatenate([base, from_low], axis=0), high.astype(BF16))
    downward = exact(jnp.concatenate([base, from_high], axis=0), low.astype(BF16))
    send_ref[...] = jnp.concatenate([upward, downward], axis=0)


def halo_rows(refs, side, rows=slice(None)):
    if len(refs) == 2:
        return refs[side][rows]
    half = refs[0].shape[0] // 2
    start, stop, _ = rows.indices(half)
    return refs[0][side * half + start : side * half + stop]


def gather_kernel(sums_ref, *refs):
    halo_refs, out_ref = refs[:-1], refs[-1]
    rows = sums_ref.shape[0]
    out_ref[:rows, :] = sums_ref[...]
    out_ref[rows:, :] = jnp.concatenate([halo_rows(halo_refs, 0), halo_rows(halo_refs, 1)], axis=1)

def half_slices(width):
    low, high = [], []
    for plane in range(width // PLANE):
        low.append((plane * PLANE, plane * HALF))
        high.append((plane * PLANE + HALF, plane * HALF))
    return low, high


def move_rows(rows_ref, plane, value_ref, send_ref, side, first):
    cells, width = value_ref.shape
    ranges = half_slices(width)[side]

    def move(at, _):
        row = rows_ref[0, plane, at]
        for source, target in ranges:
            send_ref[pl.ds(first + at, 1), target : target + HALF] = value_ref[
                pl.ds(row, 1), source : source + HALF
            ]
        return 0

    lax.fori_loop(0, cells // 2, move, 0, unroll=8)


def wall_rows(temp_ref):
    cooling = (-0.5 * LOG2E) / temp_ref[...]
    axis_point = point(lax.broadcasted_iota(jnp.int32, (NV, 1), 0))
    profile = jnp.exp2(axis_point * axis_point * cooling)
    mass = jnp.sum(profile, axis=0, keepdims=True)
    flux = jnp.sum(jnp.maximum(axis_point, 0.0) * profile, axis=0, keepdims=True)
    return 1.0 / (WEIGHT * flux * mass * mass), cooling


def near_plane_kernel(rows_ref, face_ref, temp_ref, mask_ref, dist_ref, send_ref):
    cells, _ = dist_ref.shape
    count = cells // 2
    inv_norm, cooling = wall_rows(temp_ref)
    notes = jnp.concatenate([mask_ref[...].astype(F32), inv_norm, cooling], axis=0)
    low, high = face_hits(face_ref, cells)
    for side, hits in ((1, high), (0, low)):
        first = (1 - side) * (count + NOTES)
        send_ref[first + count : first + count + NOTES, :count] = exact(notes, hits.astype(BF16))
        move_rows(rows_ref, side, dist_ref, send_ref, side, first)


def far_plane_kernel(rows_ref, dist_ref, send_ref):
    for side in (1, 0):
        first = (1 - side) * (dist_ref.shape[0] // 2)
        move_rows(rows_ref, 1 - side, dist_ref, send_ref, side, first)


def picks(near_ref, mask_ref, face, cell_start, cells):
    index = near_ref[face : face + 1, :] - cell_start
    hit = lax.broadcasted_iota(jnp.int32, (cells, cells), 0) == index
    open_face = mask_ref[face : face + 1, :] != 1
    return jnp.where(hit & open_face, 1.0, 0.0).astype(F32)


def along(near_ref, mask_ref, upward):
    cells = near_ref.shape[1]
    cell_start = lax.axis_index("space") * cells
    faces = [picks(near_ref, mask_ref, face, cell_start, cells) for face in range(6)]
    return [faces[0], faces[1], jnp.where(upward, faces[2], faces[3]), faces[4], faces[5]]


def stream_tiles(near_ref, mask_ref, value_ref, store):
    cells, width = value_ref.shape
    planes, upward = planes_y(width)
    chosen = []
    for face in along(near_ref, mask_ref, upward):
        flipped = face.T.astype(BF16)
        chosen.append(jnp.concatenate([flipped, flipped], axis=1))
    rest = jnp.concatenate(chosen[2:], axis=0)
    for start in range(0, width, COLUMN_TILE):
        side = chosen[0] if start % PLANE >= HALF else chosen[1]
        vel_x, vel_z = lane_points(start, COLUMN_TILE)
        values = value_ref[:, start : start + COLUMN_TILE]
        pieces = jnp.concatenate(split(values, 2), axis=0)
        moved = dot(jnp.concatenate([side, rest], axis=0), pieces)
        speed_x, speed_z = jnp.abs(vel_x), jnp.abs(vel_z)
        speed_y = jnp.abs(planes[start // PLANE])
        from_z = jnp.where(vel_z > 0, moved[2 * cells : 3 * cells], moved[3 * cells :])
        stream = (
            speed_x * moved[:cells]
            + speed_y * moved[cells : 2 * cells]
            + speed_z * from_z
            - (speed_x + speed_y + speed_z) * values
        )
        store(slice(start, start + COLUMN_TILE), values, stream)


def stream_kernel(near_ref, mask_ref, value_ref, out_ref):
    def store(lanes, values, stream):
        out_ref[:, lanes] = TIME_STEP * stream

    stream_tiles(near_ref, mask_ref, value_ref, store)


def stream_last_kernel(near_ref, mask_ref, dist_ref, middle_ref, out_ref):
    def store(lanes, values, stream):
        out_ref[:, lanes] = 0.5 * (dist_ref[:, lanes] + values) + (0.5 * TIME_STEP) * stream

    stream_tiles(near_ref, mask_ref, middle_ref, store)


def wall_kernel(face_ref, temp_ref, mask_ref, shape_ref, back_ref, side_ref):
    cells, width = shape_ref.shape
    count = cells // 2
    planes, _ = planes_y(width)
    inv_norm, cooling = wall_rows(temp_ref)
    mask = mask_ref[...]
    back_ref[...] = jnp.concatenate(
        [jnp.where(mask == 1, inv_norm, 0.0), cooling, jnp.zeros((1, cells), F32)],
        axis=0,
    )
    rows = [mask[:2].astype(F32), cooling, jnp.zeros((LANES - 3, cells), F32)]
    columns = jnp.concatenate(rows, axis=0).T
    row = lax.broadcasted_iota(jnp.int32, (cells, count), 0)
    for side, face in enumerate((1, 0)):
        hit = (row == face_ref[0, face : face + 1, :]) & (columns[:, face : face + 1] != 1.0)
        picked = jnp.where(hit, 1.0, 0.0).astype(BF16)
        side_ref[side * cells : (side + 1) * cells, :] = jnp.concatenate([picked, picked], axis=1)
    cooling = jnp.broadcast_to(columns[:, 2:3], (cells, LANES))
    for start in range(0, PLANE, LANES):
        vel_x, vel_z = lane_points(start, LANES)
        flat = vel_x * vel_x + vel_z * vel_z
        for at, vel_y in enumerate(planes):
            lanes = slice(at * PLANE + start, at * PLANE + start + LANES)
            shape_ref[:, lanes] = jnp.exp2((flat + vel_y * vel_y) * cooling)


def coefficients(sums, back, step, keep):
    count = sums[0:1]
    inv_count = 1.0 / count
    flow_x = (sums[11:12] - sums[10:11]) * inv_count
    flow_y = (sums[13:14] - sums[12:13]) * inv_count
    flow_z = (sums[15:16] - sums[14:15]) * inv_count
    p_xx, p_yy, p_zz, p_xy, p_xz, p_yz = (sums[at : at + 1] for at in range(1, 7))
    energy = p_xx + p_yy + p_zz
    flow_sq = flow_x * flow_x + flow_y * flow_y + flow_z * flow_z
    temp = (energy * inv_count - flow_sq) / 3.0
    inv_temp = 1.0 / temp

    def heat(third, flow, press):
        return 0.5 * (
            third
            - 2.0 * (press[0] * flow_x + press[1] * flow_y + press[2] * flow_z)
            - flow * energy
            + 2.0 * count * flow * flow_sq
        )

    scale = ((1.0 - MOMENTUM_RATIO) / 5.0) * inv_count * inv_temp * inv_temp * (-2.0 / LOG2E)
    rate = (count * jnp.exp((1.0 - SHEAR_EXPONENT) * jnp.log(temp))) * (step / BASELINE_SHEAR)
    returned = (back[0:6] * step) * sums[10:16]
    rows = [
        flow_x,
        flow_y,
        flow_z,
        (-0.5 * LOG2E) * inv_temp,
        scale * heat(sums[7:8], flow_x, (p_xx, p_xy, p_xz)),
        scale * heat(sums[8:9], flow_y, (p_xy, p_yy, p_yz)),
        scale * heat(sums[9:10], flow_z, (p_xz, p_yz, p_zz)),
        count * inv_temp * lax.rsqrt(temp) * rate,
        keep - rate,
    ]
    return rows, returned


def columns_of(sums, back, width, step, keep):
    _, upward = planes_y(width)
    rows, returned = coefficients(sums, back, step, keep)
    rows += [
        jnp.where(upward, returned[2:3], returned[3:4]),
        returned[0:2],
        returned[4:6],
        jnp.zeros((LANES - 14, sums.shape[1]), F32),
    ]
    return jnp.concatenate(rows, axis=0).T


def relax(columns_ref, base_ref, value_ref, shape_ref, out_ref, half=False):
    cells, width = value_ref.shape
    planes, _ = planes_y(2 * width if half else width)
    lane = lax.broadcasted_iota(jnp.int32, (ROWS, LANES), 1)
    first_x, vel_z = point((lane >> 5) & (NV - 1)), point(lane & (NV - 1))
    z_plus, z_minus = jnp.maximum(vel_z, 0.0), jnp.maximum(-vel_z, 0.0)

    def group(at, _, tiles=range(PLANE // LANES), stride=PLANE):
        rows = pl.ds(pl.multiple_of(at * ROWS, ROWS), ROWS)
        columns = columns_ref[rows, :]
        flow_x, flow_y, flow_z, cool, heat_x, heat_y, heat_z, gain, keep, back_y, *back = (
            jnp.broadcast_to(columns[:, column : column + 1], (ROWS, LANES)) for column in range(14)
        )
        rel_z = vel_z - flow_z
        square_z = rel_z * rel_z * cool
        heat_of_z = rel_z * heat_z
        back_z = z_plus * back[2] + z_minus * back[3]
        of_y = []
        for vel_y in planes:
            rel_y = vel_y - flow_y
            of_y.append((rel_y * rel_y * cool, rel_y * heat_y, jnp.abs(vel_y) * back_y))
        for tile in tiles:
            vel_x = first_x + (tile * (LANES // NV)) * SPACING
            rel_x = vel_x - flow_x
            square_xz = rel_x * rel_x * cool + square_z
            heat_xz = rel_x * heat_x + heat_of_z
            upper = tile * LANES >= HALF
            back_xz = jnp.abs(vel_x) * (back[0] if upper else back[1]) + back_z
            for plane, (square_y, heat_of_y, back_of_y) in enumerate(of_y):
                start = plane * stride + (tile - tiles[0]) * LANES
                lanes = slice(start, start + LANES)
                square = square_xz + square_y
                skew = (heat_xz + heat_of_y) * (square + 2.5 * LOG2E) + 1.0
                out_ref[rows, lanes] = (
                    base_ref[rows, lanes]
                    + keep * value_ref[rows, lanes]
                    + gain * jnp.exp2(square) * skew
                    + shape_ref[rows, lanes] * (back_xz + back_of_y)
                )
        return 0

    groups = cells // ROWS
    if half:
        low, high = range(HALF // LANES), range(HALF // LANES, PLANE // LANES)
        lax.fori_loop(0, groups // 2, functools.partial(group, tiles=high, stride=HALF), 0)
        lax.fori_loop(groups // 2, groups, functools.partial(group, tiles=low, stride=HALF), 0)
    else:
        lax.fori_loop(0, groups, group, 0)


def middle_kernel(sums_ref, back_ref, side_ref, own_ref, stream_ref, shape_ref, *refs):
    halo_refs, (out_ref, columns_ref, base_ref) = refs[:-3], refs[-3:]
    cells, width = own_ref.shape
    columns_ref[...] = columns_of(sums_ref[:SUMS], back_ref[...], width, TIME_STEP, 1.0)
    for side, ranges in enumerate(half_slices(width)):
        pick = side_ref[side * cells : (side + 1) * cells, :]
        for source, target in ranges:
            for tile in range(0, HALF, COLUMN_TILE):
                lanes = slice(source + tile, source + tile + COLUMN_TILE)
                vel_x, _ = lane_points(source + tile, COLUMN_TILE)
                rows = halo_rows(halo_refs, 1 - side, slice(0, cells // 2))
                rows = rows[:, target + tile : target + tile + COLUMN_TILE]
                halo = dot(pick, jnp.concatenate(split(rows, 2), axis=0))
                base_ref[:, lanes] = stream_ref[:, lanes] + (TIME_STEP * jnp.abs(vel_x)) * halo
    relax(columns_ref, base_ref, own_ref, shape_ref, out_ref)


def relax_kernel(sums_ref, back_ref, middle_ref, part_ref, shape_ref, out_ref, columns_ref):
    width = middle_ref.shape[1]
    step = 0.5 * TIME_STEP
    columns_ref[...] = columns_of(sums_ref[...], back_ref[...], width, step, 0.0)
    relax(columns_ref, part_ref, middle_ref, shape_ref, out_ref)


ORDERS = (
    [(0, 0, 0)],
    [(2, 0, 0)],
    [(0, 2, 0)],
    [(0, 0, 2)],
    [(1, 1, 0)],
    [(1, 0, 1)],
    [(0, 1, 1)],
    [(3, 0, 0), (1, 2, 0), (1, 0, 2)],
    [(0, 3, 0), (2, 1, 0), (0, 1, 2)],
    [(0, 0, 3), (2, 0, 1), (0, 2, 1)],
    [("-", 0, 0)],
    [("+", 0, 0)],
    [(0, "-", 0)],
    [(0, "+", 0)],
    [(0, 0, "-")],
    [(0, 0, "+")],
)


def power(value, order):
    if order == "+":
        return jnp.maximum(value, 0.0)
    if order == "-":
        return jnp.maximum(-value, 0.0)
    result = None
    for _ in range(order):
        result = value if result is None else result * value
    return result


def advance_kernel(face_ref, near_ref, mask_ref, sums_ref, back_ref, out_ref):
    cells = near_ref.shape[1]
    count = cells // 2
    cell_start = lax.axis_index("space") * cells
    sums = sums_ref[:SUMS]
    flux = [sums_ref[SUMS * (face + 1) : SUMS * (face + 2)] for face in range(FACES)]
    gas = 0.0
    for face in range(FACES):
        hits = picks(near_ref, mask_ref, face, cell_start, cells).astype(BF16)
        gas += exact(flux[face], hits) - flux[face]
    arrived = sums_ref[SUMS * (FACES + 2) :]
    for face, hits in enumerate(face_hits(face_ref, cells)):
        found = exact(
            arrived[:, face * count : (face + 1) * count], hits.astype(BF16), ((1,), (1,))
        )
        gas += jnp.where(mask_ref[face : face + 1, :] != 1, found, 0.0)

    rows, returned = coefficients(sums, back_ref[...], TIME_STEP, 1.0)
    flows, cool, heats, gain, keep = rows[0:3], rows[3], rows[4:7], rows[7], rows[8]
    points = jnp.broadcast_to(point(lax.broadcasted_iota(jnp.int32, (NV, cells), 0)), (NV, cells))
    axes = []
    for flow in flows:
        off = points - flow
        bell = jnp.exp2(off * off * cool)
        axes.append([bell, bell * off, bell * off * off, bell * off * off * off])
    known = {}

    def along_axis(axis, order):
        if (axis, order) not in known:
            factor = power(points, order)
            known[axis, order] = [
                jnp.sum(term if factor is None else factor * term, axis=0, keepdims=True)
                for term in axes[axis]
            ]
        return known[axis, order]

    wall_bell = jnp.exp2(points * points * back_ref[6:7])
    above = jnp.maximum(points, 0.0)
    wall_sums = [jnp.sum(jnp.where(points > 0, wall_bell, 0.0), axis=0, keepdims=True)]
    for _ in range(4):
        wall_bell = wall_bell * above
        wall_sums.append(jnp.sum(wall_bell, axis=0, keepdims=True))

    def wall_full(order):
        if order in ("+", "-"):
            return wall_sums[1]
        return None if order % 2 else 2.0 * wall_sums[order]

    def wall_half(order, sign):
        if order in ("+", "-"):
            return wall_sums[2] if order == sign else None
        found = wall_sums[order + 1]
        return -found if order % 2 and sign == "-" else found

    found_rows = []
    for orders in ORDERS:
        bells, walls = 0.0, 0.0
        for order in orders:
            (x0, x1, x2, x3), (y0, y1, y2, y3), (z0, z1, z2, z3) = (
                along_axis(axis, order[axis]) for axis in range(3)
            )
            xy, xz, yz = x0 * y0, x0 * z0, y0 * z0
            skew = heats[0] * (x1 * (BEND * yz + cool * (y2 * z0 + y0 * z2)) + cool * x3 * yz)
            skew += heats[1] * (y1 * (BEND * xz + cool * (x2 * z0 + x0 * z2)) + cool * y3 * xz)
            skew += heats[2] * (z1 * (BEND * xy + cool * (x2 * y0 + x0 * y2)) + cool * z3 * xy)
            bells += xy * z0 + skew
            for face in range(FACES):
                terms = [
                    wall_half(order[axis], "+-"[face % 2])
                    if axis == face // 2
                    else wall_full(order[axis])
                    for axis in range(3)
                ]
                if all(term is not None for term in terms):
                    walls += returned[face : face + 1] * terms[0] * terms[1] * terms[2]
        found_rows.append(gain * bells + walls)
    found = WEIGHT * jnp.concatenate(found_rows, axis=0)
    out_ref[...] = found + keep * sums + TIME_STEP * gas


def halo_stream_kernel(face_ref, near_ref, *refs):
    halo_refs, (base_ref, shape_ref, values_ref, notes_ref, open_ref) = refs[:-5], refs[-5:]
    rows, width = base_ref.shape
    count = rows // 2
    planes, upward = planes_y(2 * width)
    cell_start = lax.axis_index("space") * rows
    notes = jnp.concatenate(
        [halo_rows(halo_refs, side, slice(count, count + NOTES))[:, :count] for side in range(2)],
        axis=1,
    )
    notes_ref[...] = notes
    passing = jnp.where(notes[:FACES] != 1.0, 1.0, 0.0)
    lane = lax.broadcasted_iota(jnp.int32, (1, rows), 1)
    picked = [
        jnp.where(lane < count, passing[0:1], passing[1:2]),
        jnp.where(upward, passing[2:3], passing[3:4]),
        passing[4:6],
        notes[7:8],
        jnp.zeros((LANES - 5, rows), F32),
    ]
    columns = jnp.concatenate(picked, axis=0).T
    open_x, open_y, open_low, open_high, cooling = (
        jnp.broadcast_to(columns[:, at : at + 1], (rows, LANES)) for at in range(5)
    )
    open_ref[...] = TIME_STEP * open_x
    low = face_hits(face_ref, rows)[0]
    low_flipped, low = low.T.astype(BF16), low.astype(BF16)
    row = lax.broadcasted_iota(jnp.int32, (rows, rows), 0)
    steps = []
    for face in range(2, FACES):
        hits = jnp.where(row == near_ref[face : face + 1, :] - cell_start, 1.0, 0.0)
        from_rows = dot(low_flipped, hits.T.astype(BF16)).astype(BF16)
        steps.append(dot(from_rows, low))
    along_y = jnp.where(upward, steps[0], steps[1])
    picks_all = jnp.concatenate([along_y, steps[2], steps[3]], axis=0).astype(BF16)
    picks_all = jnp.concatenate([picks_all, picks_all], axis=1)
    for side in range(2):
        block = slice(side * count, (side + 1) * count)
        values_ref[block, :] = halo_rows(halo_refs, side, slice(0, count))

        def wide(column):
            return jnp.concatenate([column[block]] * (COLUMN_TILE // LANES), axis=1)

        for start in range(0, width, COLUMN_TILE):
            lanes = slice(start, start + COLUMN_TILE)
            vel_x, vel_z = lane_points((1 - side) * HALF + start % HALF, COLUMN_TILE)
            vel_y = planes[start // HALF]
            values = values_ref[block, lanes]
            moved = dot(picks_all, jnp.concatenate(split(values, 2), axis=0))
            speed_x, speed_y, speed_z = jnp.abs(vel_x), jnp.abs(vel_y), jnp.abs(vel_z)
            from_z = jnp.where(
                vel_z > 0,
                wide(open_low) * moved[count : 2 * count],
                wide(open_high) * moved[2 * count :],
            )
            base_ref[block, lanes] = TIME_STEP * (
                speed_y * (wide(open_y) * moved[:count])
                + speed_z * from_z
                - (speed_x + speed_y + speed_z) * values
            )
            speed_sq = vel_x * vel_x + vel_y * vel_y + vel_z * vel_z
            shape_ref[block, lanes] = jnp.exp2(speed_sq * wide(cooling))


def halo_relax_kernel(sums_ref, notes_ref, base_ref, shape_ref, values_ref, out_ref, columns_ref):
    width = values_ref.shape[1]
    sums = sums_ref[SUMS * (FACES + 1) : SUMS * (FACES + 2)]
    notes = notes_ref[...]
    back = jnp.where(notes[:FACES] == 1.0, notes[6:7], 0.0)
    columns_ref[...] = columns_of(sums, back, 2 * width, TIME_STEP, 1.0)
    relax(columns_ref, base_ref, values_ref, shape_ref, out_ref, half=True)


def last_kernel(side_ref, part_ref, plane_ref, open_ref, *refs):
    halo_refs, (out_ref, result_ref, sems) = refs[:-3], refs[-3:]
    cells, width = part_ref.shape
    count = cells // 2
    copies = []
    for side, ranges in enumerate(half_slices(width)):
        pick = side_ref[side * cells : (side + 1) * cells, :]
        block = slice((1 - side) * count, (2 - side) * count)
        gate = jnp.concatenate([open_ref[block]] * (COLUMN_TILE // LANES), axis=1)
        for source, target in ranges:
            for tile in range(0, HALF, COLUMN_TILE):
                lanes = slice(source + tile, source + tile + COLUMN_TILE)
                there = slice(target + tile, target + tile + COLUMN_TILE)
                speed_x = jnp.abs(lane_points(source + tile, COLUMN_TILE)[0])
                rows = halo_rows(halo_refs, 1 - side)[:, there]
                rows = plane_ref[block, there] + gate * speed_x * rows
                halo = dot(pick, jnp.concatenate(split(rows, 2), axis=0))
                result_ref[:, lanes] = part_ref[:, lanes] + (0.5 * TIME_STEP * speed_x) * halo
                copy = pltpu.make_async_copy(
                    result_ref.at[:, lanes], out_ref.at[:, lanes], sems.at[len(copies)]
                )
                copy.start()
                copies.append(copy)
    for copy in copies:
        copy.wait()


def call(kernel, outs, arrays, scratch=(), scalars=0, far_outs=False, flops=0):
    specs = [
        pl.BlockSpec(memory_space=pltpu.SMEM if at < scalars else pltpu.VMEM)
        for at in range(len(arrays))
    ]
    out_space = pltpu.HBM if far_outs else pltpu.VMEM
    size = sum(math.prod(array.shape) * 4 for array in arrays)
    return pl.pallas_call(
        kernel,
        out_shape=[jax.ShapeDtypeStruct(shape, dtype) for shape, dtype in outs],
        in_specs=specs,
        out_specs=[pl.BlockSpec(memory_space=out_space)] * len(outs),
        scratch_shapes=list(scratch),
        compiler_params=pltpu.CompilerParams(vmem_limit_bytes=40 * 2**20),
        cost_estimate=pl.CostEstimate(flops=flops, bytes_accessed=size, transcendentals=0),
    )(*arrays)


def total(value):
    count = lax.axis_size("vel")
    step = 1
    while step < count:
        value = value + lax.ppermute(value, "vel", [(i, i ^ step) for i in range(count)])
        step *= 2
    return value


def exchange(send):
    count = lax.axis_size("space")
    forward = [(i, (i + 1) % count) for i in range(count)]
    backward = [(target, source) for source, target in forward]
    if count == 2:
        return [lax.ppermute(send, "space", forward)]
    half = send.shape[0] // 2
    return [
        lax.ppermute(send[:half], "space", forward),
        lax.ppermute(send[half:], "space", backward),
    ]


def on_device(dist, wall_temp, neighbours, wall_mask, face_rows):
    cells, width = dist.shape
    count, half = cells // 2, width // 2
    temp = wall_temp[None, :]
    whole, plane = ((cells, width), F32), ((cells, half), F32)
    every = SUMS * (FACES + 1)
    columns = pltpu.VMEM((cells, LANES), F32)

    own_sums, sent = call(
        sums_kernel, [((every, cells), F32), ((4 * SUMS, count), F32)], [face_rows, dist]
    )
    halo_sums = exchange(sent)
    (sent,) = call(
        near_plane_kernel,
        [((2 * (count + NOTES), half), F32)],
        [face_rows, face_rows, temp, wall_mask, dist],
        scalars=1,
    )
    near = exchange(sent)
    (sent,) = call(far_plane_kernel, [plane], [face_rows, dist], scalars=1)
    far = exchange(sent)
    (sums,) = call(gather_kernel, [((every + 2 * SUMS, cells), F32)], [own_sums, *halo_sums])
    shape, back, side = call(
        wall_kernel,
        [whole, ((8, cells), F32), ((2 * cells, cells), BF16)],
        [face_rows, temp, wall_mask],
    )
    (stream,) = call(stream_kernel, [whole], [neighbours, wall_mask, dist])
    base, halo_shape, values, notes, gate = call(
        halo_stream_kernel,
        [plane, plane, plane, ((NOTES, cells), F32), ((cells, LANES), F32)],
        [face_rows, neighbours, *near],
    )
    sums = total(sums)
    (middle,) = call(
        middle_kernel,
        [whole],
        [sums, back, side, dist, stream, shape, *near],
        [columns, pltpu.VMEM((cells, width), F32)],
    )
    (sums_two,) = call(
        advance_kernel, [((SUMS, cells), F32)], [face_rows, neighbours, wall_mask, sums, back]
    )
    (part,) = call(stream_last_kernel, [whole], [neighbours, wall_mask, dist, middle])
    (part,) = call(relax_kernel, [whole], [sums_two, back, middle, part, shape], [columns])
    (plane_one,) = call(
        halo_relax_kernel, [plane], [sums, notes, base, halo_shape, values], [columns]
    )
    (result,) = call(
        last_kernel,
        [whole],
        [side, part, plane_one, gate, *far],
        [pltpu.VMEM((cells, width), F32), pltpu.SemaphoreType.DMA((width // COLUMN_TILE,))],
        far_outs=True,
    )
    return result


def solution(mesh):
    return jax.shard_map(
        on_device,
        mesh=mesh,
        in_specs=(
            P("space", "vel"),
            P("space"),
            P(None, "space"),
            P(None, "space"),
            P("space", None, None),
        ),
        out_specs=P("space", "vel"),
        check_vma=False,
    )
```

```python
import functools
import math

import jax
import jax.numpy as jnp
from jax import lax
from jax.experimental import pallas as pl
from jax.experimental.pallas import tpu as pltpu
from jax.sharding import PartitionSpec as P

NV = 32
LIMIT = 4.5
SPACING = 2.0 * LIMIT / NV
WEIGHT = SPACING**3 * (2.0 * math.pi) ** (-1.5)
TIME_STEP = 0.05
BASELINE_SHEAR = 0.1
SHEAR_EXPONENT = 0.66
MOMENTUM_RATIO = 2.0 / 3.0
PLANE = NV * NV
HALF = PLANE // 2
ROWS = 8
LANES = 128
COLUMN_TILE = 256
SUMS = 16
FACES = 6
NOTES = 8
BEND = 2.5 * math.log2(math.e)
LOG2E = math.log2(math.e)
F32 = jnp.float32
BF16 = jnp.bfloat16


def point(slot):
    return -LIMIT + (slot.astype(F32) + 0.5) * SPACING


def lane_points(start, width):
    lane = lax.broadcasted_iota(jnp.int32, (1, width), 1) + start
    return point((lane >> 5) & (NV - 1)), point(lane & (NV - 1))


def planes_y(width):
    planes = width // PLANE
    first = lax.axis_index("vel") * planes
    return [point(first + at) for at in range(planes)], first >= NV // 2


def split(value, count):
    pieces = []
    for _ in range(count - 1):
        piece = value.astype(BF16)
        pieces.append(piece)
        value = value - piece.astype(F32)
    pieces.append(value.astype(BF16))
    return pieces


def dot(left, right, dims=((1,), (0,))):
    return lax.dot_general(left, right, (dims, ((), ())), preferred_element_type=F32)


def exact(left, right, dims=((1,), (0,))):
    rows = left.shape[0]
    found = dot(jnp.concatenate(split(left, 3), axis=0), right, dims)
    return found[:rows] + found[rows : 2 * rows] + found[2 * rows :]


def inward(vel_x, vel_y, vel_z):
    return [
        jnp.maximum(sign * vel, 0.0) for vel in (vel_x, vel_y, vel_z) for sign in (1.0, -1.0)
    ]


def weights(vel_x, vel_y, vel_z):
    speed_sq = vel_x * vel_x + vel_y * vel_y + vel_z * vel_z
    into = inward(vel_x, vel_y, vel_z)
    rows = [
        jnp.ones_like(vel_x),
        vel_x * vel_x,
        vel_y * vel_y,
        vel_z * vel_z,
        vel_x * vel_y,
        vel_x * vel_z,
        vel_y * vel_z,
        vel_x * speed_sq,
        vel_y * speed_sq,
        vel_z * speed_sq,
        into[1],
        into[0],
        into[3],
        into[2],
        into[5],
        into[4],
    ]
    return WEIGHT * jnp.concatenate(rows, axis=0), into


def face_hits(face_ref, cells):
    row = lax.broadcasted_iota(jnp.int32, (cells, face_ref.shape[2]), 0)
    return [jnp.where(row == face_ref[0, side : side + 1, :], 1.0, 0.0) for side in range(2)]


def sums_kernel(face_ref, dist_ref, sums_ref, send_ref):
    cells, width = dist_ref.shape
    planes, _ = planes_y(width)
    total = None
    for start in range(0, width, HALF):
        lanes = slice(start, start + HALF)
        vel_x, vel_z = lane_points(start, HALF)
        vel_y = jnp.full((1, HALF), planes[start // PLANE])
        base, into = weights(vel_x, vel_y, vel_z)
        table = jnp.concatenate([base] + [base * speed for speed in into], axis=0)
        coarse, fine = split(table, 2)
        finest = split(base, 3)[2]
        pieces = split(dist_ref[:, lanes], 3)
        across = ((1,), (1,))
        one = dot(jnp.concatenate([coarse, fine, finest], axis=0), pieces[0], across)
        two = dot(jnp.concatenate([coarse, fine], axis=0), pieces[1], across)
        three = dot(coarse, pieces[2], across)
        rows = table.shape[0]
        part = one[:rows] + one[rows : 2 * rows] + two[:rows] + two[rows:] + three
        part = jnp.concatenate([part[:SUMS] + one[2 * rows :], part[SUMS:]], axis=0)
        total = part if total is None else total + part
    sums_ref[...] = total
    low, high = face_hits(face_ref, cells)
    base, from_low, from_high = total[:SUMS], total[SUMS : 2 * SUMS], total[2 * SUMS : 3 * SUMS]
    upward = exact(jnp.concatenate([base, from_low], axis=0), high.astype(BF16))
    downward = exact(jnp.concatenate([base, from_high], axis=0), low.astype(BF16))
    send_ref[...] = jnp.concatenate([upward, downward], axis=0)


def halo_rows(refs, side, rows=slice(None)):
    if len(refs) == 2:
        return refs[side][rows]
    half = refs[0].shape[0] // 2
    start, stop, _ = rows.indices(half)
    return refs[0][side * half + start : side * half + stop]


def gather_kernel(sums_ref, *refs):
    halo_refs, out_ref = refs[:-1], refs[-1]
    rows = sums_ref.shape[0]
    out_ref[:rows, :] = sums_ref[...]
    out_ref[rows:, :] = jnp.concatenate([halo_rows(halo_refs, 0), halo_rows(halo_refs, 1)], axis=1)

def half_slices(width):
    low, high = [], []
    for plane in range(width // PLANE):
        low.append((plane * PLANE, plane * HALF))
        high.append((plane * PLANE + HALF, plane * HALF))
    return low, high


def move_rows(rows_ref, plane, value_ref, send_ref, side, first):
    cells, width = value_ref.shape
    ranges = half_slices(width)[side]

    def move(at, _):
        row = rows_ref[0, plane, at]
        for source, target in ranges:
            send_ref[pl.ds(first + at, 1), target : target + HALF] = value_ref[
                pl.ds(row, 1), source : source + HALF
            ]
        return 0

    lax.fori_loop(0, cells // 2, move, 0, unroll=8)


def wall_rows(temp_ref):
    cooling = (-0.5 * LOG2E) / temp_ref[...]
    axis_point = point(lax.broadcasted_iota(jnp.int32, (NV, 1), 0))
    profile = jnp.exp2(axis_point * axis_point * cooling)
    mass = jnp.sum(profile, axis=0, keepdims=True)
    flux = jnp.sum(jnp.maximum(axis_point, 0.0) * profile, axis=0, keepdims=True)
    return 1.0 / (WEIGHT * flux * mass * mass), cooling


def near_plane_kernel(rows_ref, face_ref, temp_ref, mask_ref, dist_ref, send_ref):
    cells, _ = dist_ref.shape
    count = cells // 2
    inv_norm, cooling = wall_rows(temp_ref)
    notes = jnp.concatenate([mask_ref[...].astype(F32), inv_norm, cooling], axis=0)
    low, high = face_hits(face_ref, cells)
    for side, hits in ((1, high), (0, low)):
        first = (1 - side) * (count + NOTES)
        send_ref[first + count : first + count + NOTES, :count] = exact(notes, hits.astype(BF16))
        move_rows(rows_ref, side, dist_ref, send_ref, side, first)


def far_plane_kernel(rows_ref, dist_ref, send_ref):
    for side in (1, 0):
        first = (1 - side) * (dist_ref.shape[0] // 2)
        move_rows(rows_ref, 1 - side, dist_ref, send_ref, side, first)


def picks(near_ref, mask_ref, face, cell_start, cells):
    index = near_ref[face : face + 1, :] - cell_start
    hit = lax.broadcasted_iota(jnp.int32, (cells, cells), 0) == index
    open_face = mask_ref[face : face + 1, :] != 1
    return jnp.where(hit & open_face, 1.0, 0.0).astype(F32)


def along(near_ref, mask_ref, upward):
    cells = near_ref.shape[1]
    cell_start = lax.axis_index("space") * cells
    faces = [picks(near_ref, mask_ref, face, cell_start, cells) for face in range(6)]
    return [faces[0], faces[1], jnp.where(upward, faces[2], faces[3]), faces[4], faces[5]]


def stream_tiles(near_ref, mask_ref, value_ref, store):
    cells, width = value_ref.shape
    planes, upward = planes_y(width)
    chosen = []
    for face in along(near_ref, mask_ref, upward):
        flipped = face.T.astype(BF16)
        chosen.append(jnp.concatenate([flipped, flipped], axis=1))
    rest = jnp.concatenate(chosen[2:], axis=0)
    for start in range(0, width, COLUMN_TILE):
        side = chosen[0] if start % PLANE >= HALF else chosen[1]
        vel_x, vel_z = lane_points(start, COLUMN_TILE)
        values = value_ref[:, start : start + COLUMN_TILE]
        pieces = jnp.concatenate(split(values, 2), axis=0)
        moved = dot(jnp.concatenate([side, rest], axis=0), pieces)
        speed_x, speed_z = jnp.abs(vel_x), jnp.abs(vel_z)
        speed_y = jnp.abs(planes[start // PLANE])
        from_z = jnp.where(vel_z > 0, moved[2 * cells : 3 * cells], moved[3 * cells :])
        stream = (
            speed_x * moved[:cells]
            + speed_y * moved[cells : 2 * cells]
            + speed_z * from_z
            - (speed_x + speed_y + speed_z) * values
        )
        store(slice(start, start + COLUMN_TILE), values, stream)


def stream_kernel(near_ref, mask_ref, value_ref, out_ref):
    def store(lanes, values, stream):
        out_ref[:, lanes] = TIME_STEP * stream

    stream_tiles(near_ref, mask_ref, value_ref, store)


def stream_last_kernel(near_ref, mask_ref, dist_ref, middle_ref, out_ref):
    def store(lanes, values, stream):
        out_ref[:, lanes] = 0.5 * (dist_ref[:, lanes] + values) + (0.5 * TIME_STEP) * stream

    stream_tiles(near_ref, mask_ref, middle_ref, store)


def wall_kernel(face_ref, temp_ref, mask_ref, shape_ref, back_ref, side_ref):
    cells, width = shape_ref.shape
    count = cells // 2
    planes, _ = planes_y(width)
    inv_norm, cooling = wall_rows(temp_ref)
    mask = mask_ref[...]
    back_ref[...] = jnp.concatenate(
        [jnp.where(mask == 1, inv_norm, 0.0), cooling, jnp.zeros((1, cells), F32)],
        axis=0,
    )
    rows = [mask[:2].astype(F32), cooling, jnp.zeros((LANES - 3, cells), F32)]
    columns = jnp.concatenate(rows, axis=0).T
    row = lax.broadcasted_iota(jnp.int32, (cells, count), 0)
    for side, face in enumerate((1, 0)):
        hit = (row == face_ref[0, face : face + 1, :]) & (columns[:, face : face + 1] != 1.0)
        picked = jnp.where(hit, 1.0, 0.0).astype(BF16)
        side_ref[side * cells : (side + 1) * cells, :] = jnp.concatenate([picked, picked], axis=1)
    cooling = jnp.broadcast_to(columns[:, 2:3], (cells, LANES))
    for start in range(0, PLANE, LANES):
        vel_x, vel_z = lane_points(start, LANES)
        flat = vel_x * vel_x + vel_z * vel_z
        for at, vel_y in enumerate(planes):
            lanes = slice(at * PLANE + start, at * PLANE + start + LANES)
            shape_ref[:, lanes] = jnp.exp2((flat + vel_y * vel_y) * cooling)


def coefficients(sums, back, step, keep):
    count = sums[0:1]
    inv_count = 1.0 / count
    flow_x = (sums[11:12] - sums[10:11]) * inv_count
    flow_y = (sums[13:14] - sums[12:13]) * inv_count
    flow_z = (sums[15:16] - sums[14:15]) * inv_count
    p_xx, p_yy, p_zz, p_xy, p_xz, p_yz = (sums[at : at + 1] for at in range(1, 7))
    energy = p_xx + p_yy + p_zz
    flow_sq = flow_x * flow_x + flow_y * flow_y + flow_z * flow_z
    temp = (energy * inv_count - flow_sq) / 3.0
    inv_temp = 1.0 / temp

    def heat(third, flow, press):
        return 0.5 * (
            third
            - 2.0 * (press[0] * flow_x + press[1] * flow_y + press[2] * flow_z)
            - flow * energy
            + 2.0 * count * flow * flow_sq
        )

    scale = ((1.0 - MOMENTUM_RATIO) / 5.0) * inv_count * inv_temp * inv_temp * (-2.0 / LOG2E)
    rate = (count * jnp.exp((1.0 - SHEAR_EXPONENT) * jnp.log(temp))) * (step / BASELINE_SHEAR)
    returned = (back[0:6] * step) * sums[10:16]
    rows = [
        flow_x,
        flow_y,
        flow_z,
        (-0.5 * LOG2E) * inv_temp,
        scale * heat(sums[7:8], flow_x, (p_xx, p_xy, p_xz)),
        scale * heat(sums[8:9], flow_y, (p_xy, p_yy, p_yz)),
        scale * heat(sums[9:10], flow_z, (p_xz, p_yz, p_zz)),
        count * inv_temp * lax.rsqrt(temp) * rate,
        keep - rate,
    ]
    return rows, returned


def columns_of(sums, back, width, step, keep):
    _, upward = planes_y(width)
    rows, returned = coefficients(sums, back, step, keep)
    rows += [
        jnp.where(upward, returned[2:3], returned[3:4]),
        returned[0:2],
        returned[4:6],
        jnp.zeros((LANES - 14, sums.shape[1]), F32),
    ]
    return jnp.concatenate(rows, axis=0).T


def relax(columns_ref, base_ref, value_ref, shape_ref, out_ref, half=False):
    cells, width = value_ref.shape
    planes, _ = planes_y(2 * width if half else width)
    lane = lax.broadcasted_iota(jnp.int32, (ROWS, LANES), 1)
    first_x, vel_z = point((lane >> 5) & (NV - 1)), point(lane & (NV - 1))
    z_plus, z_minus = jnp.maximum(vel_z, 0.0), jnp.maximum(-vel_z, 0.0)

    def group(at, _, tiles=range(PLANE // LANES), stride=PLANE):
        rows = pl.ds(pl.multiple_of(at * ROWS, ROWS), ROWS)
        columns = columns_ref[rows, :]
        flow_x, flow_y, flow_z, cool, heat_x, heat_y, heat_z, gain, keep, back_y, *back = (
            jnp.broadcast_to(columns[:, column : column + 1], (ROWS, LANES)) for column in range(14)
        )
        rel_z = vel_z - flow_z
        square_z = rel_z * rel_z * cool
        heat_of_z = rel_z * heat_z
        back_z = z_plus * back[2] + z_minus * back[3]
        of_y = []
        for vel_y in planes:
            rel_y = vel_y - flow_y
            of_y.append((rel_y * rel_y * cool, rel_y * heat_y, jnp.abs(vel_y) * back_y))
        for tile in tiles:
            vel_x = first_x + (tile * (LANES // NV)) * SPACING
            rel_x = vel_x - flow_x
            square_xz = rel_x * rel_x * cool + square_z
            heat_xz = rel_x * heat_x + heat_of_z
            upper = tile * LANES >= HALF
            back_xz = jnp.abs(vel_x) * (back[0] if upper else back[1]) + back_z
            for plane, (square_y, heat_of_y, back_of_y) in enumerate(of_y):
                start = plane * stride + (tile - tiles[0]) * LANES
                lanes = slice(start, start + LANES)
                square = square_xz + square_y
                skew = (heat_xz + heat_of_y) * (square + 2.5 * LOG2E) + 1.0
                out_ref[rows, lanes] = (
                    base_ref[rows, lanes]
                    + keep * value_ref[rows, lanes]
                    + gain * jnp.exp2(square) * skew
                    + shape_ref[rows, lanes] * (back_xz + back_of_y)
                )
        return 0

    groups = cells // ROWS
    if half:
        low, high = range(HALF // LANES), range(HALF // LANES, PLANE // LANES)
        lax.fori_loop(0, groups // 2, functools.partial(group, tiles=high, stride=HALF), 0)
        lax.fori_loop(groups // 2, groups, functools.partial(group, tiles=low, stride=HALF), 0)
    else:
        lax.fori_loop(0, groups, group, 0)


def middle_kernel(sums_ref, back_ref, side_ref, own_ref, stream_ref, shape_ref, *refs):
    halo_refs, (out_ref, columns_ref, base_ref) = refs[:-3], refs[-3:]
    cells, width = own_ref.shape
    columns_ref[...] = columns_of(sums_ref[:SUMS], back_ref[...], width, TIME_STEP, 1.0)
    for side, ranges in enumerate(half_slices(width)):
        pick = side_ref[side * cells : (side + 1) * cells, :]
        for source, target in ranges:
            for tile in range(0, HALF, COLUMN_TILE):
                lanes = slice(source + tile, source + tile + COLUMN_TILE)
                vel_x, _ = lane_points(source + tile, COLUMN_TILE)
                rows = halo_rows(halo_refs, 1 - side, slice(0, cells // 2))
                rows = rows[:, target + tile : target + tile + COLUMN_TILE]
                halo = dot(pick, jnp.concatenate(split(rows, 2), axis=0))
                base_ref[:, lanes] = stream_ref[:, lanes] + (TIME_STEP * jnp.abs(vel_x)) * halo
    relax(columns_ref, base_ref, own_ref, shape_ref, out_ref)


def relax_kernel(sums_ref, back_ref, middle_ref, part_ref, shape_ref, out_ref, columns_ref):
    width = middle_ref.shape[1]
    step = 0.5 * TIME_STEP
    columns_ref[...] = columns_of(sums_ref[...], back_ref[...], width, step, 0.0)
    relax(columns_ref, part_ref, middle_ref, shape_ref, out_ref)


ORDERS = (
    [(0, 0, 0)],
    [(2, 0, 0)],
    [(0, 2, 0)],
    [(0, 0, 2)],
    [(1, 1, 0)],
    [(1, 0, 1)],
    [(0, 1, 1)],
    [(3, 0, 0), (1, 2, 0), (1, 0, 2)],
    [(0, 3, 0), (2, 1, 0), (0, 1, 2)],
    [(0, 0, 3), (2, 0, 1), (0, 2, 1)],
    [("-", 0, 0)],
    [("+", 0, 0)],
    [(0, "-", 0)],
    [(0, "+", 0)],
    [(0, 0, "-")],
    [(0, 0, "+")],
)


def power(value, order):
    if order == "+":
        return jnp.maximum(value, 0.0)
    if order == "-":
        return jnp.maximum(-value, 0.0)
    result = None
    for _ in range(order):
        result = value if result is None else result * value
    return result


def advance_kernel(face_ref, near_ref, mask_ref, sums_ref, back_ref, out_ref):
    cells = near_ref.shape[1]
    count = cells // 2
    cell_start = lax.axis_index("space") * cells
    sums = sums_ref[:SUMS]
    flux = [sums_ref[SUMS * (face + 1) : SUMS * (face + 2)] for face in range(FACES)]
    gas = 0.0
    for face in range(FACES):
        hits = picks(near_ref, mask_ref, face, cell_start, cells).astype(BF16)
        gas += exact(flux[face], hits) - flux[face]
    arrived = sums_ref[SUMS * (FACES + 2) :]
    for face, hits in enumerate(face_hits(face_ref, cells)):
        found = exact(
            arrived[:, face * count : (face + 1) * count], hits.astype(BF16), ((1,), (1,))
        )
        gas += jnp.where(mask_ref[face : face + 1, :] != 1, found, 0.0)

    rows, returned = coefficients(sums, back_ref[...], TIME_STEP, 1.0)
    flows, cool, heats, gain, keep = rows[0:3], rows[3], rows[4:7], rows[7], rows[8]
    points = jnp.broadcast_to(point(lax.broadcasted_iota(jnp.int32, (NV, cells), 0)), (NV, cells))
    axes = []
    for flow in flows:
        off = points - flow
        bell = jnp.exp2(off * off * cool)
        axes.append([bell, bell * off, bell * off * off, bell * off * off * off])
    known = {}

    def along_axis(axis, order):
        if (axis, order) not in known:
            factor = power(points, order)
            known[axis, order] = [
                jnp.sum(term if factor is None else factor * term, axis=0, keepdims=True)
                for term in axes[axis]
            ]
        return known[axis, order]

    wall_bell = jnp.exp2(points * points * back_ref[6:7])
    above = jnp.maximum(points, 0.0)
    wall_sums = [jnp.sum(jnp.where(points > 0, wall_bell, 0.0), axis=0, keepdims=True)]
    for _ in range(4):
        wall_bell = wall_bell * above
        wall_sums.append(jnp.sum(wall_bell, axis=0, keepdims=True))

    def wall_full(order):
        if order in ("+", "-"):
            return wall_sums[1]
        return None if order % 2 else 2.0 * wall_sums[order]

    def wall_half(order, sign):
        if order in ("+", "-"):
            return wall_sums[2] if order == sign else None
        found = wall_sums[order + 1]
        return -found if order % 2 and sign == "-" else found

    found_rows = []
    for orders in ORDERS:
        bells, walls = 0.0, 0.0
        for order in orders:
            (x0, x1, x2, x3), (y0, y1, y2, y3), (z0, z1, z2, z3) = (
                along_axis(axis, order[axis]) for axis in range(3)
            )
            xy, xz, yz = x0 * y0, x0 * z0, y0 * z0
            skew = heats[0] * (x1 * (BEND * yz + cool * (y2 * z0 + y0 * z2)) + cool * x3 * yz)
            skew += heats[1] * (y1 * (BEND * xz + cool * (x2 * z0 + x0 * z2)) + cool * y3 * xz)
            skew += heats[2] * (z1 * (BEND * xy + cool * (x2 * y0 + x0 * y2)) + cool * z3 * xy)
            bells += xy * z0 + skew
            for face in range(FACES):
                terms = [
                    wall_half(order[axis], "+-"[face % 2])
                    if axis == face // 2
                    else wall_full(order[axis])
                    for axis in range(3)
                ]
                if all(term is not None for term in terms):
                    walls += returned[face : face + 1] * terms[0] * terms[1] * terms[2]
        found_rows.append(gain * bells + walls)
    found = WEIGHT * jnp.concatenate(found_rows, axis=0)
    out_ref[...] = found + keep * sums + TIME_STEP * gas


def halo_stream_kernel(face_ref, near_ref, *refs):
    halo_refs, (base_ref, shape_ref, values_ref, notes_ref, open_ref) = refs[:-5], refs[-5:]
    rows, width = base_ref.shape
    count = rows // 2
    planes, upward = planes_y(2 * width)
    cell_start = lax.axis_index("space") * rows
    notes = jnp.concatenate(
        [halo_rows(halo_refs, side, slice(count, count + NOTES))[:, :count] for side in range(2)],
        axis=1,
    )
    notes_ref[...] = notes
    passing = jnp.where(notes[:FACES] != 1.0, 1.0, 0.0)
    lane = lax.broadcasted_iota(jnp.int32, (1, rows), 1)
    picked = [
        jnp.where(lane < count, passing[0:1], passing[1:2]),
        jnp.where(upward, passing[2:3], passing[3:4]),
        passing[4:6],
        notes[7:8],
        jnp.zeros((LANES - 5, rows), F32),
    ]
    columns = jnp.concatenate(picked, axis=0).T
    open_x, open_y, open_low, open_high, cooling = (
        jnp.broadcast_to(columns[:, at : at + 1], (rows, LANES)) for at in range(5)
    )
    open_ref[...] = TIME_STEP * open_x
    low = face_hits(face_ref, rows)[0]
    low_flipped, low = low.T.astype(BF16), low.astype(BF16)
    row = lax.broadcasted_iota(jnp.int32, (rows, rows), 0)
    steps = []
    for face in range(2, FACES):
        hits = jnp.where(row == near_ref[face : face + 1, :] - cell_start, 1.0, 0.0)
        from_rows = dot(low_flipped, hits.T.astype(BF16)).astype(BF16)
        steps.append(dot(from_rows, low))
    along_y = jnp.where(upward, steps[0], steps[1])
    picks_all = jnp.concatenate([along_y, steps[2], steps[3]], axis=0).astype(BF16)
    picks_all = jnp.concatenate([picks_all, picks_all], axis=1)
    for side in range(2):
        block = slice(side * count, (side + 1) * count)
        values_ref[block, :] = halo_rows(halo_refs, side, slice(0, count))

        def wide(column):
            return jnp.concatenate([column[block]] * (COLUMN_TILE // LANES), axis=1)

        for start in range(0, width, COLUMN_TILE):
            lanes = slice(start, start + COLUMN_TILE)
            vel_x, vel_z = lane_points((1 - side) * HALF + start % HALF, COLUMN_TILE)
            vel_y = planes[start // HALF]
            values = values_ref[block, lanes]
            moved = dot(picks_all, jnp.concatenate(split(values, 2), axis=0))
            speed_x, speed_y, speed_z = jnp.abs(vel_x), jnp.abs(vel_y), jnp.abs(vel_z)
            from_z = jnp.where(
                vel_z > 0,
                wide(open_low) * moved[count : 2 * count],
                wide(open_high) * moved[2 * count :],
            )
            base_ref[block, lanes] = TIME_STEP * (
                speed_y * (wide(open_y) * moved[:count])
                + speed_z * from_z
                - (speed_x + speed_y + speed_z) * values
            )
            speed_sq = vel_x * vel_x + vel_y * vel_y + vel_z * vel_z
            shape_ref[block, lanes] = jnp.exp2(speed_sq * wide(cooling))


def halo_relax_kernel(sums_ref, notes_ref, base_ref, shape_ref, values_ref, out_ref, columns_ref):
    width = values_ref.shape[1]
    sums = sums_ref[SUMS * (FACES + 1) : SUMS * (FACES + 2)]
    notes = notes_ref[...]
    back = jnp.where(notes[:FACES] == 1.0, notes[6:7], 0.0)
    columns_ref[...] = columns_of(sums, back, 2 * width, TIME_STEP, 1.0)
    relax(columns_ref, base_ref, values_ref, shape_ref, out_ref, half=True)


def last_kernel(side_ref, part_ref, plane_ref, open_ref, *refs):
    halo_refs, (out_ref, result_ref, sems) = refs[:-3], refs[-3:]
    cells, width = part_ref.shape
    count = cells // 2
    copies = []
    for side, ranges in enumerate(half_slices(width)):
        pick = side_ref[side * cells : (side + 1) * cells, :]
        block = slice((1 - side) * count, (2 - side) * count)
        gate = jnp.concatenate([open_ref[block]] * (COLUMN_TILE // LANES), axis=1)
        for source, target in ranges:
            for tile in range(0, HALF, COLUMN_TILE):
                lanes = slice(source + tile, source + tile + COLUMN_TILE)
                there = slice(target + tile, target + tile + COLUMN_TILE)
                speed_x = jnp.abs(lane_points(source + tile, COLUMN_TILE)[0])
                rows = halo_rows(halo_refs, 1 - side)[:, there]
                rows = plane_ref[block, there] + gate * speed_x * rows
                halo = dot(pick, jnp.concatenate(split(rows, 2), axis=0))
                result_ref[:, lanes] = part_ref[:, lanes] + (0.5 * TIME_STEP * speed_x) * halo
                copy = pltpu.make_async_copy(
                    result_ref.at[:, lanes], out_ref.at[:, lanes], sems.at[len(copies)]
                )
                copy.start()
                copies.append(copy)
    for copy in copies:
        copy.wait()


def call(kernel, outs, arrays, scratch=(), scalars=0, far_outs=False):
    specs = [
        pl.BlockSpec(memory_space=pltpu.SMEM if at < scalars else pltpu.VMEM)
        for at in range(len(arrays))
    ]
    out_space = pltpu.HBM if far_outs else pltpu.VMEM
    size = sum(math.prod(array.shape) * 4 for array in arrays)
    return pl.pallas_call(
        kernel,
        out_shape=[jax.ShapeDtypeStruct(shape, dtype) for shape, dtype in outs],
        in_specs=specs,
        out_specs=[pl.BlockSpec(memory_space=out_space)] * len(outs),
        scratch_shapes=list(scratch),
        name=kernel.__name__,
        compiler_params=pltpu.CompilerParams(vmem_limit_bytes=40 * 2**20),
        cost_estimate=pl.CostEstimate(flops=COST.get(kernel.__name__, 0), bytes_accessed=size, transcendentals=0),
    )(*arrays)


COST = {"advance_kernel": 3 * 10**9}


def total(value):
    count = lax.axis_size("vel")
    step = 1
    while step < count:
        value = value + lax.ppermute(value, "vel", [(i, i ^ step) for i in range(count)])
        step *= 2
    return value


def exchange(send):
    count = lax.axis_size("space")
    forward = [(i, (i + 1) % count) for i in range(count)]
    backward = [(target, source) for source, target in forward]
    if count == 2:
        return [lax.ppermute(send, "space", forward)]
    half = send.shape[0] // 2
    return [
        lax.ppermute(send[:half], "space", forward),
        lax.ppermute(send[half:], "space", backward),
    ]


def on_device(dist, wall_temp, neighbours, wall_mask, face_rows):
    cells, width = dist.shape
    count, half = cells // 2, width // 2
    temp = wall_temp[None, :]
    whole, plane = ((cells, width), F32), ((cells, half), F32)
    every = SUMS * (FACES + 1)
    columns = pltpu.VMEM((cells, LANES), F32)

    own_sums, sent = call(
        sums_kernel, [((every, cells), F32), ((4 * SUMS, count), F32)], [face_rows, dist]
    )
    halo_sums = exchange(sent)
    (sent,) = call(
        near_plane_kernel,
        [((2 * (count + NOTES), half), F32)],
        [face_rows, face_rows, temp, wall_mask, dist],
        scalars=1,
    )
    near = exchange(sent)
    (sent,) = call(far_plane_kernel, [plane], [face_rows, dist], scalars=1)
    far = exchange(sent)
    (sums,) = call(gather_kernel, [((every + 2 * SUMS, cells), F32)], [own_sums, *halo_sums])
    shape, back, side = call(
        wall_kernel,
        [whole, ((8, cells), F32), ((2 * cells, cells), BF16)],
        [face_rows, temp, wall_mask],
    )
    (stream,) = call(stream_kernel, [whole], [neighbours, wall_mask, dist])
    base, halo_shape, values, notes, gate = call(
        halo_stream_kernel,
        [plane, plane, plane, ((NOTES, cells), F32), ((cells, LANES), F32)],
        [face_rows, neighbours, *near],
    )
    sums = total(sums)
    (middle,) = call(
        middle_kernel,
        [whole],
        [sums, back, side, dist, stream, shape, *near],
        [columns, pltpu.VMEM((cells, width), F32)],
    )
    (sums_two,) = call(
        advance_kernel, [((SUMS, cells), F32)], [face_rows, neighbours, wall_mask, sums, back]
    )
    (part,) = call(stream_last_kernel, [whole], [neighbours, wall_mask, dist, middle])
    (part,) = call(relax_kernel, [whole], [sums_two, back, middle, part, shape], [columns])
    (plane_one,) = call(
        halo_relax_kernel, [plane], [sums, notes, base, halo_shape, values], [columns]
    )
    (result,) = call(
        last_kernel,
        [whole],
        [side, part, plane_one, gate, *far],
        [pltpu.VMEM((cells, width), F32), pltpu.SemaphoreType.DMA((width // COLUMN_TILE,))],
        far_outs=True,
    )
    return result


def solution(mesh):
    return jax.shard_map(
        on_device,
        mesh=mesh,
        in_specs=(
            P("space", "vel"),
            P("space"),
            P(None, "space"),
            P(None, "space"),
            P("space", None, None),
        ),
        out_specs=P("space", "vel"),
        check_vma=False,
    )
```

```python
import functools
import math

import jax
import jax.numpy as jnp
from jax import lax
from jax.experimental import pallas as pl
from jax.experimental.pallas import tpu as pltpu
from jax.sharding import PartitionSpec as P

NV = 32
LIMIT = 4.5
SPACING = 2.0 * LIMIT / NV
WEIGHT = SPACING**3 * (2.0 * math.pi) ** (-1.5)
TIME_STEP = 0.05
BASELINE_SHEAR = 0.1
SHEAR_EXPONENT = 0.66
MOMENTUM_RATIO = 2.0 / 3.0
PLANE = NV * NV
HALF = PLANE // 2
ROWS = 8
LANES = 128
COLUMN_TILE = 256
SUMS = 16
FACES = 6
NOTES = 8
PARTS = 2
BEND = 2.5 * math.log2(math.e)
LOG2E = math.log2(math.e)
F32 = jnp.float32
BF16 = jnp.bfloat16


def point(slot):
    return -LIMIT + (slot.astype(F32) + 0.5) * SPACING


def lane_points(start, width):
    lane = lax.broadcasted_iota(jnp.int32, (1, width), 1) + start
    return point((lane >> 5) & (NV - 1)), point(lane & (NV - 1))


def planes_y(width):
    planes = width // PLANE
    first = lax.axis_index("vel") * planes
    return [point(first + at) for at in range(planes)], first >= NV // 2


def split(value, count):
    pieces = []
    for _ in range(count - 1):
        piece = value.astype(BF16)
        pieces.append(piece)
        value = value - piece.astype(F32)
    pieces.append(value.astype(BF16))
    return pieces


def dot(left, right, dims=((1,), (0,))):
    return lax.dot_general(left, right, (dims, ((), ())), preferred_element_type=F32)


def exact(left, right, dims=((1,), (0,))):
    rows = left.shape[0]
    found = dot(jnp.concatenate(split(left, 3), axis=0), right, dims)
    return found[:rows] + found[rows : 2 * rows] + found[2 * rows :]


def inward(vel_x, vel_y, vel_z):
    return [
        jnp.maximum(sign * vel, 0.0) for vel in (vel_x, vel_y, vel_z) for sign in (1.0, -1.0)
    ]


def weights(vel_x, vel_y, vel_z):
    speed_sq = vel_x * vel_x + vel_y * vel_y + vel_z * vel_z
    into = inward(vel_x, vel_y, vel_z)
    rows = [
        jnp.ones_like(vel_x),
        vel_x * vel_x,
        vel_y * vel_y,
        vel_z * vel_z,
        vel_x * vel_y,
        vel_x * vel_z,
        vel_y * vel_z,
        vel_x * speed_sq,
        vel_y * speed_sq,
        vel_z * speed_sq,
        into[1],
        into[0],
        into[3],
        into[2],
        into[5],
        into[4],
    ]
    return WEIGHT * jnp.concatenate(rows, axis=0), into


def face_hits(face_ref, cells):
    row = lax.broadcasted_iota(jnp.int32, (cells, face_ref.shape[2]), 0)
    return [jnp.where(row == face_ref[0, side : side + 1, :], 1.0, 0.0) for side in range(2)]


def sums_kernel(dist_ref, sums_ref):
    width = dist_ref.shape[1]
    planes, _ = planes_y(width)
    total = None
    for start in range(0, width, HALF):
        lanes = slice(start, start + HALF)
        vel_x, vel_z = lane_points(start, HALF)
        vel_y = jnp.full((1, HALF), planes[start // PLANE])
        base, into = weights(vel_x, vel_y, vel_z)
        table = jnp.concatenate([base] + [base * speed for speed in into], axis=0)
        coarse, fine = split(table, 2)
        finest = split(base, 3)[2]
        pieces = split(dist_ref[:, lanes], 3)
        across = ((1,), (1,))
        one = dot(jnp.concatenate([coarse, fine, finest], axis=0), pieces[0], across)
        two = dot(jnp.concatenate([coarse, fine], axis=0), pieces[1], across)
        three = dot(coarse, pieces[2], across)
        rows = table.shape[0]
        part = one[:rows] + one[rows : 2 * rows] + two[:rows] + two[rows:] + three
        part = jnp.concatenate([part[:SUMS] + one[2 * rows :], part[SUMS:]], axis=0)
        total = part if total is None else total + part
    sums_ref[...] = total


def share_kernel(face_ref, sums_ref, notes_ref, send_ref):
    low, high = face_hits(face_ref, sums_ref.shape[1])
    total, notes = sums_ref[: 3 * SUMS], notes_ref[...]
    base, from_low, from_high = total[:SUMS], total[SUMS : 2 * SUMS], total[2 * SUMS :]
    upward = exact(jnp.concatenate([base, from_low, notes], axis=0), high.astype(BF16))
    downward = exact(jnp.concatenate([base, from_high, notes], axis=0), low.astype(BF16))
    send_ref[...] = jnp.concatenate([upward, downward], axis=0)


def halo_rows(refs, side, rows=slice(None)):
    if len(refs) == 2:
        return refs[side][rows]
    half = refs[0].shape[0] // 2
    start, stop, _ = rows.indices(half)
    return refs[0][side * half + start : side * half + stop]


def shared_rows(refs, start, stop):
    rows = slice(start, stop)
    return jnp.concatenate([halo_rows(refs, 0, rows), halo_rows(refs, 1, rows)], axis=1)


def half_tiles(width, part=0, parts=1):
    half = width // 2
    lanes = range(part * half // parts, (part + 1) * half // parts, COLUMN_TILE)
    low = [(lane // HALF * PLANE + lane % HALF, lane) for lane in lanes]
    return low, [(source + HALF, target) for source, target in low]


def move_rows(rows_ref, value_ref, send_ref, crossed, part=0, parts=1):
    cells, width = value_ref.shape
    count = cells // 2
    low, high = half_tiles(width, part, parts)
    begin = low[0][1]

    def move(at, _):
        for first, tiles, plane in ((0, high, 1 - crossed), (count, low, crossed)):
            row = rows_ref[0, plane, at]
            for source, target in tiles:
                send_ref[pl.ds(first + at, 1), target - begin : target - begin + COLUMN_TILE] = (
                    value_ref[pl.ds(row, 1), source : source + COLUMN_TILE]
                )
        return 0

    lax.fori_loop(0, count, move, 0, unroll=True)


def wall_rows(temp_ref):
    cooling = (-0.5 * LOG2E) / temp_ref[...]
    axis_point = point(lax.broadcasted_iota(jnp.int32, (NV, 1), 0))
    profile = jnp.exp2(axis_point * axis_point * cooling)
    mass = jnp.sum(profile, axis=0, keepdims=True)
    flux = jnp.sum(jnp.maximum(axis_point, 0.0) * profile, axis=0, keepdims=True)
    return 1.0 / (WEIGHT * flux * mass * mass), cooling


def near_plane_kernel(rows_ref, dist_ref, send_ref):
    move_rows(rows_ref, dist_ref, send_ref, 0)


def far_plane_kernel(part, rows_ref, dist_ref, *refs):
    move_rows(rows_ref, dist_ref, refs[-1], 1, part, PARTS)


def picks(near_ref, mask_ref, face, cell_start, cells):
    index = near_ref[face : face + 1, :] - cell_start
    hit = lax.broadcasted_iota(jnp.int32, (cells, cells), 0) == index
    open_face = mask_ref[face : face + 1, :] != 1
    return jnp.where(hit & open_face, 1.0, 0.0).astype(F32)


def along(near_ref, mask_ref, upward):
    cells = near_ref.shape[1]
    cell_start = lax.axis_index("space") * cells
    faces = [picks(near_ref, mask_ref, face, cell_start, cells) for face in range(6)]
    return [faces[0], faces[1], jnp.where(upward, faces[2], faces[3]), faces[4], faces[5]]


def stream_tiles(near_ref, mask_ref, value_ref, store):
    cells, width = value_ref.shape
    planes, upward = planes_y(width)
    chosen = []
    for face in along(near_ref, mask_ref, upward):
        flipped = face.T.astype(BF16)
        chosen.append(jnp.concatenate([flipped, flipped], axis=1))
    rest = jnp.concatenate(chosen[2:], axis=0)
    for start in range(0, width, COLUMN_TILE):
        side = chosen[0] if start % PLANE >= HALF else chosen[1]
        vel_x, vel_z = lane_points(start, COLUMN_TILE)
        values = value_ref[:, start : start + COLUMN_TILE]
        pieces = jnp.concatenate(split(values, 2), axis=0)
        moved = dot(jnp.concatenate([side, rest], axis=0), pieces)
        speed_x, speed_z = jnp.abs(vel_x), jnp.abs(vel_z)
        speed_y = jnp.abs(planes[start // PLANE])
        from_z = jnp.where(vel_z > 0, moved[2 * cells : 3 * cells], moved[3 * cells :])
        stream = (
            speed_x * moved[:cells]
            + speed_y * moved[cells : 2 * cells]
            + speed_z * from_z
            - (speed_x + speed_y + speed_z) * values
        )
        store(slice(start, start + COLUMN_TILE), values, stream)


def stream_kernel(near_ref, mask_ref, value_ref, out_ref):
    def store(lanes, values, stream):
        out_ref[:, lanes] = TIME_STEP * stream

    stream_tiles(near_ref, mask_ref, value_ref, store)


def stream_last_kernel(near_ref, mask_ref, dist_ref, middle_ref, out_ref):
    def store(lanes, values, stream):
        out_ref[:, lanes] = 0.5 * (dist_ref[:, lanes] + values) + (0.5 * TIME_STEP) * stream

    stream_tiles(near_ref, mask_ref, middle_ref, store)


def wall_kernel(face_ref, temp_ref, mask_ref, shape_ref, back_ref, side_ref, notes_ref):
    cells, width = shape_ref.shape
    count = cells // 2
    planes, _ = planes_y(width)
    inv_norm, cooling = wall_rows(temp_ref)
    mask = mask_ref[...]
    notes_ref[...] = jnp.concatenate([mask.astype(F32), inv_norm, cooling], axis=0)
    back_ref[...] = jnp.concatenate(
        [jnp.where(mask == 1, inv_norm, 0.0), cooling, jnp.zeros((1, cells), F32)],
        axis=0,
    )
    rows = [mask[:2].astype(F32), cooling, jnp.zeros((LANES - 3, cells), F32)]
    columns = jnp.concatenate(rows, axis=0).T
    row = lax.broadcasted_iota(jnp.int32, (cells, count), 0)
    for side, face in enumerate((1, 0)):
        hit = (row == face_ref[0, face : face + 1, :]) & (columns[:, face : face + 1] != 1.0)
        picked = jnp.where(hit, 1.0, 0.0).astype(BF16)
        side_ref[side * cells : (side + 1) * cells, :] = jnp.concatenate([picked, picked], axis=1)
    cooling = jnp.broadcast_to(columns[:, 2:3], (cells, LANES))
    for start in range(0, PLANE, LANES):
        vel_x, vel_z = lane_points(start, LANES)
        flat = vel_x * vel_x + vel_z * vel_z
        for at, vel_y in enumerate(planes):
            lanes = slice(at * PLANE + start, at * PLANE + start + LANES)
            shape_ref[:, lanes] = jnp.exp2((flat + vel_y * vel_y) * cooling)


def coefficients(sums, back, step, keep):
    count = sums[0:1]
    inv_count = 1.0 / count
    flow_x = (sums[11:12] - sums[10:11]) * inv_count
    flow_y = (sums[13:14] - sums[12:13]) * inv_count
    flow_z = (sums[15:16] - sums[14:15]) * inv_count
    p_xx, p_yy, p_zz, p_xy, p_xz, p_yz = (sums[at : at + 1] for at in range(1, 7))
    energy = p_xx + p_yy + p_zz
    flow_sq = flow_x * flow_x + flow_y * flow_y + flow_z * flow_z
    temp = (energy * inv_count - flow_sq) / 3.0
    inv_temp = 1.0 / temp

    def heat(third, flow, press):
        return 0.5 * (
            third
            - 2.0 * (press[0] * flow_x + press[1] * flow_y + press[2] * flow_z)
            - flow * energy
            + 2.0 * count * flow * flow_sq
        )

    scale = ((1.0 - MOMENTUM_RATIO) / 5.0) * inv_count * inv_temp * inv_temp * (-2.0 / LOG2E)
    rate = (count * jnp.exp((1.0 - SHEAR_EXPONENT) * jnp.log(temp))) * (step / BASELINE_SHEAR)
    returned = (back[0:6] * step) * sums[10:16]
    rows = [
        flow_x,
        flow_y,
        flow_z,
        (-0.5 * LOG2E) * inv_temp,
        scale * heat(sums[7:8], flow_x, (p_xx, p_xy, p_xz)),
        scale * heat(sums[8:9], flow_y, (p_xy, p_yy, p_yz)),
        scale * heat(sums[9:10], flow_z, (p_xz, p_yz, p_zz)),
        count * inv_temp * lax.rsqrt(temp) * rate,
        keep - rate,
    ]
    return rows, returned


def columns_of(sums, back, width, step, keep):
    _, upward = planes_y(width)
    rows, returned = coefficients(sums, back, step, keep)
    rows += [
        jnp.where(upward, returned[2:3], returned[3:4]),
        returned[0:2],
        returned[4:6],
        jnp.zeros((LANES - 14, sums.shape[1]), F32),
    ]
    return jnp.concatenate(rows, axis=0).T


def relax(columns_ref, base_ref, value_ref, shape_ref, out_ref, half=False):
    cells, width = value_ref.shape
    planes, _ = planes_y(2 * width if half else width)
    lane = lax.broadcasted_iota(jnp.int32, (ROWS, LANES), 1)
    first_x, vel_z = point((lane >> 5) & (NV - 1)), point(lane & (NV - 1))
    z_plus, z_minus = jnp.maximum(vel_z, 0.0), jnp.maximum(-vel_z, 0.0)

    def group(at, _, tiles=range(PLANE // LANES), stride=PLANE):
        rows = pl.ds(pl.multiple_of(at * ROWS, ROWS), ROWS)
        columns = columns_ref[rows, :]
        flow_x, flow_y, flow_z, cool, heat_x, heat_y, heat_z, gain, keep, back_y, *back = (
            jnp.broadcast_to(columns[:, column : column + 1], (ROWS, LANES)) for column in range(14)
        )
        rel_z = vel_z - flow_z
        square_z = rel_z * rel_z * cool
        heat_of_z = rel_z * heat_z
        back_z = z_plus * back[2] + z_minus * back[3]
        of_y = []
        for vel_y in planes:
            rel_y = vel_y - flow_y
            of_y.append((rel_y * rel_y * cool, rel_y * heat_y, jnp.abs(vel_y) * back_y))
        for tile in tiles:
            vel_x = first_x + (tile * (LANES // NV)) * SPACING
            rel_x = vel_x - flow_x
            square_xz = rel_x * rel_x * cool + square_z
            heat_xz = rel_x * heat_x + heat_of_z
            upper = tile * LANES >= HALF
            back_xz = jnp.abs(vel_x) * (back[0] if upper else back[1]) + back_z
            for plane, (square_y, heat_of_y, back_of_y) in enumerate(of_y):
                start = plane * stride + (tile - tiles[0]) * LANES
                lanes = slice(start, start + LANES)
                square = square_xz + square_y
                skew = (heat_xz + heat_of_y) * (square + 2.5 * LOG2E) + 1.0
                out_ref[rows, lanes] = (
                    base_ref[rows, lanes]
                    + keep * value_ref[rows, lanes]
                    + gain * jnp.exp2(square) * skew
                    + shape_ref[rows, lanes] * (back_xz + back_of_y)
                )
        return 0

    groups = cells // ROWS
    if half:
        low, high = range(HALF // LANES), range(HALF // LANES, PLANE // LANES)
        lax.fori_loop(
            0, groups // 2, functools.partial(group, tiles=high, stride=HALF), 0, unroll=True
        )
        lax.fori_loop(
            groups // 2, groups, functools.partial(group, tiles=low, stride=HALF), 0, unroll=True
        )
    else:
        lax.fori_loop(0, groups, group, 0, unroll=True)


def middle_kernel(sums_ref, back_ref, side_ref, own_ref, stream_ref, shape_ref, *refs):
    halo_refs, (out_ref, columns_ref, base_ref) = refs[:-3], refs[-3:]
    cells, width = own_ref.shape
    columns_ref[...] = columns_of(sums_ref[:SUMS], back_ref[...], width, TIME_STEP, 1.0)
    for side, tiles in enumerate(half_tiles(width)):
        pick = side_ref[side * cells : (side + 1) * cells, :]
        for source, target in tiles:
            lanes = slice(source, source + COLUMN_TILE)
            vel_x, _ = lane_points(source, COLUMN_TILE)
            rows = halo_rows(halo_refs, 1 - side)[:, target : target + COLUMN_TILE]
            halo = dot(pick, jnp.concatenate(split(rows, 2), axis=0))
            base_ref[:, lanes] = stream_ref[:, lanes] + (TIME_STEP * jnp.abs(vel_x)) * halo
    relax(columns_ref, base_ref, own_ref, shape_ref, out_ref)


def relax_kernel(sums_ref, back_ref, middle_ref, part_ref, shape_ref, out_ref, columns_ref):
    width = middle_ref.shape[1]
    step = 0.5 * TIME_STEP
    columns_ref[...] = columns_of(sums_ref[...], back_ref[...], width, step, 0.0)
    relax(columns_ref, part_ref, middle_ref, shape_ref, out_ref)


ORDERS = (
    [(0, 0, 0)],
    [(2, 0, 0)],
    [(0, 2, 0)],
    [(0, 0, 2)],
    [(1, 1, 0)],
    [(1, 0, 1)],
    [(0, 1, 1)],
    [(3, 0, 0), (1, 2, 0), (1, 0, 2)],
    [(0, 3, 0), (2, 1, 0), (0, 1, 2)],
    [(0, 0, 3), (2, 0, 1), (0, 2, 1)],
    [("-", 0, 0)],
    [("+", 0, 0)],
    [(0, "-", 0)],
    [(0, "+", 0)],
    [(0, 0, "-")],
    [(0, 0, "+")],
)


def power(value, order):
    if order == "+":
        return jnp.maximum(value, 0.0)
    if order == "-":
        return jnp.maximum(-value, 0.0)
    result = None
    for _ in range(order):
        result = value if result is None else result * value
    return result


def advance_kernel(face_ref, near_ref, _, mask_ref, sums_ref, back_ref, *refs):
    shared_refs, out_ref = refs[:-1], refs[-1]
    cells = near_ref.shape[1]
    cell_start = lax.axis_index("space") * cells
    sums = sums_ref[:SUMS]
    flux = [sums_ref[SUMS * (face + 1) : SUMS * (face + 2)] for face in range(FACES)]
    gas = 0.0
    for face in range(FACES):
        hits = picks(near_ref, mask_ref, face, cell_start, cells).astype(BF16)
        gas += exact(flux[face], hits) - flux[face]
    for face, hits in enumerate(face_hits(face_ref, cells)):
        arrived = halo_rows(shared_refs, face, slice(SUMS, 2 * SUMS))
        found = exact(arrived, hits.astype(BF16), ((1,), (1,)))
        gas += jnp.where(mask_ref[face : face + 1, :] != 1, found, 0.0)

    rows, returned = coefficients(sums, back_ref[...], TIME_STEP, 1.0)
    flows, cool, heats, gain, keep = rows[0:3], rows[3], rows[4:7], rows[7], rows[8]
    points = jnp.broadcast_to(point(lax.broadcasted_iota(jnp.int32, (NV, cells), 0)), (NV, cells))
    axes = []
    for flow in flows:
        off = points - flow
        bell = jnp.exp2(off * off * cool)
        axes.append([bell, bell * off, bell * off * off, bell * off * off * off])
    known = {}

    def along_axis(axis, order):
        if (axis, order) not in known:
            factor = power(points, order)
            known[axis, order] = [
                jnp.sum(term if factor is None else factor * term, axis=0, keepdims=True)
                for term in axes[axis]
            ]
        return known[axis, order]

    wall_bell = jnp.exp2(points * points * back_ref[6:7])
    above = jnp.maximum(points, 0.0)
    wall_sums = [jnp.sum(jnp.where(points > 0, wall_bell, 0.0), axis=0, keepdims=True)]
    for _ in range(4):
        wall_bell = wall_bell * above
        wall_sums.append(jnp.sum(wall_bell, axis=0, keepdims=True))

    def wall_full(order):
        if order in ("+", "-"):
            return wall_sums[1]
        return None if order % 2 else 2.0 * wall_sums[order]

    def wall_half(order, sign):
        if order in ("+", "-"):
            return wall_sums[2] if order == sign else None
        found = wall_sums[order + 1]
        return -found if order % 2 and sign == "-" else found

    found_rows = []
    for orders in ORDERS:
        bells, walls = 0.0, 0.0
        for order in orders:
            (x0, x1, x2, x3), (y0, y1, y2, y3), (z0, z1, z2, z3) = (
                along_axis(axis, order[axis]) for axis in range(3)
            )
            xy, xz, yz = x0 * y0, x0 * z0, y0 * z0
            skew = heats[0] * (x1 * (BEND * yz + cool * (y2 * z0 + y0 * z2)) + cool * x3 * yz)
            skew += heats[1] * (y1 * (BEND * xz + cool * (x2 * z0 + x0 * z2)) + cool * y3 * xz)
            skew += heats[2] * (z1 * (BEND * xy + cool * (x2 * y0 + x0 * y2)) + cool * z3 * xy)
            bells += xy * z0 + skew
            for face in range(FACES):
                terms = [
                    wall_half(order[axis], "+-"[face % 2])
                    if axis == face // 2
                    else wall_full(order[axis])
                    for axis in range(3)
                ]
                if all(term is not None for term in terms):
                    walls += returned[face : face + 1] * terms[0] * terms[1] * terms[2]
        found_rows.append(gain * bells + walls)
    found = WEIGHT * jnp.concatenate(found_rows, axis=0)
    out_ref[...] = found + keep * sums + TIME_STEP * gas


def halo_stream_kernel(face_ref, near_ref, *refs):
    base_ref, shape_ref, values_ref, open_ref = refs[-4:]
    refs = refs[:-4]
    shared_refs, halo_refs = refs[: len(refs) // 2], refs[len(refs) // 2 :]
    rows, width = base_ref.shape
    count = rows // 2
    planes, upward = planes_y(2 * width)
    cell_start = lax.axis_index("space") * rows
    notes = shared_rows(shared_refs, 2 * SUMS, 2 * SUMS + NOTES)
    passing = jnp.where(notes[:FACES] != 1.0, 1.0, 0.0)
    lane = lax.broadcasted_iota(jnp.int32, (1, rows), 1)
    picked = [
        jnp.where(lane < count, passing[0:1], passing[1:2]),
        jnp.where(upward, passing[2:3], passing[3:4]),
        passing[4:6],
        notes[7:8],
        jnp.zeros((LANES - 5, rows), F32),
    ]
    columns = jnp.concatenate(picked, axis=0).T
    open_x, open_y, open_low, open_high, cooling = (
        jnp.broadcast_to(columns[:, at : at + 1], (rows, LANES)) for at in range(5)
    )
    open_ref[...] = TIME_STEP * open_x
    low = face_hits(face_ref, rows)[0]
    low_flipped, low = low.T.astype(BF16), low.astype(BF16)
    row = lax.broadcasted_iota(jnp.int32, (rows, rows), 0)
    steps = []
    for face in range(2, FACES):
        hits = jnp.where(row == near_ref[face : face + 1, :] - cell_start, 1.0, 0.0)
        from_rows = dot(low_flipped, hits.T.astype(BF16)).astype(BF16)
        steps.append(dot(from_rows, low))
    along_y = jnp.where(upward, steps[0], steps[1])
    picks_all = jnp.concatenate([along_y, steps[2], steps[3]], axis=0).astype(BF16)
    picks_all = jnp.concatenate([picks_all, picks_all], axis=1)
    for side in range(2):
        block = slice(side * count, (side + 1) * count)
        values_ref[block, :] = halo_rows(halo_refs, side)

        def wide(column):
            return jnp.concatenate([column[block]] * (COLUMN_TILE // LANES), axis=1)

        for start in range(0, width, COLUMN_TILE):
            lanes = slice(start, start + COLUMN_TILE)
            vel_x, vel_z = lane_points((1 - side) * HALF + start % HALF, COLUMN_TILE)
            vel_y = planes[start // HALF]
            values = values_ref[block, lanes]
            moved = dot(picks_all, jnp.concatenate(split(values, 2), axis=0))
            speed_x, speed_y, speed_z = jnp.abs(vel_x), jnp.abs(vel_y), jnp.abs(vel_z)
            from_z = jnp.where(
                vel_z > 0,
                wide(open_low) * moved[count : 2 * count],
                wide(open_high) * moved[2 * count :],
            )
            base_ref[block, lanes] = TIME_STEP * (
                speed_y * (wide(open_y) * moved[:count])
                + speed_z * from_z
                - (speed_x + speed_y + speed_z) * values
            )
            speed_sq = vel_x * vel_x + vel_y * vel_y + vel_z * vel_z
            shape_ref[block, lanes] = jnp.exp2(speed_sq * wide(cooling))


def halo_relax_kernel(base_ref, shape_ref, values_ref, *refs):
    width = values_ref.shape[1]
    shared_refs, (out_ref, columns_ref) = refs[:-2], refs[-2:]
    sums = shared_rows(shared_refs, 0, SUMS)
    notes = shared_rows(shared_refs, 2 * SUMS, 2 * SUMS + NOTES)
    back = jnp.where(notes[:FACES] == 1.0, notes[6:7], 0.0)
    columns_ref[...] = columns_of(sums, back, 2 * width, TIME_STEP, 1.0)
    relax(columns_ref, base_ref, values_ref, shape_ref, out_ref, half=True)


def last_kernel(part, side_ref, part_ref, plane_ref, open_ref, *refs):
    refs, (out_ref, result_ref, sems) = refs[:-3], refs[-3:]
    halo_refs = refs[part > 0 :]
    cells, width = part_ref.shape
    count = cells // 2
    copies = []
    for side, tiles in enumerate(half_tiles(width, part, PARTS)):
        pick = side_ref[side * cells : (side + 1) * cells, :]
        block = slice((1 - side) * count, (2 - side) * count)
        gate = jnp.concatenate([open_ref[block]] * (COLUMN_TILE // LANES), axis=1)
        begin = tiles[0][1]
        for source, target in tiles:
            lanes = slice(source, source + COLUMN_TILE)
            speed_x = jnp.abs(lane_points(source, COLUMN_TILE)[0])
            rows = halo_rows(halo_refs, 1 - side)[:, target - begin : target - begin + COLUMN_TILE]
            rows = plane_ref[block, target : target + COLUMN_TILE] + gate * speed_x * rows
            halo = dot(pick, jnp.concatenate(split(rows, 2), axis=0))
            result_ref[:, lanes] = part_ref[:, lanes] + (0.5 * TIME_STEP * speed_x) * halo
            copy = pltpu.make_async_copy(
                result_ref.at[:, lanes], out_ref.at[:, lanes], sems.at[len(copies)]
            )
            copy.start()
            copies.append(copy)
    for copy in copies:
        copy.wait()


def call(kernel, outs, arrays, scratch=(), scalars=0, far_outs=False, unread=(), aliases=None):
    spaces = [
        pltpu.SMEM if at < scalars else pl.ANY if at in unread else pltpu.VMEM
        for at in range(len(arrays))
    ]
    if isinstance(kernel, functools.partial):
        name = f"{kernel.func.__name__}_{kernel.args[0]}"
    else:
        name = kernel.__name__
    size = sum(math.prod(array.shape) * 4 for array in arrays)
    return pl.pallas_call(
        kernel,
        out_shape=[jax.ShapeDtypeStruct(shape, dtype) for shape, dtype in outs],
        in_specs=[pl.BlockSpec(memory_space=space) for space in spaces],
        out_specs=[pl.BlockSpec(memory_space=pl.ANY if far_outs else pltpu.VMEM)] * len(outs),
        scratch_shapes=list(scratch),
        input_output_aliases=aliases or {},
        name=name,
        compiler_params=pltpu.CompilerParams(vmem_limit_bytes=40 * 2**20),
        cost_estimate=pl.CostEstimate(
            flops=COST.get(name, 0), bytes_accessed=size, transcendentals=0
        ),
    )(*arrays)


COST = {"advance_kernel": 10**9, "relax_kernel": 10**9, "last_kernel_0": 10**9}


def total(value):
    count = lax.axis_size("vel")
    step = 1
    while step < count:
        value = value + lax.ppermute(value, "vel", [(i, i ^ step) for i in range(count)])
        step *= 2
    return value


def exchange(send):
    count = lax.axis_size("space")
    forward = [(i, (i + 1) % count) for i in range(count)]
    backward = [(target, source) for source, target in forward]
    if count == 2:
        return [lax.ppermute(send, "space", forward)]
    half = send.shape[0] // 2
    return [
        lax.ppermute(send[:half], "space", forward),
        lax.ppermute(send[half:], "space", backward),
    ]


def on_device(dist, wall_temp, neighbours, wall_mask, face_rows):
    cells, width = dist.shape
    count, half = cells // 2, width // 2
    temp = wall_temp[None, :]
    whole, plane = ((cells, width), F32), ((cells, half), F32)
    every = SUMS * (FACES + 1)
    columns = pltpu.VMEM((cells, LANES), F32)

    (sent,) = call(near_plane_kernel, [plane], [face_rows, dist], scalars=1)
    near = exchange(sent)
    (sums,) = call(sums_kernel, [((every, cells), F32)], [dist])
    sums = total(sums)
    shape, back, side, notes = call(
        wall_kernel,
        [whole, ((8, cells), F32), ((2 * cells, cells), BF16), ((NOTES, cells), F32)],
        [face_rows, temp, wall_mask],
    )
    (stream,) = call(stream_kernel, [whole], [neighbours, wall_mask, dist])
    (sent,) = call(
        share_kernel, [((2 * (2 * SUMS + NOTES), count), F32)], [face_rows, sums, notes]
    )
    shared = exchange(sent)
    far = []
    for part in range(PARTS):
        after = [sent] if part else []
        (far_rows,) = call(
            functools.partial(far_plane_kernel, part),
            [((cells, half // PARTS), F32)],
            [face_rows, dist, *after],
            scalars=1,
            unread=(2,),
        )
        far.append(exchange(far_rows))
    (middle,) = call(
        middle_kernel,
        [whole],
        [sums, back, side, dist, stream, shape, *near],
        [columns, pltpu.VMEM((cells, width), F32)],
    )
    (part_sum,) = call(stream_last_kernel, [whole], [neighbours, wall_mask, dist, middle])
    (sums_two,) = call(
        advance_kernel,
        [((SUMS, cells), F32)],
        [face_rows, neighbours, part_sum, wall_mask, sums, back, *shared],
        unread=(2,),
    )
    (part_sum,) = call(relax_kernel, [whole], [sums_two, back, middle, part_sum, shape], [columns])
    base, halo_shape, values, gate = call(
        halo_stream_kernel,
        [plane, plane, plane, ((cells, LANES), F32)],
        [face_rows, neighbours, *shared, *near],
    )
    (plane_one,) = call(
        halo_relax_kernel, [plane], [base, halo_shape, values, *shared], [columns]
    )
    result = []
    for part in range(PARTS):
        result = call(
            functools.partial(last_kernel, part),
            [whole],
            [side, part_sum, plane_one, gate, *result, *far[part]],
            [
                pltpu.VMEM((cells, width), F32),
                pltpu.SemaphoreType.DMA((width // COLUMN_TILE // PARTS,)),
            ],
            far_outs=True,
            unread=(4,) if part else (),
            aliases={4: 0} if part else None,
        )
    return result[0]


def solution(mesh):
    return jax.shard_map(
        on_device,
        mesh=mesh,
        in_specs=(
            P("space", "vel"),
            P("space"),
            P(None, "space"),
            P(None, "space"),
            P("space", None, None),
        ),
        out_specs=P("space", "vel"),
        check_vma=False,
    )
```

```python
import functools
import math

import jax
import jax.numpy as jnp
from jax import lax
from jax.experimental import pallas as pl
from jax.experimental.pallas import tpu as pltpu
from jax.sharding import PartitionSpec as P

NV = 32
LIMIT = 4.5
SPACING = 2.0 * LIMIT / NV
WEIGHT = SPACING**3 * (2.0 * math.pi) ** (-1.5)
TIME_STEP = 0.05
BASELINE_SHEAR = 0.1
SHEAR_EXPONENT = 0.66
MOMENTUM_RATIO = 2.0 / 3.0
PLANE = NV * NV
HALF = PLANE // 2
ROWS = 8
LANES = 128
COLUMN_TILE = 256
SUMS = 16
FACES = 6
NOTES = 8
PARTS = 2
BEND = 2.5 * math.log2(math.e)
LOG2E = math.log2(math.e)
F32 = jnp.float32
BF16 = jnp.bfloat16


def point(slot):
    return -LIMIT + (slot.astype(F32) + 0.5) * SPACING


def lane_points(start, width):
    lane = lax.broadcasted_iota(jnp.int32, (1, width), 1) + start
    return point((lane >> 5) & (NV - 1)), point(lane & (NV - 1))


def planes_y(width):
    planes = width // PLANE
    first = lax.axis_index("vel") * planes
    return [point(first + at) for at in range(planes)], first >= NV // 2


def split(value, count):
    pieces = []
    for _ in range(count - 1):
        piece = value.astype(BF16)
        pieces.append(piece)
        value = value - piece.astype(F32)
    pieces.append(value.astype(BF16))
    return pieces


def dot(left, right, dims=((1,), (0,))):
    return lax.dot_general(left, right, (dims, ((), ())), preferred_element_type=F32)


def kept(face):
    other = face ^ 1
    return [*range(1, 10)] + [
        10 + out for out in range(FACES) if out == other or out // 2 > other // 2
    ]


def flux_start(face):
    return SUMS + sum(len(kept(before)) for before in range(face))


def flux_rows(base, packed, face):
    other = face ^ 1
    mine = packed[face]
    rows = [base[10 + other : 11 + other], mine[:9]]
    for out in range(FACES):
        if out == face:
            rows.append(jnp.zeros_like(mine[:1]))
            continue
        holder, row = (face, 10 + out) if 10 + out in kept(face) else (out ^ 1, 10 + other)
        at = kept(holder).index(row)
        rows.append(packed[holder][at : at + 1])
    return jnp.concatenate(rows, axis=0)


def exact(left, right, dims=((1,), (0,))):
    rows = left.shape[0]
    found = dot(jnp.concatenate(split(left, 3), axis=0), right, dims)
    return found[:rows] + found[rows : 2 * rows] + found[2 * rows :]


def inward(vel_x, vel_y, vel_z):
    return [
        jnp.maximum(sign * vel, 0.0) for vel in (vel_x, vel_y, vel_z) for sign in (1.0, -1.0)
    ]


def weights(vel_x, vel_y, vel_z):
    speed_sq = vel_x * vel_x + vel_y * vel_y + vel_z * vel_z
    into = inward(vel_x, vel_y, vel_z)
    rows = [
        jnp.ones_like(vel_x),
        vel_x * vel_x,
        vel_y * vel_y,
        vel_z * vel_z,
        vel_x * vel_y,
        vel_x * vel_z,
        vel_y * vel_z,
        vel_x * speed_sq,
        vel_y * speed_sq,
        vel_z * speed_sq,
        into[1],
        into[0],
        into[3],
        into[2],
        into[5],
        into[4],
    ]
    return WEIGHT * jnp.concatenate(rows, axis=0), into


def face_hits(face_ref, cells):
    row = lax.broadcasted_iota(jnp.int32, (cells, face_ref.shape[2]), 0)
    return [jnp.where(row == face_ref[0, side : side + 1, :], 1.0, 0.0) for side in range(2)]


def sums_kernel(dist_ref, sums_ref):
    width = dist_ref.shape[1]
    planes, _ = planes_y(width)
    total = None
    for start in range(0, width, HALF):
        lanes = slice(start, start + HALF)
        vel_x, vel_z = lane_points(start, HALF)
        vel_y = jnp.full((1, HALF), planes[start // PLANE])
        base, into = weights(vel_x, vel_y, vel_z)
        table = [base]
        for face, speed in enumerate(into):
            fluxes = base * speed
            table.append(fluxes[1:10])
            table += [fluxes[row : row + 1] for row in kept(face)[9:]]
        table = jnp.concatenate(table, axis=0)
        coarse, fine = split(table, 2)
        finest = split(base, 3)[2]
        pieces = split(dist_ref[:, lanes], 3)
        across = ((1,), (1,))
        one = dot(jnp.concatenate([coarse, fine, finest], axis=0), pieces[0], across)
        two = dot(jnp.concatenate([coarse, fine], axis=0), pieces[1], across)
        three = dot(coarse, pieces[2], across)
        rows = table.shape[0]
        part = one[:rows] + one[rows : 2 * rows] + two[:rows] + two[rows:] + three
        part = jnp.concatenate([part[:SUMS] + one[2 * rows :], part[SUMS:]], axis=0)
        total = part if total is None else total + part
    sums_ref[...] = total


def share_kernel(face_ref, sums_ref, notes_ref, send_ref):
    low, high = face_hits(face_ref, sums_ref.shape[1])
    for side, hits in ((0, high), (1, low)):
        rows = [sums_ref[:SUMS], notes_ref[...], sums_ref[flux_start(side) : flux_start(side + 1)]]
        rows = exact(jnp.concatenate(rows, axis=0), hits.astype(BF16))
        first = side * (send_ref.shape[0] // 2)
        send_ref[first : first + rows.shape[0], :] = rows


def halo_rows(refs, side, rows=slice(None)):
    if len(refs) == 2:
        return refs[side][rows]
    half = refs[0].shape[0] // 2
    start, stop, _ = rows.indices(half)
    return refs[0][side * half + start : side * half + stop]


def shared_rows(refs, start, stop):
    rows = slice(start, stop)
    return jnp.concatenate([halo_rows(refs, 0, rows), halo_rows(refs, 1, rows)], axis=1)


def half_tiles(width, part=0, parts=1):
    half = width // 2
    lanes = range(part * half // parts, (part + 1) * half // parts, COLUMN_TILE)
    low = [(lane // HALF * PLANE + lane % HALF, lane) for lane in lanes]
    return low, [(source + HALF, target) for source, target in low]


def move_rows(rows_ref, value_ref, send_ref, crossed, part=0, parts=1):
    cells, width = value_ref.shape
    count = cells // 2
    low, high = half_tiles(width, part, parts)
    begin = low[0][1]

    def move(at, _):
        for first, tiles, plane in ((0, high, 1 - crossed), (count, low, crossed)):
            row = rows_ref[0, plane, at]
            for source, target in tiles:
                send_ref[pl.ds(first + at, 1), target - begin : target - begin + COLUMN_TILE] = (
                    value_ref[pl.ds(row, 1), source : source + COLUMN_TILE]
                )
        return 0

    lax.fori_loop(0, count, move, 0, unroll=True)


def wall_rows(temp_ref):
    cooling = (-0.5 * LOG2E) / temp_ref[...]
    axis_point = point(lax.broadcasted_iota(jnp.int32, (NV, 1), 0))
    profile = jnp.exp2(axis_point * axis_point * cooling)
    mass = jnp.sum(profile, axis=0, keepdims=True)
    flux = jnp.sum(jnp.maximum(axis_point, 0.0) * profile, axis=0, keepdims=True)
    return 1.0 / (WEIGHT * flux * mass * mass), cooling


def near_plane_kernel(rows_ref, dist_ref, _, send_ref):
    move_rows(rows_ref, dist_ref, send_ref, 0)


def far_plane_kernel(part, rows_ref, dist_ref, *refs):
    move_rows(rows_ref, dist_ref, refs[-1], 1, part, PARTS)


def picks(near_ref, mask_ref, face, cell_start, cells):
    index = near_ref[face : face + 1, :] - cell_start
    hit = lax.broadcasted_iota(jnp.int32, (cells, cells), 0) == index
    open_face = mask_ref[face : face + 1, :] != 1
    return jnp.where(hit & open_face, 1.0, 0.0).astype(F32)


def along(near_ref, mask_ref, upward):
    cells = near_ref.shape[1]
    cell_start = lax.axis_index("space") * cells
    faces = [picks(near_ref, mask_ref, face, cell_start, cells) for face in range(6)]
    return [faces[0], faces[1], jnp.where(upward, faces[2], faces[3]), faces[4], faces[5]]


def stream_tiles(near_ref, mask_ref, value_ref, store):
    cells, width = value_ref.shape
    planes, upward = planes_y(width)
    chosen = []
    for face in along(near_ref, mask_ref, upward):
        flipped = face.T.astype(BF16)
        chosen.append(jnp.concatenate([flipped, flipped], axis=1))
    rest = jnp.concatenate(chosen[2:], axis=0)
    for start in range(0, width, COLUMN_TILE):
        side = chosen[0] if start % PLANE >= HALF else chosen[1]
        vel_x, vel_z = lane_points(start, COLUMN_TILE)
        values = value_ref[:, start : start + COLUMN_TILE]
        pieces = jnp.concatenate(split(values, 2), axis=0)
        moved = dot(jnp.concatenate([side, rest], axis=0), pieces)
        speed_x, speed_z = jnp.abs(vel_x), jnp.abs(vel_z)
        speed_y = jnp.abs(planes[start // PLANE])
        from_z = jnp.where(vel_z > 0, moved[2 * cells : 3 * cells], moved[3 * cells :])
        stream = (
            speed_x * moved[:cells]
            + speed_y * moved[cells : 2 * cells]
            + speed_z * from_z
            - (speed_x + speed_y + speed_z) * values
        )
        store(slice(start, start + COLUMN_TILE), values, stream)


def stream_kernel(near_ref, mask_ref, value_ref, out_ref):
    def store(lanes, values, stream):
        out_ref[:, lanes] = TIME_STEP * stream

    stream_tiles(near_ref, mask_ref, value_ref, store)


def stream_last_kernel(near_ref, mask_ref, dist_ref, middle_ref, out_ref):
    def store(lanes, values, stream):
        out_ref[:, lanes] = 0.5 * (dist_ref[:, lanes] + values) + (0.5 * TIME_STEP) * stream

    stream_tiles(near_ref, mask_ref, middle_ref, store)


def wall_kernel(face_ref, temp_ref, mask_ref, shape_ref, back_ref, side_ref, notes_ref):
    cells, width = shape_ref.shape
    count = cells // 2
    planes, _ = planes_y(width)
    inv_norm, cooling = wall_rows(temp_ref)
    mask = mask_ref[...]
    notes_ref[...] = jnp.concatenate([mask.astype(F32), inv_norm, cooling], axis=0)
    back_ref[...] = jnp.concatenate(
        [jnp.where(mask == 1, inv_norm, 0.0), cooling, jnp.zeros((1, cells), F32)],
        axis=0,
    )
    rows = [mask[:2].astype(F32), cooling, jnp.zeros((LANES - 3, cells), F32)]
    columns = jnp.concatenate(rows, axis=0).T
    row = lax.broadcasted_iota(jnp.int32, (cells, count), 0)
    for side, face in enumerate((1, 0)):
        hit = (row == face_ref[0, face : face + 1, :]) & (columns[:, face : face + 1] != 1.0)
        picked = jnp.where(hit, 1.0, 0.0).astype(BF16)
        side_ref[side * cells : (side + 1) * cells, :] = jnp.concatenate([picked, picked], axis=1)
    cooling = jnp.broadcast_to(columns[:, 2:3], (cells, LANES))
    for start in range(0, PLANE, LANES):
        vel_x, vel_z = lane_points(start, LANES)
        flat = vel_x * vel_x + vel_z * vel_z
        for at, vel_y in enumerate(planes):
            lanes = slice(at * PLANE + start, at * PLANE + start + LANES)
            shape_ref[:, lanes] = jnp.exp2((flat + vel_y * vel_y) * cooling)


def coefficients(sums, back, step, keep):
    count = sums[0:1]
    inv_count = 1.0 / count
    flow_x = (sums[11:12] - sums[10:11]) * inv_count
    flow_y = (sums[13:14] - sums[12:13]) * inv_count
    flow_z = (sums[15:16] - sums[14:15]) * inv_count
    p_xx, p_yy, p_zz, p_xy, p_xz, p_yz = (sums[at : at + 1] for at in range(1, 7))
    energy = p_xx + p_yy + p_zz
    flow_sq = flow_x * flow_x + flow_y * flow_y + flow_z * flow_z
    temp = (energy * inv_count - flow_sq) / 3.0
    inv_temp = 1.0 / temp

    def heat(third, flow, press):
        return 0.5 * (
            third
            - 2.0 * (press[0] * flow_x + press[1] * flow_y + press[2] * flow_z)
            - flow * energy
            + 2.0 * count * flow * flow_sq
        )

    scale = ((1.0 - MOMENTUM_RATIO) / 5.0) * inv_count * inv_temp * inv_temp * (-2.0 / LOG2E)
    rate = (count * jnp.exp((1.0 - SHEAR_EXPONENT) * jnp.log(temp))) * (step / BASELINE_SHEAR)
    returned = (back[0:6] * step) * sums[10:16]
    rows = [
        flow_x,
        flow_y,
        flow_z,
        (-0.5 * LOG2E) * inv_temp,
        scale * heat(sums[7:8], flow_x, (p_xx, p_xy, p_xz)),
        scale * heat(sums[8:9], flow_y, (p_xy, p_yy, p_yz)),
        scale * heat(sums[9:10], flow_z, (p_xz, p_yz, p_zz)),
        count * inv_temp * lax.rsqrt(temp) * rate,
        keep - rate,
    ]
    return rows, returned


def columns_of(sums, back, width, step, keep):
    _, upward = planes_y(width)
    rows, returned = coefficients(sums, back, step, keep)
    rows += [
        jnp.where(upward, returned[2:3], returned[3:4]),
        returned[0:2],
        returned[4:6],
        jnp.zeros((LANES - 14, sums.shape[1]), F32),
    ]
    return jnp.concatenate(rows, axis=0).T


def relax(columns_ref, base_ref, value_ref, shape_ref, out_ref, half=False):
    cells, width = value_ref.shape
    planes, _ = planes_y(2 * width if half else width)
    lane = lax.broadcasted_iota(jnp.int32, (ROWS, LANES), 1)
    first_x, vel_z = point((lane >> 5) & (NV - 1)), point(lane & (NV - 1))
    z_plus, z_minus = jnp.maximum(vel_z, 0.0), jnp.maximum(-vel_z, 0.0)

    def group(at, _, tiles=range(PLANE // LANES), stride=PLANE):
        rows = pl.ds(pl.multiple_of(at * ROWS, ROWS), ROWS)
        columns = columns_ref[rows, :]
        flow_x, flow_y, flow_z, cool, heat_x, heat_y, heat_z, gain, keep, back_y, *back = (
            jnp.broadcast_to(columns[:, column : column + 1], (ROWS, LANES)) for column in range(14)
        )
        rel_z = vel_z - flow_z
        square_z = rel_z * rel_z * cool
        heat_of_z = rel_z * heat_z
        back_z = z_plus * back[2] + z_minus * back[3]
        of_y = []
        for vel_y in planes:
            rel_y = vel_y - flow_y
            of_y.append((rel_y * rel_y * cool, rel_y * heat_y, jnp.abs(vel_y) * back_y))
        for tile in tiles:
            vel_x = first_x + (tile * (LANES // NV)) * SPACING
            rel_x = vel_x - flow_x
            square_xz = rel_x * rel_x * cool + square_z
            heat_xz = rel_x * heat_x + heat_of_z
            upper = tile * LANES >= HALF
            back_xz = jnp.abs(vel_x) * (back[0] if upper else back[1]) + back_z
            for plane, (square_y, heat_of_y, back_of_y) in enumerate(of_y):
                start = plane * stride + (tile - tiles[0]) * LANES
                lanes = slice(start, start + LANES)
                square = square_xz + square_y
                skew = (heat_xz + heat_of_y) * (square + 2.5 * LOG2E) + 1.0
                out_ref[rows, lanes] = (
                    base_ref[rows, lanes]
                    + keep * value_ref[rows, lanes]
                    + gain * jnp.exp2(square) * skew
                    + shape_ref[rows, lanes] * (back_xz + back_of_y)
                )
        return 0

    groups = cells // ROWS
    if half:
        low, high = range(HALF // LANES), range(HALF // LANES, PLANE // LANES)
        lax.fori_loop(
            0, groups // 2, functools.partial(group, tiles=high, stride=HALF), 0, unroll=True
        )
        lax.fori_loop(
            groups // 2, groups, functools.partial(group, tiles=low, stride=HALF), 0, unroll=True
        )
    else:
        lax.fori_loop(0, groups, group, 0, unroll=True)


def middle_kernel(sums_ref, back_ref, side_ref, own_ref, stream_ref, shape_ref, *refs):
    halo_refs, (out_ref, columns_ref, base_ref) = refs[:-3], refs[-3:]
    cells, width = own_ref.shape
    columns_ref[...] = columns_of(sums_ref[:SUMS], back_ref[...], width, TIME_STEP, 1.0)
    for side, tiles in enumerate(half_tiles(width)):
        pick = side_ref[side * cells : (side + 1) * cells, :]
        for source, target in tiles:
            lanes = slice(source, source + COLUMN_TILE)
            vel_x, _ = lane_points(source, COLUMN_TILE)
            rows = halo_rows(halo_refs, 1 - side)[:, target : target + COLUMN_TILE]
            halo = dot(pick, jnp.concatenate(split(rows, 2), axis=0))
            base_ref[:, lanes] = stream_ref[:, lanes] + (TIME_STEP * jnp.abs(vel_x)) * halo
    relax(columns_ref, base_ref, own_ref, shape_ref, out_ref)


def relax_kernel(sums_ref, back_ref, middle_ref, part_ref, shape_ref, out_ref, columns_ref):
    width = middle_ref.shape[1]
    step = 0.5 * TIME_STEP
    columns_ref[...] = columns_of(sums_ref[...], back_ref[...], width, step, 0.0)
    relax(columns_ref, part_ref, middle_ref, shape_ref, out_ref)


ORDERS = (
    [(0, 0, 0)],
    [(2, 0, 0)],
    [(0, 2, 0)],
    [(0, 0, 2)],
    [(1, 1, 0)],
    [(1, 0, 1)],
    [(0, 1, 1)],
    [(3, 0, 0), (1, 2, 0), (1, 0, 2)],
    [(0, 3, 0), (2, 1, 0), (0, 1, 2)],
    [(0, 0, 3), (2, 0, 1), (0, 2, 1)],
    [("-", 0, 0)],
    [("+", 0, 0)],
    [(0, "-", 0)],
    [(0, "+", 0)],
    [(0, 0, "-")],
    [(0, 0, "+")],
)


def power(value, order):
    if order == "+":
        return jnp.maximum(value, 0.0)
    if order == "-":
        return jnp.maximum(-value, 0.0)
    result = None
    for _ in range(order):
        result = value if result is None else result * value
    return result


def advance_kernel(face_ref, near_ref, _, mask_ref, sums_ref, back_ref, *refs):
    shared_refs, out_ref = refs[:-1], refs[-1]
    cells = near_ref.shape[1]
    cell_start = lax.axis_index("space") * cells
    sums = sums_ref[:SUMS]
    packed = [sums_ref[flux_start(face) : flux_start(face + 1)] for face in range(FACES)]
    flux = [flux_rows(sums, packed, face) for face in range(FACES)]
    gas = 0.0
    for face in range(FACES):
        hits = picks(near_ref, mask_ref, face, cell_start, cells).astype(BF16)
        gas += exact(flux[face], hits) - flux[face]
    for face, hits in enumerate(face_hits(face_ref, cells)):
        base = halo_rows(shared_refs, face, slice(0, SUMS))
        count = len(kept(face))
        own = halo_rows(shared_refs, face, slice(SUMS + NOTES, SUMS + NOTES + count))
        arrived = flux_rows(base, {face: own}, face)
        found = exact(arrived, hits.astype(BF16), ((1,), (1,)))
        gas += jnp.where(mask_ref[face : face + 1, :] != 1, found, 0.0)

    rows, returned = coefficients(sums, back_ref[...], TIME_STEP, 1.0)
    flows, cool, heats, gain, keep = rows[0:3], rows[3], rows[4:7], rows[7], rows[8]
    points = jnp.broadcast_to(point(lax.broadcasted_iota(jnp.int32, (NV, cells), 0)), (NV, cells))
    axes = []
    for flow in flows:
        off = points - flow
        bell = jnp.exp2(off * off * cool)
        axes.append([bell, bell * off, bell * off * off, bell * off * off * off])
    known = {}

    def along_axis(axis, order):
        if (axis, order) not in known:
            factor = power(points, order)
            known[axis, order] = [
                jnp.sum(term if factor is None else factor * term, axis=0, keepdims=True)
                for term in axes[axis]
            ]
        return known[axis, order]

    wall_bell = jnp.exp2(points * points * back_ref[6:7])
    above = jnp.maximum(points, 0.0)
    wall_sums = [jnp.sum(jnp.where(points > 0, wall_bell, 0.0), axis=0, keepdims=True)]
    for _ in range(4):
        wall_bell = wall_bell * above
        wall_sums.append(jnp.sum(wall_bell, axis=0, keepdims=True))

    def wall_full(order):
        if order in ("+", "-"):
            return wall_sums[1]
        return None if order % 2 else 2.0 * wall_sums[order]

    def wall_half(order, sign):
        if order in ("+", "-"):
            return wall_sums[2] if order == sign else None
        found = wall_sums[order + 1]
        return -found if order % 2 and sign == "-" else found

    found_rows = []
    for orders in ORDERS:
        bells, walls = 0.0, 0.0
        for order in orders:
            (x0, x1, x2, x3), (y0, y1, y2, y3), (z0, z1, z2, z3) = (
                along_axis(axis, order[axis]) for axis in range(3)
            )
            xy, xz, yz = x0 * y0, x0 * z0, y0 * z0
            skew = heats[0] * (x1 * (BEND * yz + cool * (y2 * z0 + y0 * z2)) + cool * x3 * yz)
            skew += heats[1] * (y1 * (BEND * xz + cool * (x2 * z0 + x0 * z2)) + cool * y3 * xz)
            skew += heats[2] * (z1 * (BEND * xy + cool * (x2 * y0 + x0 * y2)) + cool * z3 * xy)
            bells += xy * z0 + skew
            for face in range(FACES):
                terms = [
                    wall_half(order[axis], "+-"[face % 2])
                    if axis == face // 2
                    else wall_full(order[axis])
                    for axis in range(3)
                ]
                if all(term is not None for term in terms):
                    walls += returned[face : face + 1] * terms[0] * terms[1] * terms[2]
        found_rows.append(gain * bells + walls)
    found = WEIGHT * jnp.concatenate(found_rows, axis=0)
    out_ref[...] = found + keep * sums + TIME_STEP * gas


def halo_stream_kernel(face_ref, near_ref, *refs):
    base_ref, shape_ref, values_ref, open_ref = refs[-4:]
    refs = refs[:-4]
    shared_refs, halo_refs = refs[: len(refs) // 2], refs[len(refs) // 2 :]
    rows, width = base_ref.shape
    count = rows // 2
    planes, upward = planes_y(2 * width)
    cell_start = lax.axis_index("space") * rows
    notes = shared_rows(shared_refs, SUMS, SUMS + NOTES)
    passing = jnp.where(notes[:FACES] != 1.0, 1.0, 0.0)
    lane = lax.broadcasted_iota(jnp.int32, (1, rows), 1)
    picked = [
        jnp.where(lane < count, passing[0:1], passing[1:2]),
        jnp.where(upward, passing[2:3], passing[3:4]),
        passing[4:6],
        notes[7:8],
        jnp.zeros((LANES - 5, rows), F32),
    ]
    columns = jnp.concatenate(picked, axis=0).T
    open_x, open_y, open_low, open_high, cooling = (
        jnp.broadcast_to(columns[:, at : at + 1], (rows, LANES)) for at in range(5)
    )
    open_ref[...] = TIME_STEP * open_x
    low = face_hits(face_ref, rows)[0]
    low_flipped, low = low.T.astype(BF16), low.astype(BF16)
    row = lax.broadcasted_iota(jnp.int32, (rows, rows), 0)
    steps = []
    for face in range(2, FACES):
        hits = jnp.where(row == near_ref[face : face + 1, :] - cell_start, 1.0, 0.0)
        from_rows = dot(low_flipped, hits.T.astype(BF16)).astype(BF16)
        steps.append(dot(from_rows, low))
    along_y = jnp.where(upward, steps[0], steps[1])
    picks_all = jnp.concatenate([along_y, steps[2], steps[3]], axis=0).astype(BF16)
    picks_all = jnp.concatenate([picks_all, picks_all], axis=1)
    for side in range(2):
        block = slice(side * count, (side + 1) * count)
        values_ref[block, :] = halo_rows(halo_refs, side)

        def wide(column):
            return jnp.concatenate([column[block]] * (COLUMN_TILE // LANES), axis=1)

        for start in range(0, width, COLUMN_TILE):
            lanes = slice(start, start + COLUMN_TILE)
            vel_x, vel_z = lane_points((1 - side) * HALF + start % HALF, COLUMN_TILE)
            vel_y = planes[start // HALF]
            values = values_ref[block, lanes]
            moved = dot(picks_all, jnp.concatenate(split(values, 2), axis=0))
            speed_x, speed_y, speed_z = jnp.abs(vel_x), jnp.abs(vel_y), jnp.abs(vel_z)
            from_z = jnp.where(
                vel_z > 0,
                wide(open_low) * moved[count : 2 * count],
                wide(open_high) * moved[2 * count :],
            )
            base_ref[block, lanes] = TIME_STEP * (
                speed_y * (wide(open_y) * moved[:count])
                + speed_z * from_z
                - (speed_x + speed_y + speed_z) * values
            )
            speed_sq = vel_x * vel_x + vel_y * vel_y + vel_z * vel_z
            shape_ref[block, lanes] = jnp.exp2(speed_sq * wide(cooling))


def halo_relax_kernel(base_ref, shape_ref, values_ref, *refs):
    width = values_ref.shape[1]
    shared_refs, (out_ref, columns_ref) = refs[:-2], refs[-2:]
    sums = shared_rows(shared_refs, 0, SUMS)
    notes = shared_rows(shared_refs, SUMS, SUMS + NOTES)
    back = jnp.where(notes[:FACES] == 1.0, notes[6:7], 0.0)
    columns_ref[...] = columns_of(sums, back, 2 * width, TIME_STEP, 1.0)
    relax(columns_ref, base_ref, values_ref, shape_ref, out_ref, half=True)


def last_kernel(part, side_ref, part_ref, plane_ref, open_ref, *refs):
    refs, (out_ref, result_ref, sems) = refs[:-3], refs[-3:]
    halo_refs = refs[part > 0 :]
    cells, width = part_ref.shape
    count = cells // 2
    copies = []
    for side, tiles in enumerate(half_tiles(width, part, PARTS)):
        pick = side_ref[side * cells : (side + 1) * cells, :]
        block = slice((1 - side) * count, (2 - side) * count)
        gate = jnp.concatenate([open_ref[block]] * (COLUMN_TILE // LANES), axis=1)
        begin = tiles[0][1]
        for source, target in tiles:
            lanes = slice(source, source + COLUMN_TILE)
            speed_x = jnp.abs(lane_points(source, COLUMN_TILE)[0])
            rows = halo_rows(halo_refs, 1 - side)[:, target - begin : target - begin + COLUMN_TILE]
            rows = plane_ref[block, target : target + COLUMN_TILE] + gate * speed_x * rows
            halo = dot(pick, jnp.concatenate(split(rows, 2), axis=0))
            result_ref[:, lanes] = part_ref[:, lanes] + (0.5 * TIME_STEP * speed_x) * halo
            copy = pltpu.make_async_copy(
                result_ref.at[:, lanes], out_ref.at[:, lanes], sems.at[len(copies)]
            )
            copy.start()
            copies.append(copy)
    for copy in copies:
        copy.wait()


def call(kernel, outs, arrays, scratch=(), scalars=0, far_outs=False, unread=(), aliases=None):
    spaces = [
        pltpu.SMEM if at < scalars else pl.ANY if at in unread else pltpu.VMEM
        for at in range(len(arrays))
    ]
    if isinstance(kernel, functools.partial):
        name = f"{kernel.func.__name__}_{kernel.args[0]}"
    else:
        name = kernel.__name__
    size = sum(math.prod(array.shape) * 4 for array in arrays)
    return pl.pallas_call(
        kernel,
        out_shape=[jax.ShapeDtypeStruct(shape, dtype) for shape, dtype in outs],
        in_specs=[pl.BlockSpec(memory_space=space) for space in spaces],
        out_specs=[pl.BlockSpec(memory_space=pl.ANY if far_outs else pltpu.VMEM)] * len(outs),
        scratch_shapes=list(scratch),
        input_output_aliases=aliases or {},
        name=name,
        compiler_params=pltpu.CompilerParams(vmem_limit_bytes=40 * 2**20),
        cost_estimate=pl.CostEstimate(
            flops=COST.get(name, 0), bytes_accessed=size, transcendentals=0
        ),
    )(*arrays)


COST = {"advance_kernel": 13 * 10**8, "last_kernel_0": 4 * 10**9}


def total(value):
    count = lax.axis_size("vel")
    step = 1
    while step < count:
        value = value + lax.ppermute(value, "vel", [(i, i ^ step) for i in range(count)])
        step *= 2
    return value


def exchange(send):
    count = lax.axis_size("space")
    forward = [(i, (i + 1) % count) for i in range(count)]
    backward = [(target, source) for source, target in forward]
    if count == 2:
        return [lax.ppermute(send, "space", forward)]
    half = send.shape[0] // 2
    return [
        lax.ppermute(send[:half], "space", forward),
        lax.ppermute(send[half:], "space", backward),
    ]


def on_device(dist, wall_temp, neighbours, wall_mask, face_rows):
    cells, width = dist.shape
    count, half = cells // 2, width // 2
    temp = wall_temp[None, :]
    whole, plane = ((cells, width), F32), ((cells, half), F32)
    every = flux_start(FACES)
    columns = pltpu.VMEM((cells, LANES), F32)

    (sums,) = call(sums_kernel, [((every, cells), F32)], [dist])
    (sent,) = call(near_plane_kernel, [plane], [face_rows, dist, sums], scalars=1, unread=(2,))
    near = exchange(sent)
    sums = total(sums)
    shape, back, side, notes = call(
        wall_kernel,
        [whole, ((8, cells), F32), ((2 * cells, cells), BF16), ((NOTES, cells), F32)],
        [face_rows, temp, wall_mask],
    )
    (stream,) = call(stream_kernel, [whole], [neighbours, wall_mask, dist])
    (sent,) = call(
        share_kernel, [((2 * (2 * SUMS + NOTES), count), F32)], [face_rows, sums, notes]
    )
    shared = exchange(sent)
    far = []
    for part in range(PARTS):
        after = [sent] if part else []
        (far_rows,) = call(
            functools.partial(far_plane_kernel, part),
            [((cells, half // PARTS), F32)],
            [face_rows, dist, *after],
            scalars=1,
            unread=(2,),
        )
        far.append(exchange(far_rows))
    (middle,) = call(
        middle_kernel,
        [whole],
        [sums, back, side, dist, stream, shape, *near],
        [columns, pltpu.VMEM((cells, width), F32)],
    )
    (part_sum,) = call(stream_last_kernel, [whole], [neighbours, wall_mask, dist, middle])
    (sums_two,) = call(
        advance_kernel,
        [((SUMS, cells), F32)],
        [face_rows, neighbours, part_sum, wall_mask, sums, back, *shared],
        unread=(2,),
    )
    (part_sum,) = call(relax_kernel, [whole], [sums_two, back, middle, part_sum, shape], [columns])
    base, halo_shape, values, gate = call(
        halo_stream_kernel,
        [plane, plane, plane, ((cells, LANES), F32)],
        [face_rows, neighbours, *shared, *near],
    )
    (plane_one,) = call(
        halo_relax_kernel, [plane], [base, halo_shape, values, *shared], [columns]
    )
    result = []
    for part in range(PARTS):
        result = call(
            functools.partial(last_kernel, part),
            [whole],
            [side, part_sum, plane_one, gate, *result, *far[part]],
            [
                pltpu.VMEM((cells, width), F32),
                pltpu.SemaphoreType.DMA((width // COLUMN_TILE // PARTS,)),
            ],
            far_outs=True,
            unread=(4,) if part else (),
            aliases={4: 0} if part else None,
        )
    return result[0]


def solution(mesh):
    return jax.shard_map(
        on_device,
        mesh=mesh,
        in_specs=(
            P("space", "vel"),
            P("space"),
            P(None, "space"),
            P(None, "space"),
            P("space", None, None),
        ),
        out_specs=P("space", "vel"),
        check_vma=False,
    )
```

```python
import functools
import math

import jax
import jax.numpy as jnp
from jax import lax
from jax.experimental import pallas as pl
from jax.experimental.pallas import tpu as pltpu
from jax.sharding import PartitionSpec as P

NV = 32
LIMIT = 4.5
SPACING = 2.0 * LIMIT / NV
WEIGHT = SPACING**3 * (2.0 * math.pi) ** (-1.5)
TIME_STEP = 0.05
BASELINE_SHEAR = 0.1
SHEAR_EXPONENT = 0.66
MOMENTUM_RATIO = 2.0 / 3.0
PLANE = NV * NV
HALF = PLANE // 2
ROWS = 8
LANES = 128
COLUMN_TILE = 256
SUMS = 16
FACES = 6
NOTES = 8
PARTS = 2
BEND = 2.5 * math.log2(math.e)
LOG2E = math.log2(math.e)
F32 = jnp.float32
BF16 = jnp.bfloat16


def point(slot):
    return -LIMIT + (slot.astype(F32) + 0.5) * SPACING


def lane_points(start, width):
    lane = lax.broadcasted_iota(jnp.int32, (1, width), 1) + start
    return point((lane >> 5) & (NV - 1)), point(lane & (NV - 1))


def planes_y(width):
    planes = width // PLANE
    first = lax.axis_index("vel") * planes
    return [point(first + at) for at in range(planes)], first >= NV // 2


def split(value, count):
    pieces = []
    for _ in range(count - 1):
        piece = value.astype(BF16)
        pieces.append(piece)
        value = value - piece.astype(F32)
    pieces.append(value.astype(BF16))
    return pieces


def dot(left, right, dims=((1,), (0,))):
    return lax.dot_general(left, right, (dims, ((), ())), preferred_element_type=F32)


def kept(face):
    other = face ^ 1
    return [*range(1, 10)] + [
        10 + out for out in range(FACES) if out == other or out // 2 > other // 2
    ]


def flux_start(face):
    return SUMS + sum(len(kept(before)) for before in range(face))


def flux_rows(base, packed, face):
    other = face ^ 1
    mine = packed[face]
    rows = [base[10 + other : 11 + other], mine[:9]]
    for out in range(FACES):
        if out == face:
            rows.append(jnp.zeros_like(mine[:1]))
            continue
        holder, row = (face, 10 + out) if 10 + out in kept(face) else (out ^ 1, 10 + other)
        at = kept(holder).index(row)
        rows.append(packed[holder][at : at + 1])
    return jnp.concatenate(rows, axis=0)


def exact(left, right, dims=((1,), (0,))):
    rows = left.shape[0]
    found = dot(jnp.concatenate(split(left, 3), axis=0), right, dims)
    return found[:rows] + found[rows : 2 * rows] + found[2 * rows :]


def inward(vel_x, vel_y, vel_z):
    return [
        jnp.maximum(sign * vel, 0.0) for vel in (vel_x, vel_y, vel_z) for sign in (1.0, -1.0)
    ]


def weights(vel_x, vel_y, vel_z):
    speed_sq = vel_x * vel_x + vel_y * vel_y + vel_z * vel_z
    into = inward(vel_x, vel_y, vel_z)
    rows = [
        jnp.ones_like(vel_x),
        vel_x * vel_x,
        vel_y * vel_y,
        vel_z * vel_z,
        vel_x * vel_y,
        vel_x * vel_z,
        vel_y * vel_z,
        vel_x * speed_sq,
        vel_y * speed_sq,
        vel_z * speed_sq,
        into[1],
        into[0],
        into[3],
        into[2],
        into[5],
        into[4],
    ]
    return WEIGHT * jnp.concatenate(rows, axis=0), into


def face_hits(face_ref, cells):
    row = lax.broadcasted_iota(jnp.int32, (cells, face_ref.shape[2]), 0)
    return [jnp.where(row == face_ref[0, side : side + 1, :], 1.0, 0.0) for side in range(2)]


def sums_kernel(dist_ref, sums_ref):
    width = dist_ref.shape[1]
    planes, _ = planes_y(width)
    total = None
    for start in range(0, width, HALF):
        lanes = slice(start, start + HALF)
        vel_x, vel_z = lane_points(start, HALF)
        vel_y = jnp.full((1, HALF), planes[start // PLANE])
        base, into = weights(vel_x, vel_y, vel_z)
        table = [base]
        for face, speed in enumerate(into):
            fluxes = base * speed
            table.append(fluxes[1:10])
            table += [fluxes[row : row + 1] for row in kept(face)[9:]]
        table = jnp.concatenate(table, axis=0)
        coarse, fine = split(table, 2)
        finest = split(base, 3)[2]
        pieces = split(dist_ref[:, lanes], 3)
        across = ((1,), (1,))
        one = dot(jnp.concatenate([coarse, fine, finest], axis=0), pieces[0], across)
        two = dot(jnp.concatenate([coarse, fine], axis=0), pieces[1], across)
        three = dot(coarse, pieces[2], across)
        rows = table.shape[0]
        part = one[:rows] + one[rows : 2 * rows] + two[:rows] + two[rows:] + three
        part = jnp.concatenate([part[:SUMS] + one[2 * rows :], part[SUMS:]], axis=0)
        total = part if total is None else total + part
    sums_ref[...] = total


def share_kernel(face_ref, sums_ref, notes_ref, _, send_ref):
    low, high = face_hits(face_ref, sums_ref.shape[1])
    for side, hits in ((0, high), (1, low)):
        rows = [sums_ref[:SUMS], notes_ref[...], sums_ref[flux_start(side) : flux_start(side + 1)]]
        rows = exact(jnp.concatenate(rows, axis=0), hits.astype(BF16))
        first = side * (send_ref.shape[0] // 2)
        send_ref[first : first + rows.shape[0], :] = rows


def halo_rows(refs, side, rows=slice(None)):
    if len(refs) == 2:
        return refs[side][rows]
    half = refs[0].shape[0] // 2
    start, stop, _ = rows.indices(half)
    return refs[0][side * half + start : side * half + stop]


def shared_rows(refs, start, stop):
    rows = slice(start, stop)
    return jnp.concatenate([halo_rows(refs, 0, rows), halo_rows(refs, 1, rows)], axis=1)


def half_tiles(width, part=0, parts=1):
    half = width // 2
    lanes = range(part * half // parts, (part + 1) * half // parts, COLUMN_TILE)
    low = [(lane // HALF * PLANE + lane % HALF, lane) for lane in lanes]
    return low, [(source + HALF, target) for source, target in low]


def move_rows(rows_ref, value_ref, send_ref, crossed, part=0, parts=1):
    cells, width = value_ref.shape
    count = cells // 2
    low, high = half_tiles(width, part, parts)
    begin = low[0][1]
    piece = min(HALF, send_ref.shape[1])
    step = piece // COLUMN_TILE

    def move(at, _):
        for first, tiles, plane in ((0, high, 1 - crossed), (count, low, crossed)):
            row = rows_ref[0, plane, at]
            for source, target in tiles[::step]:
                send_ref[pl.ds(first + at, 1), target - begin : target - begin + piece] = (
                    value_ref[pl.ds(row, 1), source : source + piece]
                )
        return 0

    lax.fori_loop(0, count, move, 0, unroll=True)


def wall_rows(temp_ref):
    cooling = (-0.5 * LOG2E) / temp_ref[...]
    axis_point = point(lax.broadcasted_iota(jnp.int32, (NV, 1), 0))
    profile = jnp.exp2(axis_point * axis_point * cooling)
    mass = jnp.sum(profile, axis=0, keepdims=True)
    flux = jnp.sum(jnp.maximum(axis_point, 0.0) * profile, axis=0, keepdims=True)
    return 1.0 / (WEIGHT * flux * mass * mass), cooling


def near_plane_kernel(rows_ref, dist_ref, send_ref):
    move_rows(rows_ref, dist_ref, send_ref, 0)


def far_plane_kernel(rows_ref, dist_ref, *send_refs):
    for part, send_ref in enumerate(send_refs):
        move_rows(rows_ref, dist_ref, send_ref, 1, part, PARTS)


def pass_kernel(value_ref, after_ref, out_ref):
    pass


def picks(near_ref, mask_ref, face, cell_start, cells):
    index = near_ref[face : face + 1, :] - cell_start
    hit = lax.broadcasted_iota(jnp.int32, (cells, cells), 0) == index
    open_face = mask_ref[face : face + 1, :] != 1
    return jnp.where(hit & open_face, 1.0, 0.0).astype(F32)


def along(near_ref, mask_ref, upward):
    cells = near_ref.shape[1]
    cell_start = lax.axis_index("space") * cells
    faces = [picks(near_ref, mask_ref, face, cell_start, cells) for face in range(6)]
    return [faces[0], faces[1], jnp.where(upward, faces[2], faces[3]), faces[4], faces[5]]


def stream_tiles(near_ref, mask_ref, value_ref, store):
    cells, width = value_ref.shape
    planes, upward = planes_y(width)
    chosen = []
    for face in along(near_ref, mask_ref, upward):
        flipped = face.T.astype(BF16)
        chosen.append(jnp.concatenate([flipped, flipped], axis=1))
    rest = jnp.concatenate(chosen[2:], axis=0)
    for start in range(0, width, COLUMN_TILE):
        side = chosen[0] if start % PLANE >= HALF else chosen[1]
        vel_x, vel_z = lane_points(start, COLUMN_TILE)
        values = value_ref[:, start : start + COLUMN_TILE]
        pieces = jnp.concatenate(split(values, 2), axis=0)
        moved = dot(jnp.concatenate([side, rest], axis=0), pieces)
        speed_x, speed_z = jnp.abs(vel_x), jnp.abs(vel_z)
        speed_y = jnp.abs(planes[start // PLANE])
        from_z = jnp.where(vel_z > 0, moved[2 * cells : 3 * cells], moved[3 * cells :])
        stream = (
            speed_x * moved[:cells]
            + speed_y * moved[cells : 2 * cells]
            + speed_z * from_z
            - (speed_x + speed_y + speed_z) * values
        )
        store(slice(start, start + COLUMN_TILE), values, stream)


def stream_kernel(near_ref, mask_ref, value_ref, out_ref):
    def store(lanes, values, stream):
        out_ref[:, lanes] = TIME_STEP * stream

    stream_tiles(near_ref, mask_ref, value_ref, store)


def stream_last_kernel(near_ref, mask_ref, dist_ref, middle_ref, out_ref):
    def store(lanes, values, stream):
        out_ref[:, lanes] = 0.5 * (dist_ref[:, lanes] + values) + (0.5 * TIME_STEP) * stream

    stream_tiles(near_ref, mask_ref, middle_ref, store)


def wall_kernel(face_ref, temp_ref, mask_ref, shape_ref, back_ref, side_ref, notes_ref):
    cells, width = shape_ref.shape
    count = cells // 2
    planes, _ = planes_y(width)
    inv_norm, cooling = wall_rows(temp_ref)
    mask = mask_ref[...]
    notes_ref[...] = jnp.concatenate([mask.astype(F32), inv_norm, cooling], axis=0)
    back_ref[...] = jnp.concatenate(
        [jnp.where(mask == 1, inv_norm, 0.0), cooling, jnp.zeros((1, cells), F32)],
        axis=0,
    )
    rows = [mask[:2].astype(F32), cooling, jnp.zeros((LANES - 3, cells), F32)]
    columns = jnp.concatenate(rows, axis=0).T
    row = lax.broadcasted_iota(jnp.int32, (cells, count), 0)
    for side, face in enumerate((1, 0)):
        hit = (row == face_ref[0, face : face + 1, :]) & (columns[:, face : face + 1] != 1.0)
        picked = jnp.where(hit, 1.0, 0.0).astype(BF16)
        side_ref[side * cells : (side + 1) * cells, :] = jnp.concatenate([picked, picked], axis=1)
    cooling = jnp.broadcast_to(columns[:, 2:3], (cells, LANES))
    for start in range(0, PLANE, LANES):
        vel_x, vel_z = lane_points(start, LANES)
        flat = vel_x * vel_x + vel_z * vel_z
        for at, vel_y in enumerate(planes):
            lanes = slice(at * PLANE + start, at * PLANE + start + LANES)
            shape_ref[:, lanes] = jnp.exp2((flat + vel_y * vel_y) * cooling)


def coefficients(sums, back, step, keep):
    count = sums[0:1]
    inv_count = 1.0 / count
    flow_x = (sums[11:12] - sums[10:11]) * inv_count
    flow_y = (sums[13:14] - sums[12:13]) * inv_count
    flow_z = (sums[15:16] - sums[14:15]) * inv_count
    p_xx, p_yy, p_zz, p_xy, p_xz, p_yz = (sums[at : at + 1] for at in range(1, 7))
    energy = p_xx + p_yy + p_zz
    flow_sq = flow_x * flow_x + flow_y * flow_y + flow_z * flow_z
    temp = (energy * inv_count - flow_sq) / 3.0
    inv_temp = 1.0 / temp

    def heat(third, flow, press):
        return 0.5 * (
            third
            - 2.0 * (press[0] * flow_x + press[1] * flow_y + press[2] * flow_z)
            - flow * energy
            + 2.0 * count * flow * flow_sq
        )

    scale = ((1.0 - MOMENTUM_RATIO) / 5.0) * inv_count * inv_temp * inv_temp * (-2.0 / LOG2E)
    rate = (count * jnp.exp((1.0 - SHEAR_EXPONENT) * jnp.log(temp))) * (step / BASELINE_SHEAR)
    returned = (back[0:6] * step) * sums[10:16]
    rows = [
        flow_x,
        flow_y,
        flow_z,
        (-0.5 * LOG2E) * inv_temp,
        scale * heat(sums[7:8], flow_x, (p_xx, p_xy, p_xz)),
        scale * heat(sums[8:9], flow_y, (p_xy, p_yy, p_yz)),
        scale * heat(sums[9:10], flow_z, (p_xz, p_yz, p_zz)),
        count * inv_temp * lax.rsqrt(temp) * rate,
        keep - rate,
    ]
    return rows, returned


def columns_of(sums, back, width, step, keep, more=()):
    _, upward = planes_y(width)
    rows, returned = coefficients(sums, back, step, keep)
    rows += [
        jnp.where(upward, returned[2:3], returned[3:4]),
        returned[0:2],
        returned[4:6],
        *more,
        jnp.zeros((LANES - 14 - sum(row.shape[0] for row in more), sums.shape[1]), F32),
    ]
    return jnp.concatenate(rows, axis=0).T


def relax(columns_ref, base_ref, value_ref, shape_ref, out_ref, planes_refs=None):
    cells, width = value_ref.shape
    half = planes_refs is not None
    planes, _ = planes_y(2 * width if half else width)
    lane = lax.broadcasted_iota(jnp.int32, (ROWS, LANES), 1)
    first_x, vel_z = point((lane >> 5) & (NV - 1)), point(lane & (NV - 1))
    z_plus, z_minus = jnp.maximum(vel_z, 0.0), jnp.maximum(-vel_z, 0.0)

    def group(at, _, tiles=range(PLANE // LANES), stride=PLANE):
        rows = pl.ds(pl.multiple_of(at * ROWS, ROWS), ROWS)
        columns = columns_ref[rows, :]
        flow_x, flow_y, flow_z, cool, heat_x, heat_y, heat_z, gain, keep, back_y, *back = (
            jnp.broadcast_to(columns[:, column : column + 1], (ROWS, LANES))
            for column in range(18 if half else 14)
        )
        if half:
            open_y, open_low, open_high, cooling = back[4:]
            open_z = jnp.where(vel_z > 0, open_low, open_high)
        rel_z = vel_z - flow_z
        square_z = rel_z * rel_z * cool
        heat_of_z = rel_z * heat_z
        back_z = z_plus * back[2] + z_minus * back[3]
        of_y = []
        for vel_y in planes:
            rel_y = vel_y - flow_y
            of_y.append((rel_y * rel_y * cool, rel_y * heat_y, jnp.abs(vel_y) * back_y))
        for tile in tiles:
            vel_x = first_x + (tile * (LANES // NV)) * SPACING
            rel_x = vel_x - flow_x
            square_xz = rel_x * rel_x * cool + square_z
            heat_xz = rel_x * heat_x + heat_of_z
            upper = tile * LANES >= HALF
            back_xz = jnp.abs(vel_x) * (back[0] if upper else back[1]) + back_z
            for plane, (square_y, heat_of_y, back_of_y) in enumerate(of_y):
                start = plane * stride + (tile - tiles[0]) * LANES
                lanes = slice(start, start + LANES)
                square = square_xz + square_y
                skew = (heat_xz + heat_of_y) * (square + 2.5 * LOG2E) + 1.0
                base = base_ref[rows, lanes]
                if half:
                    from_y_ref, from_z_ref = planes_refs
                    base += open_y * from_y_ref[rows, lanes] + open_z * from_z_ref[rows, lanes]
                    speed_sq = vel_x * vel_x + vel_z * vel_z + planes[plane] * planes[plane]
                    shape = jnp.exp2(speed_sq * cooling)
                else:
                    shape = shape_ref[rows, lanes]
                out_ref[rows, lanes] = (
                    base
                    + keep * value_ref[rows, lanes]
                    + gain * jnp.exp2(square) * skew
                    + shape * (back_xz + back_of_y)
                )
        return 0

    groups = cells // ROWS
    if half:
        low, high = range(HALF // LANES), range(HALF // LANES, PLANE // LANES)
        lax.fori_loop(
            0, groups // 2, functools.partial(group, tiles=high, stride=HALF), 0, unroll=True
        )
        lax.fori_loop(
            groups // 2, groups, functools.partial(group, tiles=low, stride=HALF), 0, unroll=True
        )
    else:
        lax.fori_loop(0, groups, group, 0, unroll=True)


def middle_kernel(sums_ref, back_ref, side_ref, own_ref, stream_ref, shape_ref, *refs):
    halo_refs, (out_ref, columns_ref, base_ref) = refs[:-3], refs[-3:]
    cells, width = own_ref.shape
    columns_ref[...] = columns_of(sums_ref[:SUMS], back_ref[...], width, TIME_STEP, 1.0)
    for side, tiles in enumerate(half_tiles(width)):
        pick = side_ref[side * cells : (side + 1) * cells, :]
        for source, target in tiles:
            lanes = slice(source, source + COLUMN_TILE)
            vel_x, _ = lane_points(source, COLUMN_TILE)
            rows = halo_rows(halo_refs, 1 - side)[:, target : target + COLUMN_TILE]
            halo = dot(pick, jnp.concatenate(split(rows, 2), axis=0))
            base_ref[:, lanes] = stream_ref[:, lanes] + (TIME_STEP * jnp.abs(vel_x)) * halo
    relax(columns_ref, base_ref, own_ref, shape_ref, out_ref)


def relax_kernel(sums_ref, back_ref, middle_ref, part_ref, shape_ref, out_ref, columns_ref):
    width = middle_ref.shape[1]
    step = 0.5 * TIME_STEP
    columns_ref[...] = columns_of(sums_ref[...], back_ref[...], width, step, 0.0)
    relax(columns_ref, part_ref, middle_ref, shape_ref, out_ref)


ORDERS = (
    [(0, 0, 0)],
    [(2, 0, 0)],
    [(0, 2, 0)],
    [(0, 0, 2)],
    [(1, 1, 0)],
    [(1, 0, 1)],
    [(0, 1, 1)],
    [(3, 0, 0), (1, 2, 0), (1, 0, 2)],
    [(0, 3, 0), (2, 1, 0), (0, 1, 2)],
    [(0, 0, 3), (2, 0, 1), (0, 2, 1)],
    [("-", 0, 0)],
    [("+", 0, 0)],
    [(0, "-", 0)],
    [(0, "+", 0)],
    [(0, 0, "-")],
    [(0, 0, "+")],
)


def power(value, order):
    if order == "+":
        return jnp.maximum(value, 0.0)
    if order == "-":
        return jnp.maximum(-value, 0.0)
    result = None
    for _ in range(order):
        result = value if result is None else result * value
    return result


def advance_kernel(face_ref, near_ref, _, __, mask_ref, sums_ref, back_ref, *refs):
    shared_refs, out_ref = refs[:-1], refs[-1]
    cells = near_ref.shape[1]
    cell_start = lax.axis_index("space") * cells
    sums = sums_ref[:SUMS]
    packed = [sums_ref[flux_start(face) : flux_start(face + 1)] for face in range(FACES)]
    flux = [flux_rows(sums, packed, face) for face in range(FACES)]
    gas = 0.0
    for face in range(FACES):
        hits = picks(near_ref, mask_ref, face, cell_start, cells).astype(BF16)
        gas += exact(flux[face], hits) - flux[face]
    for face, hits in enumerate(face_hits(face_ref, cells)):
        base = halo_rows(shared_refs, face, slice(0, SUMS))
        count = len(kept(face))
        own = halo_rows(shared_refs, face, slice(SUMS + NOTES, SUMS + NOTES + count))
        arrived = flux_rows(base, {face: own}, face)
        found = exact(arrived, hits.astype(BF16), ((1,), (1,)))
        gas += jnp.where(mask_ref[face : face + 1, :] != 1, found, 0.0)

    rows, returned = coefficients(sums, back_ref[...], TIME_STEP, 1.0)
    flows, cool, heats, gain, keep = rows[0:3], rows[3], rows[4:7], rows[7], rows[8]
    points = jnp.broadcast_to(point(lax.broadcasted_iota(jnp.int32, (NV, cells), 0)), (NV, cells))
    axes = []
    for flow in flows:
        off = points - flow
        bell = jnp.exp2(off * off * cool)
        axes.append([bell, bell * off, bell * off * off, bell * off * off * off])
    known = {}

    def along_axis(axis, order):
        if (axis, order) not in known:
            factor = power(points, order)
            known[axis, order] = [
                jnp.sum(term if factor is None else factor * term, axis=0, keepdims=True)
                for term in axes[axis]
            ]
        return known[axis, order]

    wall_bell = jnp.exp2(points * points * back_ref[6:7])
    above = jnp.maximum(points, 0.0)
    wall_sums = [jnp.sum(jnp.where(points > 0, wall_bell, 0.0), axis=0, keepdims=True)]
    for _ in range(4):
        wall_bell = wall_bell * above
        wall_sums.append(jnp.sum(wall_bell, axis=0, keepdims=True))

    def wall_full(order):
        if order in ("+", "-"):
            return wall_sums[1]
        return None if order % 2 else 2.0 * wall_sums[order]

    def wall_half(order, sign):
        if order in ("+", "-"):
            return wall_sums[2] if order == sign else None
        found = wall_sums[order + 1]
        return -found if order % 2 and sign == "-" else found

    found_rows = []
    for orders in ORDERS:
        bells, walls = 0.0, 0.0
        for order in orders:
            (x0, x1, x2, x3), (y0, y1, y2, y3), (z0, z1, z2, z3) = (
                along_axis(axis, order[axis]) for axis in range(3)
            )
            xy, xz, yz = x0 * y0, x0 * z0, y0 * z0
            skew = heats[0] * (x1 * (BEND * yz + cool * (y2 * z0 + y0 * z2)) + cool * x3 * yz)
            skew += heats[1] * (y1 * (BEND * xz + cool * (x2 * z0 + x0 * z2)) + cool * y3 * xz)
            skew += heats[2] * (z1 * (BEND * xy + cool * (x2 * y0 + x0 * y2)) + cool * z3 * xy)
            bells += xy * z0 + skew
            for face in range(FACES):
                terms = [
                    wall_half(order[axis], "+-"[face % 2])
                    if axis == face // 2
                    else wall_full(order[axis])
                    for axis in range(3)
                ]
                if all(term is not None for term in terms):
                    walls += returned[face : face + 1] * terms[0] * terms[1] * terms[2]
        found_rows.append(gain * bells + walls)
    found = WEIGHT * jnp.concatenate(found_rows, axis=0)
    out_ref[...] = found + keep * sums + TIME_STEP * gas


def halo_stream_kernel(face_ref, near_ref, *refs):
    halo_refs, (base_ref, from_y_ref, from_z_ref, values_ref) = refs[:-4], refs[-4:]
    rows, width = base_ref.shape
    count = rows // 2
    planes, upward = planes_y(2 * width)
    cell_start = lax.axis_index("space") * rows
    low = face_hits(face_ref, rows)[0]
    low_flipped, low = low.T.astype(BF16), low.astype(BF16)
    row = lax.broadcasted_iota(jnp.int32, (rows, rows), 0)
    steps = []
    for face in range(2, FACES):
        hits = jnp.where(row == near_ref[face : face + 1, :] - cell_start, 1.0, 0.0)
        from_rows = dot(low_flipped, hits.T.astype(BF16)).astype(BF16)
        steps.append(dot(from_rows, low))
    along_y = jnp.where(upward, steps[0], steps[1])
    picks_all = jnp.concatenate([along_y, steps[2], steps[3]], axis=0).astype(BF16)
    picks_all = jnp.concatenate([picks_all, picks_all], axis=1)
    for side in range(2):
        block = slice(side * count, (side + 1) * count)
        values_ref[block, :] = halo_rows(halo_refs, side)
        for start in range(0, width, COLUMN_TILE):
            lanes = slice(start, start + COLUMN_TILE)
            vel_x, vel_z = lane_points((1 - side) * HALF + start % HALF, COLUMN_TILE)
            vel_y = planes[start // HALF]
            values = values_ref[block, lanes]
            moved = dot(picks_all, jnp.concatenate(split(values, 2), axis=0))
            speed_x, speed_y, speed_z = jnp.abs(vel_x), jnp.abs(vel_y), jnp.abs(vel_z)
            from_z = jnp.where(vel_z > 0, moved[count : 2 * count], moved[2 * count :])
            from_y_ref[block, lanes] = (TIME_STEP * speed_y) * moved[:count]
            from_z_ref[block, lanes] = (TIME_STEP * speed_z) * from_z
            base_ref[block, lanes] = -TIME_STEP * (speed_x + speed_y + speed_z) * values


def halo_relax_kernel(base_ref, from_y_ref, from_z_ref, values_ref, *refs):
    shared_refs, (out_ref, open_ref, columns_ref) = refs[:-3], refs[-3:]
    rows, width = values_ref.shape
    _, upward = planes_y(2 * width)
    sums = shared_rows(shared_refs, 0, SUMS)
    notes = shared_rows(shared_refs, SUMS, SUMS + NOTES)
    back = jnp.where(notes[:FACES] == 1.0, notes[6:7], 0.0)
    passing = jnp.where(notes[:FACES] != 1.0, 1.0, 0.0)
    lane = lax.broadcasted_iota(jnp.int32, (1, rows), 1)
    more = [
        jnp.where(upward, passing[2:3], passing[3:4]),
        passing[4:6],
        notes[7:8],
        TIME_STEP * jnp.where(lane < rows // 2, passing[0:1], passing[1:2]),
    ]
    columns = columns_of(sums, back, 2 * width, TIME_STEP, 1.0, more)
    columns_ref[...] = columns
    open_ref[...] = jnp.broadcast_to(columns[:, 18:19], (rows, LANES))
    relax(columns_ref, base_ref, values_ref, None, out_ref, (from_y_ref, from_z_ref))


def last_kernel(part, side_ref, part_ref, plane_ref, open_ref, *refs):
    refs, (out_ref, result_ref, sems) = refs[:-3], refs[-3:]
    halo_refs = refs[part > 0 :]
    cells, width = part_ref.shape
    count = cells // 2
    copies = []
    for side, tiles in enumerate(half_tiles(width, part, PARTS)):
        pick = side_ref[side * cells : (side + 1) * cells, :]
        block = slice((1 - side) * count, (2 - side) * count)
        gate = jnp.concatenate([open_ref[block]] * (COLUMN_TILE // LANES), axis=1)
        begin = tiles[0][1]
        for source, target in tiles:
            lanes = slice(source, source + COLUMN_TILE)
            speed_x = jnp.abs(lane_points(source, COLUMN_TILE)[0])
            rows = halo_rows(halo_refs, 1 - side)[:, target - begin : target - begin + COLUMN_TILE]
            rows = plane_ref[block, target : target + COLUMN_TILE] + gate * speed_x * rows
            halo = dot(pick, jnp.concatenate(split(rows, 2), axis=0))
            result_ref[:, lanes] = part_ref[:, lanes] + (0.5 * TIME_STEP * speed_x) * halo
            copy = pltpu.make_async_copy(
                result_ref.at[:, lanes], out_ref.at[:, lanes], sems.at[len(copies)]
            )
            copy.start()
            copies.append(copy)
    for copy in copies:
        copy.wait()


def call(kernel, outs, arrays, scratch=(), scalars=0, far_outs=False, unread=(), aliases=None):
    spaces = [
        pltpu.SMEM if at < scalars else pl.ANY if at in unread else pltpu.VMEM
        for at in range(len(arrays))
    ]
    if isinstance(kernel, functools.partial):
        name = f"{kernel.func.__name__}_{kernel.args[0]}"
    else:
        name = kernel.__name__
    size = sum(math.prod(array.shape) * 4 for array in arrays)
    return pl.pallas_call(
        kernel,
        out_shape=[jax.ShapeDtypeStruct(shape, dtype) for shape, dtype in outs],
        in_specs=[pl.BlockSpec(memory_space=space) for space in spaces],
        out_specs=[pl.BlockSpec(memory_space=pl.ANY if far_outs else pltpu.VMEM)] * len(outs),
        scratch_shapes=list(scratch),
        input_output_aliases=aliases or {},
        name=name,
        compiler_params=pltpu.CompilerParams(vmem_limit_bytes=40 * 2**20),
        cost_estimate=pl.CostEstimate(
            flops=COST.get(name, 0), bytes_accessed=size, transcendentals=0
        ),
    )(*arrays)


COST = {"advance_kernel": 14 * 10**8, "last_kernel_0": 4 * 10**9}


def total(value):
    count = lax.axis_size("vel")
    step = 1
    while step < count:
        value = value + lax.ppermute(value, "vel", [(i, i ^ step) for i in range(count)])
        step *= 2
    return value


def exchange(send):
    count = lax.axis_size("space")
    forward = [(i, (i + 1) % count) for i in range(count)]
    backward = [(target, source) for source, target in forward]
    if count == 2:
        return [lax.ppermute(send, "space", forward)]
    half = send.shape[0] // 2
    return [
        lax.ppermute(send[:half], "space", forward),
        lax.ppermute(send[half:], "space", backward),
    ]


def on_device(dist, wall_temp, neighbours, wall_mask, face_rows):
    cells, width = dist.shape
    count, half = cells // 2, width // 2
    temp = wall_temp[None, :]
    whole, plane = ((cells, width), F32), ((cells, half), F32)
    every = flux_start(FACES)
    columns = pltpu.VMEM((cells, LANES), F32)

    face_rows = jnp.clip(face_rows, 0, cells - 1)
    (sent,) = call(near_plane_kernel, [plane], [face_rows, dist], scalars=1)
    near = exchange(sent)
    (sums,) = call(sums_kernel, [((every, cells), F32)], [dist])
    sums = total(sums)
    shape, back, side, notes = call(
        wall_kernel,
        [whole, ((8, cells), F32), ((2 * cells, cells), BF16), ((NOTES, cells), F32)],
        [face_rows, temp, wall_mask],
    )
    (stream,) = call(stream_kernel, [whole], [neighbours, wall_mask, dist])
    (sent,) = call(
        share_kernel,
        [((2 * (2 * SUMS + NOTES), count), F32)],
        [face_rows, sums, notes, stream],
        unread=(3,),
    )
    shared = exchange(sent)
    part_shape = ((cells, half // PARTS), F32)
    far_rows = call(far_plane_kernel, [part_shape] * PARTS, [face_rows, dist], scalars=1)
    far = []
    for part in range(PARTS):
        rows = far_rows[part]
        if part:
            (rows,) = call(
                pass_kernel,
                [part_shape],
                [rows, sent],
                far_outs=True,
                unread=(0, 1),
                aliases={0: 0},
            )
        far.append(exchange(rows))
    (middle,) = call(
        middle_kernel,
        [whole],
        [sums, back, side, dist, stream, shape, *near],
        [columns, pltpu.VMEM((cells, width), F32)],
    )
    (part_sum,) = call(stream_last_kernel, [whole], [neighbours, wall_mask, dist, middle])
    halo_parts = call(halo_stream_kernel, [plane] * 4, [face_rows, neighbours, *near])
    (sums_two,) = call(
        advance_kernel,
        [((SUMS, cells), F32)],
        [face_rows, neighbours, part_sum, halo_parts[0], wall_mask, sums, back, *shared],
        unread=(2, 3),
    )
    (part_sum,) = call(relax_kernel, [whole], [sums_two, back, middle, part_sum, shape], [columns])
    plane_one, gate = call(
        halo_relax_kernel, [plane, ((cells, LANES), F32)], [*halo_parts, *shared], [columns]
    )
    result = []
    for part in range(PARTS):
        result = call(
            functools.partial(last_kernel, part),
            [whole],
            [side, part_sum, plane_one, gate, *result, *far[part]],
            [
                pltpu.VMEM((cells, width), F32),
                pltpu.SemaphoreType.DMA((width // COLUMN_TILE // PARTS,)),
            ],
            far_outs=True,
            unread=(4,) if part else (),
            aliases={4: 0} if part else None,
        )
    return result[0]


def solution(mesh):
    return jax.shard_map(
        on_device,
        mesh=mesh,
        in_specs=(
            P("space", "vel"),
            P("space"),
            P(None, "space"),
            P(None, "space"),
            P("space", None, None),
        ),
        out_specs=P("space", "vel"),
        check_vma=False,
    )
```

```python
import functools
import math

import jax
import jax.numpy as jnp
from jax import lax
from jax.experimental import pallas as pl
from jax.experimental.pallas import tpu as pltpu
from jax.sharding import PartitionSpec as P

NV = 32
LIMIT = 4.5
SPACING = 2.0 * LIMIT / NV
WEIGHT = SPACING**3 * (2.0 * math.pi) ** (-1.5)
TIME_STEP = 0.05
BASELINE_SHEAR = 0.1
SHEAR_EXPONENT = 0.66
MOMENTUM_RATIO = 2.0 / 3.0
PLANE = NV * NV
HALF = PLANE // 2
ROWS = 8
LANES = 128
COLUMN_TILE = 256
SUMS = 16
FACES = 6
NOTES = 8
PARTS = 2
BEND = 2.5 * math.log2(math.e)
LOG2E = math.log2(math.e)
F32 = jnp.float32
BF16 = jnp.bfloat16


def point(slot):
    return -LIMIT + (slot.astype(F32) + 0.5) * SPACING


def lane_points(start, width):
    lane = lax.broadcasted_iota(jnp.int32, (1, width), 1) + start
    return point((lane >> 5) & (NV - 1)), point(lane & (NV - 1))


def planes_y(width):
    planes = width // PLANE
    first = lax.axis_index("vel") * planes
    return [point(first + at) for at in range(planes)], first >= NV // 2


def split(value, count):
    pieces = []
    for _ in range(count - 1):
        piece = value.astype(BF16)
        pieces.append(piece)
        value = value - piece.astype(F32)
    pieces.append(value.astype(BF16))
    return pieces


def dot(left, right, dims=((1,), (0,))):
    return lax.dot_general(left, right, (dims, ((), ())), preferred_element_type=F32)


def kept(face):
    other = face ^ 1
    return [*range(1, 10)] + [
        10 + out for out in range(FACES) if out == other or out // 2 > other // 2
    ]


def flux_start(face):
    return SUMS + sum(len(kept(before)) for before in range(face))


def flux_rows(base, packed, face):
    other = face ^ 1
    mine = packed[face]
    rows = [base[10 + other : 11 + other], mine[:9]]
    for out in range(FACES):
        if out == face:
            rows.append(jnp.zeros_like(mine[:1]))
            continue
        holder, row = (face, 10 + out) if 10 + out in kept(face) else (out ^ 1, 10 + other)
        at = kept(holder).index(row)
        rows.append(packed[holder][at : at + 1])
    return jnp.concatenate(rows, axis=0)


def exact(left, right, dims=((1,), (0,))):
    rows = left.shape[0]
    found = dot(jnp.concatenate(split(left, 3), axis=0), right, dims)
    return found[:rows] + found[rows : 2 * rows] + found[2 * rows :]


def inward(vel_x, vel_y, vel_z):
    return [
        jnp.maximum(sign * vel, 0.0) for vel in (vel_x, vel_y, vel_z) for sign in (1.0, -1.0)
    ]


def weights(vel_x, vel_y, vel_z):
    speed_sq = vel_x * vel_x + vel_y * vel_y + vel_z * vel_z
    into = inward(vel_x, vel_y, vel_z)
    rows = [
        jnp.ones_like(vel_x),
        vel_x * vel_x,
        vel_y * vel_y,
        vel_z * vel_z,
        vel_x * vel_y,
        vel_x * vel_z,
        vel_y * vel_z,
        vel_x * speed_sq,
        vel_y * speed_sq,
        vel_z * speed_sq,
        into[1],
        into[0],
        into[3],
        into[2],
        into[5],
        into[4],
    ]
    return WEIGHT * jnp.concatenate(rows, axis=0), into


def face_hits(face_ref, cells):
    row = lax.broadcasted_iota(jnp.int32, (cells, face_ref.shape[2]), 0)
    return [jnp.where(row == face_ref[0, side : side + 1, :], 1.0, 0.0) for side in range(2)]


def sums_kernel(dist_ref, sums_ref):
    width = dist_ref.shape[1]
    planes, _ = planes_y(width)
    total = None
    for start in range(0, width, HALF):
        lanes = slice(start, start + HALF)
        vel_x, vel_z = lane_points(start, HALF)
        vel_y = jnp.full((1, HALF), planes[start // PLANE])
        base, into = weights(vel_x, vel_y, vel_z)
        table = [base]
        for face, speed in enumerate(into):
            fluxes = base * speed
            table.append(fluxes[1:10])
            table += [fluxes[row : row + 1] for row in kept(face)[9:]]
        table = jnp.concatenate(table, axis=0)
        coarse, fine = split(table, 2)
        finest = split(base, 3)[2]
        pieces = split(dist_ref[:, lanes], 3)
        across = ((1,), (1,))
        one = dot(jnp.concatenate([coarse, fine, finest], axis=0), pieces[0], across)
        two = dot(jnp.concatenate([coarse, fine], axis=0), pieces[1], across)
        three = dot(coarse, pieces[2], across)
        rows = table.shape[0]
        part = one[:rows] + one[rows : 2 * rows] + two[:rows] + two[rows:] + three
        part = jnp.concatenate([part[:SUMS] + one[2 * rows :], part[SUMS:]], axis=0)
        total = part if total is None else total + part
    sums_ref[...] = total


def share_kernel(face_ref, sums_ref, notes_ref, _, send_ref):
    low, high = face_hits(face_ref, sums_ref.shape[1])
    for side, hits in ((0, high), (1, low)):
        rows = [sums_ref[:SUMS], notes_ref[...], sums_ref[flux_start(side) : flux_start(side + 1)]]
        rows = exact(jnp.concatenate(rows, axis=0), hits.astype(BF16))
        first = side * (send_ref.shape[0] // 2)
        send_ref[first : first + rows.shape[0], :] = rows


def halo_rows(refs, side, rows=slice(None)):
    if len(refs) == 2:
        return refs[side][rows]
    half = refs[0].shape[0] // 2
    start, stop, _ = rows.indices(half)
    return refs[0][side * half + start : side * half + stop]


def shared_rows(refs, start, stop):
    rows = slice(start, stop)
    return jnp.concatenate([halo_rows(refs, 0, rows), halo_rows(refs, 1, rows)], axis=1)


def half_tiles(width, part=0, parts=1):
    half = width // 2
    lanes = range(part * half // parts, (part + 1) * half // parts, COLUMN_TILE)
    low = [(lane // HALF * PLANE + lane % HALF, lane) for lane in lanes]
    return low, [(source + HALF, target) for source, target in low]


def move_rows(rows_ref, value_ref, send_ref, part):
    cells, width = value_ref.shape
    count = cells // 2
    low, high = half_tiles(width, part, PARTS)
    begin = low[0][1]
    piece = min(HALF, send_ref.shape[1])
    step = piece // COLUMN_TILE

    def move(at, _):
        for first, tiles, plane in ((0, high, 0), (count, low, 1)):
            row = rows_ref[0, plane, at]
            for source, target in tiles[::step]:
                send_ref[pl.ds(first + at, 1), target - begin : target - begin + piece] = (
                    value_ref[pl.ds(row, 1), source : source + piece]
                )
        return 0

    lax.fori_loop(0, count, move, 0, unroll=True)


def wall_rows(temp_ref):
    cooling = (-0.5 * LOG2E) / temp_ref[...]
    axis_point = point(lax.broadcasted_iota(jnp.int32, (NV, 1), 0))
    profile = jnp.exp2(axis_point * axis_point * cooling)
    mass = jnp.sum(profile, axis=0, keepdims=True)
    flux = jnp.sum(jnp.maximum(axis_point, 0.0) * profile, axis=0, keepdims=True)
    return 1.0 / (WEIGHT * flux * mass * mass), cooling


def near_plane_kernel(face_ref, dist_ref, own_ref, send_ref, rows_ref, row_sem, sems):
    cells, width = dist_ref.shape
    count = cells // 2
    rows_copy = pltpu.make_async_copy(face_ref, rows_ref, row_sem)
    rows_copy.start()
    copies = []
    for start in range(0, width, HALF):
        lanes = slice(start, start + HALF)
        copy = pltpu.make_async_copy(
            dist_ref.at[:, lanes], own_ref.at[:, lanes], sems.at[len(copies)]
        )
        copy.start()
        copies.append(copy)
    rows_copy.wait()
    for at, copy in enumerate(copies):
        copy.wait()
        side = at % 2
        source, target, first = at * HALF, at // 2 * HALF, (1 - side) * count

        def move(at, _):
            row = rows_ref[0, side, at]
            send_ref[pl.ds(first + at, 1), target : target + HALF] = own_ref[
                pl.ds(row, 1), source : source + HALF
            ]
            return 0

        lax.fori_loop(0, count, move, 0, unroll=True)


def far_plane_kernel(rows_ref, dist_ref, *send_refs):
    for part, send_ref in enumerate(send_refs):
        move_rows(rows_ref, dist_ref, send_ref, part)


def pass_kernel(value_ref, after_ref, out_ref):
    pass


def picks(near_ref, mask_ref, face, cell_start, cells):
    index = near_ref[face : face + 1, :] - cell_start
    hit = lax.broadcasted_iota(jnp.int32, (cells, cells), 0) == index
    open_face = mask_ref[face : face + 1, :] != 1
    return jnp.where(hit & open_face, 1.0, 0.0).astype(F32)


def along(near_ref, mask_ref, upward):
    cells = near_ref.shape[1]
    cell_start = lax.axis_index("space") * cells
    faces = [picks(near_ref, mask_ref, face, cell_start, cells) for face in range(6)]
    return [faces[0], faces[1], jnp.where(upward, faces[2], faces[3]), faces[4], faces[5]]


def stream_tiles(near_ref, mask_ref, value_ref, store):
    cells, width = value_ref.shape
    planes, upward = planes_y(width)
    chosen = []
    for face in along(near_ref, mask_ref, upward):
        flipped = face.T.astype(BF16)
        chosen.append(jnp.concatenate([flipped, flipped], axis=1))
    rest = jnp.concatenate(chosen[2:], axis=0)
    for start in range(0, width, COLUMN_TILE):
        side = chosen[0] if start % PLANE >= HALF else chosen[1]
        vel_x, vel_z = lane_points(start, COLUMN_TILE)
        values = value_ref[:, start : start + COLUMN_TILE]
        pieces = jnp.concatenate(split(values, 2), axis=0)
        moved = dot(jnp.concatenate([side, rest], axis=0), pieces)
        speed_x, speed_z = jnp.abs(vel_x), jnp.abs(vel_z)
        speed_y = jnp.abs(planes[start // PLANE])
        from_z = jnp.where(vel_z > 0, moved[2 * cells : 3 * cells], moved[3 * cells :])
        stream = (
            speed_x * moved[:cells]
            + speed_y * moved[cells : 2 * cells]
            + speed_z * from_z
            - (speed_x + speed_y + speed_z) * values
        )
        store(slice(start, start + COLUMN_TILE), values, stream)


def stream_kernel(near_ref, mask_ref, value_ref, out_ref):
    def store(lanes, values, stream):
        out_ref[:, lanes] = TIME_STEP * stream

    stream_tiles(near_ref, mask_ref, value_ref, store)


def stream_last_kernel(near_ref, mask_ref, dist_ref, middle_ref, out_ref):
    def store(lanes, values, stream):
        out_ref[:, lanes] = 0.5 * (dist_ref[:, lanes] + values) + (0.5 * TIME_STEP) * stream

    stream_tiles(near_ref, mask_ref, middle_ref, store)


def wall_kernel(face_ref, temp_ref, mask_ref, shape_ref, back_ref, side_ref, notes_ref):
    cells, width = shape_ref.shape
    count = cells // 2
    planes, _ = planes_y(width)
    inv_norm, cooling = wall_rows(temp_ref)
    mask = mask_ref[...]
    notes_ref[...] = jnp.concatenate([mask.astype(F32), inv_norm, cooling], axis=0)
    back_ref[...] = jnp.concatenate(
        [jnp.where(mask == 1, inv_norm, 0.0), cooling, jnp.zeros((1, cells), F32)],
        axis=0,
    )
    rows = [mask[:2].astype(F32), cooling, jnp.zeros((LANES - 3, cells), F32)]
    columns = jnp.concatenate(rows, axis=0).T
    row = lax.broadcasted_iota(jnp.int32, (cells, count), 0)
    for side, face in enumerate((1, 0)):
        hit = (row == face_ref[0, face : face + 1, :]) & (columns[:, face : face + 1] != 1.0)
        picked = jnp.where(hit, 1.0, 0.0).astype(BF16)
        side_ref[side * cells : (side + 1) * cells, :] = jnp.concatenate([picked, picked], axis=1)
    cooling = jnp.broadcast_to(columns[:, 2:3], (cells, LANES))
    for start in range(0, PLANE, LANES):
        vel_x, vel_z = lane_points(start, LANES)
        flat = vel_x * vel_x + vel_z * vel_z
        for at, vel_y in enumerate(planes):
            lanes = slice(at * PLANE + start, at * PLANE + start + LANES)
            shape_ref[:, lanes] = jnp.exp2((flat + vel_y * vel_y) * cooling)


def coefficients(sums, back, step, keep):
    count = sums[0:1]
    inv_count = 1.0 / count
    flow_x = (sums[11:12] - sums[10:11]) * inv_count
    flow_y = (sums[13:14] - sums[12:13]) * inv_count
    flow_z = (sums[15:16] - sums[14:15]) * inv_count
    p_xx, p_yy, p_zz, p_xy, p_xz, p_yz = (sums[at : at + 1] for at in range(1, 7))
    energy = p_xx + p_yy + p_zz
    flow_sq = flow_x * flow_x + flow_y * flow_y + flow_z * flow_z
    temp = (energy * inv_count - flow_sq) / 3.0
    inv_temp = 1.0 / temp

    def heat(third, flow, press):
        return 0.5 * (
            third
            - 2.0 * (press[0] * flow_x + press[1] * flow_y + press[2] * flow_z)
            - flow * energy
            + 2.0 * count * flow * flow_sq
        )

    scale = ((1.0 - MOMENTUM_RATIO) / 5.0) * inv_count * inv_temp * inv_temp * (-2.0 / LOG2E)
    rate = (count * jnp.exp((1.0 - SHEAR_EXPONENT) * jnp.log(temp))) * (step / BASELINE_SHEAR)
    returned = (back[0:6] * step) * sums[10:16]
    rows = [
        flow_x,
        flow_y,
        flow_z,
        (-0.5 * LOG2E) * inv_temp,
        scale * heat(sums[7:8], flow_x, (p_xx, p_xy, p_xz)),
        scale * heat(sums[8:9], flow_y, (p_xy, p_yy, p_yz)),
        scale * heat(sums[9:10], flow_z, (p_xz, p_yz, p_zz)),
        count * inv_temp * lax.rsqrt(temp) * rate,
        keep - rate,
    ]
    return rows, returned


def columns_of(sums, back, width, step, keep, more=()):
    _, upward = planes_y(width)
    rows, returned = coefficients(sums, back, step, keep)
    rows += [
        jnp.where(upward, returned[2:3], returned[3:4]),
        returned[0:2],
        returned[4:6],
        *more,
        jnp.zeros((LANES - 14 - sum(row.shape[0] for row in more), sums.shape[1]), F32),
    ]
    return jnp.concatenate(rows, axis=0).T


def relax(columns_ref, base_ref, value_ref, shape_ref, out_ref, planes_refs=None):
    cells, width = value_ref.shape
    half = planes_refs is not None
    planes, _ = planes_y(2 * width if half else width)
    lane = lax.broadcasted_iota(jnp.int32, (ROWS, LANES), 1)
    first_x, vel_z = point((lane >> 5) & (NV - 1)), point(lane & (NV - 1))
    z_plus, z_minus = jnp.maximum(vel_z, 0.0), jnp.maximum(-vel_z, 0.0)

    def group(at, _, tiles=range(PLANE // LANES), stride=PLANE):
        rows = pl.ds(pl.multiple_of(at * ROWS, ROWS), ROWS)
        columns = columns_ref[rows, :]
        flow_x, flow_y, flow_z, cool, heat_x, heat_y, heat_z, gain, keep, back_y, *back = (
            jnp.broadcast_to(columns[:, column : column + 1], (ROWS, LANES))
            for column in range(18 if half else 14)
        )
        if half:
            open_y, open_low, open_high, cooling = back[4:]
            open_z = jnp.where(vel_z > 0, open_low, open_high)
        rel_z = vel_z - flow_z
        square_z = rel_z * rel_z * cool
        heat_of_z = rel_z * heat_z
        back_z = z_plus * back[2] + z_minus * back[3]
        of_y = []
        for vel_y in planes:
            rel_y = vel_y - flow_y
            of_y.append((rel_y * rel_y * cool, rel_y * heat_y, jnp.abs(vel_y) * back_y))
        for tile in tiles:
            vel_x = first_x + (tile * (LANES // NV)) * SPACING
            rel_x = vel_x - flow_x
            square_xz = rel_x * rel_x * cool + square_z
            heat_xz = rel_x * heat_x + heat_of_z
            upper = tile * LANES >= HALF
            back_xz = jnp.abs(vel_x) * (back[0] if upper else back[1]) + back_z
            for plane, (square_y, heat_of_y, back_of_y) in enumerate(of_y):
                start = plane * stride + (tile - tiles[0]) * LANES
                lanes = slice(start, start + LANES)
                square = square_xz + square_y
                skew = (heat_xz + heat_of_y) * (square + 2.5 * LOG2E) + 1.0
                base = base_ref[rows, lanes]
                if half:
                    from_y_ref, from_z_ref = planes_refs
                    base += open_y * from_y_ref[rows, lanes] + open_z * from_z_ref[rows, lanes]
                    speed_sq = vel_x * vel_x + vel_z * vel_z + planes[plane] * planes[plane]
                    shape = jnp.exp2(speed_sq * cooling)
                else:
                    shape = shape_ref[rows, lanes]
                out_ref[rows, lanes] = (
                    base
                    + keep * value_ref[rows, lanes]
                    + gain * jnp.exp2(square) * skew
                    + shape * (back_xz + back_of_y)
                )
        return 0

    groups = cells // ROWS
    if half:
        low, high = range(HALF // LANES), range(HALF // LANES, PLANE // LANES)
        lax.fori_loop(
            0, groups // 2, functools.partial(group, tiles=high, stride=HALF), 0, unroll=True
        )
        lax.fori_loop(
            groups // 2, groups, functools.partial(group, tiles=low, stride=HALF), 0, unroll=True
        )
    else:
        lax.fori_loop(0, groups, group, 0, unroll=True)


def middle_kernel(sums_ref, back_ref, side_ref, own_ref, stream_ref, shape_ref, *refs):
    halo_refs, (out_ref, columns_ref, base_ref) = refs[:-3], refs[-3:]
    cells, width = own_ref.shape
    columns_ref[...] = columns_of(sums_ref[:SUMS], back_ref[...], width, TIME_STEP, 1.0)
    for side, tiles in enumerate(half_tiles(width)):
        pick = side_ref[side * cells : (side + 1) * cells, :]
        for source, target in tiles:
            lanes = slice(source, source + COLUMN_TILE)
            vel_x, _ = lane_points(source, COLUMN_TILE)
            rows = halo_rows(halo_refs, 1 - side)[:, target : target + COLUMN_TILE]
            halo = dot(pick, jnp.concatenate(split(rows, 2), axis=0))
            base_ref[:, lanes] = stream_ref[:, lanes] + (TIME_STEP * jnp.abs(vel_x)) * halo
    relax(columns_ref, base_ref, own_ref, shape_ref, out_ref)


def relax_kernel(sums_ref, back_ref, middle_ref, part_ref, shape_ref, out_ref, columns_ref):
    width = middle_ref.shape[1]
    step = 0.5 * TIME_STEP
    columns_ref[...] = columns_of(sums_ref[...], back_ref[...], width, step, 0.0)
    relax(columns_ref, part_ref, middle_ref, shape_ref, out_ref)


ORDERS = (
    [(0, 0, 0)],
    [(2, 0, 0)],
    [(0, 2, 0)],
    [(0, 0, 2)],
    [(1, 1, 0)],
    [(1, 0, 1)],
    [(0, 1, 1)],
    [(3, 0, 0), (1, 2, 0), (1, 0, 2)],
    [(0, 3, 0), (2, 1, 0), (0, 1, 2)],
    [(0, 0, 3), (2, 0, 1), (0, 2, 1)],
    [("-", 0, 0)],
    [("+", 0, 0)],
    [(0, "-", 0)],
    [(0, "+", 0)],
    [(0, 0, "-")],
    [(0, 0, "+")],
)


def power(value, order):
    if order == "+":
        return jnp.maximum(value, 0.0)
    if order == "-":
        return jnp.maximum(-value, 0.0)
    result = None
    for _ in range(order):
        result = value if result is None else result * value
    return result


def advance_kernel(face_ref, near_ref, _, __, mask_ref, sums_ref, back_ref, *refs):
    shared_refs, out_ref = refs[:-1], refs[-1]
    cells = near_ref.shape[1]
    cell_start = lax.axis_index("space") * cells
    sums = sums_ref[:SUMS]
    packed = [sums_ref[flux_start(face) : flux_start(face + 1)] for face in range(FACES)]
    flux = [flux_rows(sums, packed, face) for face in range(FACES)]
    gas = 0.0
    for face in range(FACES):
        hits = picks(near_ref, mask_ref, face, cell_start, cells).astype(BF16)
        gas += exact(flux[face], hits) - flux[face]
    for face, hits in enumerate(face_hits(face_ref, cells)):
        base = halo_rows(shared_refs, face, slice(0, SUMS))
        count = len(kept(face))
        own = halo_rows(shared_refs, face, slice(SUMS + NOTES, SUMS + NOTES + count))
        arrived = flux_rows(base, {face: own}, face)
        found = exact(arrived, hits.astype(BF16), ((1,), (1,)))
        gas += jnp.where(mask_ref[face : face + 1, :] != 1, found, 0.0)

    rows, returned = coefficients(sums, back_ref[...], TIME_STEP, 1.0)
    flows, cool, heats, gain, keep = rows[0:3], rows[3], rows[4:7], rows[7], rows[8]
    points = jnp.broadcast_to(point(lax.broadcasted_iota(jnp.int32, (NV, cells), 0)), (NV, cells))
    axes = []
    for flow in flows:
        off = points - flow
        bell = jnp.exp2(off * off * cool)
        axes.append([bell, bell * off, bell * off * off, bell * off * off * off])
    known = {}

    def along_axis(axis, order):
        if (axis, order) not in known:
            factor = power(points, order)
            known[axis, order] = [
                jnp.sum(term if factor is None else factor * term, axis=0, keepdims=True)
                for term in axes[axis]
            ]
        return known[axis, order]

    wall_bell = jnp.exp2(points * points * back_ref[6:7])
    above = jnp.maximum(points, 0.0)
    wall_sums = [jnp.sum(jnp.where(points > 0, wall_bell, 0.0), axis=0, keepdims=True)]
    for _ in range(4):
        wall_bell = wall_bell * above
        wall_sums.append(jnp.sum(wall_bell, axis=0, keepdims=True))

    def wall_full(order):
        if order in ("+", "-"):
            return wall_sums[1]
        return None if order % 2 else 2.0 * wall_sums[order]

    def wall_half(order, sign):
        if order in ("+", "-"):
            return wall_sums[2] if order == sign else None
        found = wall_sums[order + 1]
        return -found if order % 2 and sign == "-" else found

    found_rows = []
    for orders in ORDERS:
        bells, walls = 0.0, 0.0
        for order in orders:
            (x0, x1, x2, x3), (y0, y1, y2, y3), (z0, z1, z2, z3) = (
                along_axis(axis, order[axis]) for axis in range(3)
            )
            xy, xz, yz = x0 * y0, x0 * z0, y0 * z0
            skew = heats[0] * (x1 * (BEND * yz + cool * (y2 * z0 + y0 * z2)) + cool * x3 * yz)
            skew += heats[1] * (y1 * (BEND * xz + cool * (x2 * z0 + x0 * z2)) + cool * y3 * xz)
            skew += heats[2] * (z1 * (BEND * xy + cool * (x2 * y0 + x0 * y2)) + cool * z3 * xy)
            bells += xy * z0 + skew
            for face in range(FACES):
                terms = [
                    wall_half(order[axis], "+-"[face % 2])
                    if axis == face // 2
                    else wall_full(order[axis])
                    for axis in range(3)
                ]
                if all(term is not None for term in terms):
                    walls += returned[face : face + 1] * terms[0] * terms[1] * terms[2]
        found_rows.append(gain * bells + walls)
    found = WEIGHT * jnp.concatenate(found_rows, axis=0)
    out_ref[...] = found + keep * sums + TIME_STEP * gas


def halo_stream_kernel(face_ref, near_ref, *refs):
    halo_refs, (base_ref, from_y_ref, from_z_ref, values_ref) = refs[:-4], refs[-4:]
    rows, width = base_ref.shape
    count = rows // 2
    planes, upward = planes_y(2 * width)
    cell_start = lax.axis_index("space") * rows
    low = face_hits(face_ref, rows)[0]
    low_flipped, low = low.T.astype(BF16), low.astype(BF16)
    row = lax.broadcasted_iota(jnp.int32, (rows, rows), 0)
    steps = []
    for face in range(2, FACES):
        hits = jnp.where(row == near_ref[face : face + 1, :] - cell_start, 1.0, 0.0)
        from_rows = dot(low_flipped, hits.T.astype(BF16)).astype(BF16)
        steps.append(dot(from_rows, low))
    along_y = jnp.where(upward, steps[0], steps[1])
    picks_all = jnp.concatenate([along_y, steps[2], steps[3]], axis=0).astype(BF16)
    picks_all = jnp.concatenate([picks_all, picks_all], axis=1)
    for side in range(2):
        block = slice(side * count, (side + 1) * count)
        values_ref[block, :] = halo_rows(halo_refs, side)
        for start in range(0, width, COLUMN_TILE):
            lanes = slice(start, start + COLUMN_TILE)
            vel_x, vel_z = lane_points((1 - side) * HALF + start % HALF, COLUMN_TILE)
            vel_y = planes[start // HALF]
            values = values_ref[block, lanes]
            moved = dot(picks_all, jnp.concatenate(split(values, 2), axis=0))
            speed_x, speed_y, speed_z = jnp.abs(vel_x), jnp.abs(vel_y), jnp.abs(vel_z)
            from_z = jnp.where(vel_z > 0, moved[count : 2 * count], moved[2 * count :])
            from_y_ref[block, lanes] = (TIME_STEP * speed_y) * moved[:count]
            from_z_ref[block, lanes] = (TIME_STEP * speed_z) * from_z
            base_ref[block, lanes] = -TIME_STEP * (speed_x + speed_y + speed_z) * values


def halo_relax_kernel(base_ref, from_y_ref, from_z_ref, values_ref, *refs):
    shared_refs, (out_ref, open_ref, columns_ref) = refs[:-3], refs[-3:]
    rows, width = values_ref.shape
    _, upward = planes_y(2 * width)
    sums = shared_rows(shared_refs, 0, SUMS)
    notes = shared_rows(shared_refs, SUMS, SUMS + NOTES)
    back = jnp.where(notes[:FACES] == 1.0, notes[6:7], 0.0)
    passing = jnp.where(notes[:FACES] != 1.0, 1.0, 0.0)
    lane = lax.broadcasted_iota(jnp.int32, (1, rows), 1)
    more = [
        jnp.where(upward, passing[2:3], passing[3:4]),
        passing[4:6],
        notes[7:8],
        TIME_STEP * jnp.where(lane < rows // 2, passing[0:1], passing[1:2]),
    ]
    columns = columns_of(sums, back, 2 * width, TIME_STEP, 1.0, more)
    columns_ref[...] = columns
    open_ref[...] = jnp.broadcast_to(columns[:, 18:19], (rows, LANES))
    relax(columns_ref, base_ref, values_ref, None, out_ref, (from_y_ref, from_z_ref))


def last_kernel(part, side_ref, part_ref, plane_ref, open_ref, *refs):
    refs, (out_ref, result_ref, sems) = refs[:-3], refs[-3:]
    halo_refs = refs[part > 0 :]
    cells, width = part_ref.shape
    count = cells // 2
    copies = []
    for side, tiles in enumerate(half_tiles(width, part, PARTS)):
        pick = side_ref[side * cells : (side + 1) * cells, :]
        block = slice((1 - side) * count, (2 - side) * count)
        gate = jnp.concatenate([open_ref[block]] * (COLUMN_TILE // LANES), axis=1)
        begin = tiles[0][1]
        for source, target in tiles:
            lanes = slice(source, source + COLUMN_TILE)
            speed_x = jnp.abs(lane_points(source, COLUMN_TILE)[0])
            rows = halo_rows(halo_refs, 1 - side)[:, target - begin : target - begin + COLUMN_TILE]
            rows = plane_ref[block, target : target + COLUMN_TILE] + gate * speed_x * rows
            halo = dot(pick, jnp.concatenate(split(rows, 2), axis=0))
            result_ref[:, lanes] = part_ref[:, lanes] + (0.5 * TIME_STEP * speed_x) * halo
            copy = pltpu.make_async_copy(
                result_ref.at[:, lanes], out_ref.at[:, lanes], sems.at[len(copies)]
            )
            copy.start()
            copies.append(copy)
    for copy in copies:
        copy.wait()


def call(kernel, outs, arrays, scratch=(), scalars=0, far_outs=False, unread=(), aliases=None):
    spaces = [
        pltpu.SMEM if at < scalars else pl.ANY if at in unread else pltpu.VMEM
        for at in range(len(arrays))
    ]
    if isinstance(kernel, functools.partial):
        name = f"{kernel.func.__name__}_{kernel.args[0]}"
    else:
        name = kernel.__name__
    size = sum(math.prod(array.shape) * 4 for array in arrays)
    return pl.pallas_call(
        kernel,
        out_shape=[jax.ShapeDtypeStruct(shape, dtype) for shape, dtype in outs],
        in_specs=[pl.BlockSpec(memory_space=space) for space in spaces],
        out_specs=[pl.BlockSpec(memory_space=pl.ANY if far_outs else pltpu.VMEM)] * len(outs),
        scratch_shapes=list(scratch),
        input_output_aliases=aliases or {},
        name=name,
        compiler_params=pltpu.CompilerParams(vmem_limit_bytes=40 * 2**20),
        cost_estimate=pl.CostEstimate(
            flops=COST.get(name, 0), bytes_accessed=size, transcendentals=0
        ),
    )(*arrays)


COST = {"advance_kernel": 14 * 10**8, "last_kernel_0": 4 * 10**9}


def total(value):
    count = lax.axis_size("vel")
    step = 1
    while step < count:
        value = value + lax.ppermute(value, "vel", [(i, i ^ step) for i in range(count)])
        step *= 2
    return value


def exchange(send):
    count = lax.axis_size("space")
    forward = [(i, (i + 1) % count) for i in range(count)]
    backward = [(target, source) for source, target in forward]
    if count == 2:
        return [lax.ppermute(send, "space", forward)]
    half = send.shape[0] // 2
    return [
        lax.ppermute(send[:half], "space", forward),
        lax.ppermute(send[half:], "space", backward),
    ]


def on_device(dist, wall_temp, neighbours, wall_mask, face_rows):
    cells, width = dist.shape
    count, half = cells // 2, width // 2
    temp = wall_temp[None, :]
    whole, plane = ((cells, width), F32), ((cells, half), F32)
    every = flux_start(FACES)
    columns = pltpu.VMEM((cells, LANES), F32)

    dist, sent = call(
        near_plane_kernel,
        [whole, plane],
        [
            pltpu.with_memory_space_constraint(face_rows, pltpu.HBM),
            pltpu.with_memory_space_constraint(dist, pltpu.HBM),
        ],
        [
            pltpu.SMEM(face_rows.shape, jnp.int32),
            pltpu.SemaphoreType.DMA(()),
            pltpu.SemaphoreType.DMA((width // HALF,)),
        ],
        unread=(0, 1),
    )
    near = exchange(sent)
    (sums,) = call(sums_kernel, [((every, cells), F32)], [dist])
    sums = total(sums)
    shape, back, side, notes = call(
        wall_kernel,
        [whole, ((8, cells), F32), ((2 * cells, cells), BF16), ((NOTES, cells), F32)],
        [face_rows, temp, wall_mask],
    )
    (stream,) = call(stream_kernel, [whole], [neighbours, wall_mask, dist])
    (sent,) = call(
        share_kernel,
        [((2 * (2 * SUMS + NOTES), count), F32)],
        [face_rows, sums, notes, stream],
        unread=(3,),
    )
    shared = exchange(sent)
    part_shape = ((cells, half // PARTS), F32)
    far_rows = call(far_plane_kernel, [part_shape] * PARTS, [face_rows, dist], scalars=1)
    far = []
    for part in range(PARTS):
        rows = far_rows[part]
        if part:
            (rows,) = call(
                pass_kernel,
                [part_shape],
                [rows, sent],
                far_outs=True,
                unread=(0, 1),
                aliases={0: 0},
            )
        far.append(exchange(rows))
    (middle,) = call(
        middle_kernel,
        [whole],
        [sums, back, side, dist, stream, shape, *near],
        [columns, pltpu.VMEM((cells, width), F32)],
    )
    (part_sum,) = call(stream_last_kernel, [whole], [neighbours, wall_mask, dist, middle])
    halo_parts = call(halo_stream_kernel, [plane] * 4, [face_rows, neighbours, *near])
    (sums_two,) = call(
        advance_kernel,
        [((SUMS, cells), F32)],
        [face_rows, neighbours, part_sum, halo_parts[0], wall_mask, sums, back, *shared],
        unread=(2, 3),
    )
    (part_sum,) = call(relax_kernel, [whole], [sums_two, back, middle, part_sum, shape], [columns])
    plane_one, gate = call(
        halo_relax_kernel, [plane, ((cells, LANES), F32)], [*halo_parts, *shared], [columns]
    )
    result = []
    for part in range(PARTS):
        result = call(
            functools.partial(last_kernel, part),
            [whole],
            [side, part_sum, plane_one, gate, *result, *far[part]],
            [
                pltpu.VMEM((cells, width), F32),
                pltpu.SemaphoreType.DMA((width // COLUMN_TILE // PARTS,)),
            ],
            far_outs=True,
            unread=(4,) if part else (),
            aliases={4: 0} if part else None,
        )
    return result[0]


def solution(mesh):
    return jax.shard_map(
        on_device,
        mesh=mesh,
        in_specs=(
            P("space", "vel"),
            P("space"),
            P(None, "space"),
            P(None, "space"),
            P("space", None, None),
        ),
        out_specs=P("space", "vel"),
        check_vma=False,
    )
```

```python
import functools
import math

import jax
import jax.numpy as jnp
from jax import lax
from jax.experimental import pallas as pl
from jax.experimental.pallas import tpu as pltpu
from jax.sharding import PartitionSpec as P

NV = 32
LIMIT = 4.5
SPACING = 2.0 * LIMIT / NV
WEIGHT = SPACING**3 * (2.0 * math.pi) ** (-1.5)
TIME_STEP = 0.05
BASELINE_SHEAR = 0.1
SHEAR_EXPONENT = 0.66
MOMENTUM_RATIO = 2.0 / 3.0
PLANE = NV * NV
HALF = PLANE // 2
ROWS = 8
LANES = 128
COLUMN_TILE = 256
SUMS = 16
FACES = 6
NOTES = 8
BEND = 2.5 * math.log2(math.e)
LOG2E = math.log2(math.e)
F32 = jnp.float32
BF16 = jnp.bfloat16


def point(slot):
    return -LIMIT + (slot.astype(F32) + 0.5) * SPACING


def lane_points(start, width):
    lane = lax.broadcasted_iota(jnp.int32, (1, width), 1) + start
    return point((lane >> 5) & (NV - 1)), point(lane & (NV - 1))


def planes_y(width):
    planes = width // PLANE
    first = lax.axis_index("vel") * planes
    return [point(first + at) for at in range(planes)], first >= NV // 2


def split(value, count):
    pieces = []
    for _ in range(count - 1):
        piece = value.astype(BF16)
        pieces.append(piece)
        value = value - piece.astype(F32)
    pieces.append(value.astype(BF16))
    return pieces


def dot(left, right, dims=((1,), (0,))):
    return lax.dot_general(left, right, (dims, ((), ())), preferred_element_type=F32)


def kept(face):
    other = face ^ 1
    return [*range(1, 10)] + [
        10 + out for out in range(FACES) if out == other or out // 2 > other // 2
    ]


def flux_start(face):
    return SUMS + sum(len(kept(before)) for before in range(face))


def flux_rows(base, packed, face):
    other = face ^ 1
    mine = packed[face]
    rows = [base[10 + other : 11 + other], mine[:9]]
    for out in range(FACES):
        if out == face:
            rows.append(jnp.zeros_like(mine[:1]))
            continue
        holder, row = (face, 10 + out) if 10 + out in kept(face) else (out ^ 1, 10 + other)
        at = kept(holder).index(row)
        rows.append(packed[holder][at : at + 1])
    return jnp.concatenate(rows, axis=0)


def exact(left, right, dims=((1,), (0,))):
    rows = left.shape[0]
    found = dot(jnp.concatenate(split(left, 3), axis=0), right, dims)
    return found[:rows] + found[rows : 2 * rows] + found[2 * rows :]


def inward(vel_x, vel_y, vel_z):
    return [
        jnp.maximum(sign * vel, 0.0) for vel in (vel_x, vel_y, vel_z) for sign in (1.0, -1.0)
    ]


def weights(vel_x, vel_y, vel_z):
    speed_sq = vel_x * vel_x + vel_y * vel_y + vel_z * vel_z
    into = inward(vel_x, vel_y, vel_z)
    rows = [
        jnp.ones_like(vel_x),
        vel_x * vel_x,
        vel_y * vel_y,
        vel_z * vel_z,
        vel_x * vel_y,
        vel_x * vel_z,
        vel_y * vel_z,
        vel_x * speed_sq,
        vel_y * speed_sq,
        vel_z * speed_sq,
        into[1],
        into[0],
        into[3],
        into[2],
        into[5],
        into[4],
    ]
    return WEIGHT * jnp.concatenate(rows, axis=0), into


def face_hits(face_ref, cells):
    row = lax.broadcasted_iota(jnp.int32, (cells, face_ref.shape[2]), 0)
    return [jnp.where(row == face_ref[0, side : side + 1, :], 1.0, 0.0) for side in range(2)]


def sums_kernel(dist_ref, sums_ref):
    width = dist_ref.shape[1]
    planes, _ = planes_y(width)
    total = None
    for start in range(0, width, HALF):
        lanes = slice(start, start + HALF)
        vel_x, vel_z = lane_points(start, HALF)
        vel_y = jnp.full((1, HALF), planes[start // PLANE])
        base, into = weights(vel_x, vel_y, vel_z)
        table = [base]
        for face, speed in enumerate(into):
            fluxes = base * speed
            table.append(fluxes[1:10])
            table += [fluxes[row : row + 1] for row in kept(face)[9:]]
        table = jnp.concatenate(table, axis=0)
        coarse, fine = split(table, 2)
        finest = split(base, 3)[2]
        pieces = split(dist_ref[:, lanes], 3)
        across = ((1,), (1,))
        one = dot(jnp.concatenate([coarse, fine, finest], axis=0), pieces[0], across)
        two = dot(jnp.concatenate([coarse, fine], axis=0), pieces[1], across)
        three = dot(coarse, pieces[2], across)
        rows = table.shape[0]
        part = one[:rows] + one[rows : 2 * rows] + two[:rows] + two[rows:] + three
        part = jnp.concatenate([part[:SUMS] + one[2 * rows :], part[SUMS:]], axis=0)
        total = part if total is None else total + part
    sums_ref[...] = total


def share_kernel(face_ref, sums_ref, notes_ref, send_ref):
    low, high = face_hits(face_ref, sums_ref.shape[1])
    for side, hits in ((0, high), (1, low)):
        rows = [sums_ref[:SUMS], notes_ref[...], sums_ref[flux_start(side) : flux_start(side + 1)]]
        rows = exact(jnp.concatenate(rows, axis=0), hits.astype(BF16))
        first = side * (send_ref.shape[0] // 2)
        send_ref[first : first + rows.shape[0], :] = rows


def halo_rows(refs, side, rows=slice(None)):
    if len(refs) == 2:
        return refs[side][rows]
    half = refs[0].shape[0] // 2
    start, stop, _ = rows.indices(half)
    return refs[0][side * half + start : side * half + stop]


def shared_rows(refs, start, stop):
    rows = slice(start, stop)
    return jnp.concatenate([halo_rows(refs, 0, rows), halo_rows(refs, 1, rows)], axis=1)


def half_tiles(start, stop, most):
    low, high = [], []
    while start < stop:
        size = min(start // most * most + most, stop) - start
        source = start // HALF * PLANE + start % HALF
        low.append((source, start, size))
        high.append((source + HALF, start, size))
        start += size
    return low, high


def far_parts(half):
    tiles = half // LANES
    cut = (5 * tiles + 7) // 8 * LANES
    return [(0, cut), (cut, half)]


def move_rows(rows_ref, value_ref, send_ref, start, stop):
    cells, width = value_ref.shape
    count = cells // 2
    low, high = half_tiles(start, stop, HALF)

    def move(at, _):
        for first, tiles, plane in ((0, high, 0), (count, low, 1)):
            row = rows_ref[0, plane, at]
            for source, target, size in tiles:
                wide = max(size, 2 * LANES)
                begin = min(source, width - wide)
                values = value_ref[pl.ds(row, 1), begin : begin + wide]
                send_ref[pl.ds(first + at, 1), target - start : target - start + size] = values[
                    :, source - begin : source - begin + size
                ]
        return 0

    lax.fori_loop(0, count, move, 0, unroll=True)


def wall_rows(temp_ref):
    cooling = (-0.5 * LOG2E) / temp_ref[...]
    axis_point = point(lax.broadcasted_iota(jnp.int32, (NV, 1), 0))
    profile = jnp.exp2(axis_point * axis_point * cooling)
    mass = jnp.sum(profile, axis=0, keepdims=True)
    flux = jnp.sum(jnp.maximum(axis_point, 0.0) * profile, axis=0, keepdims=True)
    return 1.0 / (WEIGHT * flux * mass * mass), cooling


def near_plane_kernel(face_ref, dist_ref, own_ref, send_ref, rows_ref, row_sem, sems):
    cells, width = dist_ref.shape
    count = cells // 2
    rows_copy = pltpu.make_async_copy(face_ref, rows_ref, row_sem)
    rows_copy.start()
    copies = []
    for start in range(0, width, HALF):
        lanes = slice(start, start + HALF)
        copy = pltpu.make_async_copy(
            dist_ref.at[:, lanes], own_ref.at[:, lanes], sems.at[len(copies)]
        )
        copy.start()
        copies.append(copy)
    rows_copy.wait()
    for at, copy in enumerate(copies):
        copy.wait()
        side = at % 2
        source, target, first = at * HALF, at // 2 * HALF, (1 - side) * count

        def move(at, _):
            row = rows_ref[0, side, at]
            send_ref[pl.ds(first + at, 1), target : target + HALF] = own_ref[
                pl.ds(row, 1), source : source + HALF
            ]
            return 0

        lax.fori_loop(0, count, move, 0, unroll=True)


def far_plane_kernel(rows_ref, dist_ref, *send_refs):
    for (start, stop), send_ref in zip(far_parts(dist_ref.shape[1] // 2), send_refs):
        move_rows(rows_ref, dist_ref, send_ref, start, stop)


def pass_kernel(value_ref, after_ref, out_ref):
    pass


def picks(near_ref, mask_ref, face, cell_start, cells):
    index = near_ref[face : face + 1, :] - cell_start
    hit = lax.broadcasted_iota(jnp.int32, (cells, cells), 0) == index
    open_face = mask_ref[face : face + 1, :] != 1
    return jnp.where(hit & open_face, 1.0, 0.0).astype(F32)


def along(near_ref, mask_ref, upward):
    cells = near_ref.shape[1]
    cell_start = lax.axis_index("space") * cells
    faces = [picks(near_ref, mask_ref, face, cell_start, cells) for face in range(6)]
    return [faces[0], faces[1], jnp.where(upward, faces[2], faces[3]), faces[4], faces[5]]


def stream_tiles(near_ref, mask_ref, value_ref, store):
    cells, width = value_ref.shape
    planes, upward = planes_y(width)
    chosen = []
    for face in along(near_ref, mask_ref, upward):
        flipped = face.T.astype(BF16)
        chosen.append(jnp.concatenate([flipped, flipped], axis=1))
    rest = jnp.concatenate(chosen[2:], axis=0)
    for start in range(0, width, COLUMN_TILE):
        side = chosen[0] if start % PLANE >= HALF else chosen[1]
        vel_x, vel_z = lane_points(start, COLUMN_TILE)
        values = value_ref[:, start : start + COLUMN_TILE]
        pieces = jnp.concatenate(split(values, 2), axis=0)
        moved = dot(jnp.concatenate([side, rest], axis=0), pieces)
        speed_x, speed_z = jnp.abs(vel_x), jnp.abs(vel_z)
        speed_y = jnp.abs(planes[start // PLANE])
        from_z = jnp.where(vel_z > 0, moved[2 * cells : 3 * cells], moved[3 * cells :])
        stream = (
            speed_x * moved[:cells]
            + speed_y * moved[cells : 2 * cells]
            + speed_z * from_z
            - (speed_x + speed_y + speed_z) * values
        )
        store(slice(start, start + COLUMN_TILE), values, stream)


def stream_kernel(near_ref, mask_ref, value_ref, out_ref):
    def store(lanes, values, stream):
        out_ref[:, lanes] = TIME_STEP * stream

    stream_tiles(near_ref, mask_ref, value_ref, store)


def stream_last_kernel(near_ref, mask_ref, dist_ref, middle_ref, out_ref):
    def store(lanes, values, stream):
        out_ref[:, lanes] = 0.5 * (dist_ref[:, lanes] + values) + (0.5 * TIME_STEP) * stream

    stream_tiles(near_ref, mask_ref, middle_ref, store)


def wall_kernel(face_ref, temp_ref, mask_ref, shape_ref, back_ref, side_ref, notes_ref):
    cells, width = shape_ref.shape
    count = cells // 2
    planes, _ = planes_y(width)
    inv_norm, cooling = wall_rows(temp_ref)
    mask = mask_ref[...]
    notes_ref[...] = jnp.concatenate([mask.astype(F32), inv_norm, cooling], axis=0)
    back_ref[...] = jnp.concatenate(
        [jnp.where(mask == 1, inv_norm, 0.0), cooling, jnp.zeros((1, cells), F32)],
        axis=0,
    )
    rows = [mask[:2].astype(F32), cooling, jnp.zeros((LANES - 3, cells), F32)]
    columns = jnp.concatenate(rows, axis=0).T
    row = lax.broadcasted_iota(jnp.int32, (cells, count), 0)
    for side, face in enumerate((1, 0)):
        hit = (row == face_ref[0, face : face + 1, :]) & (columns[:, face : face + 1] != 1.0)
        picked = jnp.where(hit, 1.0, 0.0).astype(BF16)
        side_ref[side * cells : (side + 1) * cells, :] = jnp.concatenate([picked, picked], axis=1)
    cooling = jnp.broadcast_to(columns[:, 2:3], (cells, LANES))
    for start in range(0, PLANE, LANES):
        vel_x, vel_z = lane_points(start, LANES)
        flat = vel_x * vel_x + vel_z * vel_z
        for at, vel_y in enumerate(planes):
            lanes = slice(at * PLANE + start, at * PLANE + start + LANES)
            shape_ref[:, lanes] = jnp.exp2((flat + vel_y * vel_y) * cooling)


def coefficients(sums, back, step, keep):
    count = sums[0:1]
    inv_count = 1.0 / count
    flow_x = (sums[11:12] - sums[10:11]) * inv_count
    flow_y = (sums[13:14] - sums[12:13]) * inv_count
    flow_z = (sums[15:16] - sums[14:15]) * inv_count
    p_xx, p_yy, p_zz, p_xy, p_xz, p_yz = (sums[at : at + 1] for at in range(1, 7))
    energy = p_xx + p_yy + p_zz
    flow_sq = flow_x * flow_x + flow_y * flow_y + flow_z * flow_z
    temp = (energy * inv_count - flow_sq) / 3.0
    inv_temp = 1.0 / temp

    def heat(third, flow, press):
        return 0.5 * (
            third
            - 2.0 * (press[0] * flow_x + press[1] * flow_y + press[2] * flow_z)
            - flow * energy
            + 2.0 * count * flow * flow_sq
        )

    scale = ((1.0 - MOMENTUM_RATIO) / 5.0) * inv_count * inv_temp * inv_temp * (-2.0 / LOG2E)
    rate = (count * jnp.exp((1.0 - SHEAR_EXPONENT) * jnp.log(temp))) * (step / BASELINE_SHEAR)
    returned = (back[0:6] * step) * sums[10:16]
    rows = [
        flow_x,
        flow_y,
        flow_z,
        (-0.5 * LOG2E) * inv_temp,
        scale * heat(sums[7:8], flow_x, (p_xx, p_xy, p_xz)),
        scale * heat(sums[8:9], flow_y, (p_xy, p_yy, p_yz)),
        scale * heat(sums[9:10], flow_z, (p_xz, p_yz, p_zz)),
        count * inv_temp * lax.rsqrt(temp) * rate,
        keep - rate,
    ]
    return rows, returned


def columns_of(sums, back, width, step, keep, more=()):
    _, upward = planes_y(width)
    rows, returned = coefficients(sums, back, step, keep)
    rows += [
        jnp.where(upward, returned[2:3], returned[3:4]),
        returned[0:2],
        returned[4:6],
        *more,
        jnp.zeros((LANES - 14 - sum(row.shape[0] for row in more), sums.shape[1]), F32),
    ]
    return jnp.concatenate(rows, axis=0).T


def relax(columns_ref, base_ref, value_ref, shape_ref, out_ref, planes_refs=None):
    cells, width = value_ref.shape
    half = planes_refs is not None
    planes, _ = planes_y(2 * width if half else width)
    lane = lax.broadcasted_iota(jnp.int32, (ROWS, LANES), 1)
    first_x, vel_z = point((lane >> 5) & (NV - 1)), point(lane & (NV - 1))
    z_plus, z_minus = jnp.maximum(vel_z, 0.0), jnp.maximum(-vel_z, 0.0)

    def group(at, _, tiles=range(PLANE // LANES), stride=PLANE):
        rows = pl.ds(pl.multiple_of(at * ROWS, ROWS), ROWS)
        columns = columns_ref[rows, :]
        flow_x, flow_y, flow_z, cool, heat_x, heat_y, heat_z, gain, keep, back_y, *back = (
            jnp.broadcast_to(columns[:, column : column + 1], (ROWS, LANES))
            for column in range(18 if half else 14)
        )
        if half:
            open_y, open_low, open_high, cooling = back[4:]
            open_z = jnp.where(vel_z > 0, open_low, open_high)
        rel_z = vel_z - flow_z
        square_z = rel_z * rel_z * cool
        heat_of_z = rel_z * heat_z
        back_z = z_plus * back[2] + z_minus * back[3]
        of_y = []
        for vel_y in planes:
            rel_y = vel_y - flow_y
            of_y.append((rel_y * rel_y * cool, rel_y * heat_y, jnp.abs(vel_y) * back_y))
        for tile in tiles:
            vel_x = first_x + (tile * (LANES // NV)) * SPACING
            rel_x = vel_x - flow_x
            square_xz = rel_x * rel_x * cool + square_z
            heat_xz = rel_x * heat_x + heat_of_z
            upper = tile * LANES >= HALF
            back_xz = jnp.abs(vel_x) * (back[0] if upper else back[1]) + back_z
            for plane, (square_y, heat_of_y, back_of_y) in enumerate(of_y):
                start = plane * stride + (tile - tiles[0]) * LANES
                lanes = slice(start, start + LANES)
                square = square_xz + square_y
                skew = (heat_xz + heat_of_y) * (square + 2.5 * LOG2E) + 1.0
                base = base_ref[rows, lanes]
                if half:
                    from_y_ref, from_z_ref = planes_refs
                    base += open_y * from_y_ref[rows, lanes] + open_z * from_z_ref[rows, lanes]
                    speed_sq = vel_x * vel_x + vel_z * vel_z + planes[plane] * planes[plane]
                    shape = jnp.exp2(speed_sq * cooling)
                else:
                    shape = shape_ref[rows, lanes]
                out_ref[rows, lanes] = (
                    base
                    + keep * value_ref[rows, lanes]
                    + gain * jnp.exp2(square) * skew
                    + shape * (back_xz + back_of_y)
                )
        return 0

    groups = cells // ROWS
    if half:
        low, high = range(HALF // LANES), range(HALF // LANES, PLANE // LANES)
        lax.fori_loop(
            0, groups // 2, functools.partial(group, tiles=high, stride=HALF), 0, unroll=True
        )
        lax.fori_loop(
            groups // 2, groups, functools.partial(group, tiles=low, stride=HALF), 0, unroll=True
        )
    else:
        lax.fori_loop(0, groups, group, 0, unroll=True)


def middle_kernel(sums_ref, back_ref, side_ref, own_ref, stream_ref, shape_ref, *refs):
    halo_refs, (out_ref, columns_ref, base_ref) = refs[:-3], refs[-3:]
    cells, width = own_ref.shape
    columns_ref[...] = columns_of(sums_ref[:SUMS], back_ref[...], width, TIME_STEP, 1.0)
    for side, tiles in enumerate(half_tiles(0, width // 2, COLUMN_TILE)):
        pick = side_ref[side * cells : (side + 1) * cells, :]
        for source, target, _ in tiles:
            lanes = slice(source, source + COLUMN_TILE)
            vel_x, _ = lane_points(source, COLUMN_TILE)
            rows = halo_rows(halo_refs, 1 - side)[:, target : target + COLUMN_TILE]
            halo = dot(pick, jnp.concatenate(split(rows, 2), axis=0))
            base_ref[:, lanes] = stream_ref[:, lanes] + (TIME_STEP * jnp.abs(vel_x)) * halo
    relax(columns_ref, base_ref, own_ref, shape_ref, out_ref)


def relax_kernel(sums_ref, back_ref, middle_ref, part_ref, shape_ref, out_ref, columns_ref):
    width = middle_ref.shape[1]
    step = 0.5 * TIME_STEP
    columns_ref[...] = columns_of(sums_ref[...], back_ref[...], width, step, 0.0)
    relax(columns_ref, part_ref, middle_ref, shape_ref, out_ref)


ORDERS = (
    [(0, 0, 0)],
    [(2, 0, 0)],
    [(0, 2, 0)],
    [(0, 0, 2)],
    [(1, 1, 0)],
    [(1, 0, 1)],
    [(0, 1, 1)],
    [(3, 0, 0), (1, 2, 0), (1, 0, 2)],
    [(0, 3, 0), (2, 1, 0), (0, 1, 2)],
    [(0, 0, 3), (2, 0, 1), (0, 2, 1)],
    [("-", 0, 0)],
    [("+", 0, 0)],
    [(0, "-", 0)],
    [(0, "+", 0)],
    [(0, 0, "-")],
    [(0, 0, "+")],
)


def power(value, order):
    if order == "+":
        return jnp.maximum(value, 0.0)
    if order == "-":
        return jnp.maximum(-value, 0.0)
    result = None
    for _ in range(order):
        result = value if result is None else result * value
    return result


def advance_kernel(face_ref, near_ref, mask_ref, sums_ref, back_ref, *refs):
    shared_refs, out_ref = refs[:-1], refs[-1]
    cells = near_ref.shape[1]
    cell_start = lax.axis_index("space") * cells
    sums = sums_ref[:SUMS]
    packed = [sums_ref[flux_start(face) : flux_start(face + 1)] for face in range(FACES)]
    flux = [flux_rows(sums, packed, face) for face in range(FACES)]
    gas = 0.0
    for face in range(FACES):
        hits = picks(near_ref, mask_ref, face, cell_start, cells).astype(BF16)
        gas += exact(flux[face], hits) - flux[face]
    for face, hits in enumerate(face_hits(face_ref, cells)):
        base = halo_rows(shared_refs, face, slice(0, SUMS))
        count = len(kept(face))
        own = halo_rows(shared_refs, face, slice(SUMS + NOTES, SUMS + NOTES + count))
        arrived = flux_rows(base, {face: own}, face)
        found = exact(arrived, hits.astype(BF16), ((1,), (1,)))
        gas += jnp.where(mask_ref[face : face + 1, :] != 1, found, 0.0)

    rows, returned = coefficients(sums, back_ref[...], TIME_STEP, 1.0)
    flows, cool, heats, gain, keep = rows[0:3], rows[3], rows[4:7], rows[7], rows[8]
    points = jnp.broadcast_to(point(lax.broadcasted_iota(jnp.int32, (NV, cells), 0)), (NV, cells))
    axes = []
    for flow in flows:
        off = points - flow
        bell = jnp.exp2(off * off * cool)
        axes.append([bell, bell * off, bell * off * off, bell * off * off * off])
    known = {}

    def along_axis(axis, order):
        if (axis, order) not in known:
            factor = power(points, order)
            known[axis, order] = [
                jnp.sum(term if factor is None else factor * term, axis=0, keepdims=True)
                for term in axes[axis]
            ]
        return known[axis, order]

    wall_bell = jnp.exp2(points * points * back_ref[6:7])
    above = jnp.maximum(points, 0.0)
    wall_sums = [jnp.sum(jnp.where(points > 0, wall_bell, 0.0), axis=0, keepdims=True)]
    for _ in range(4):
        wall_bell = wall_bell * above
        wall_sums.append(jnp.sum(wall_bell, axis=0, keepdims=True))

    def wall_full(order):
        if order in ("+", "-"):
            return wall_sums[1]
        return None if order % 2 else 2.0 * wall_sums[order]

    def wall_half(order, sign):
        if order in ("+", "-"):
            return wall_sums[2] if order == sign else None
        found = wall_sums[order + 1]
        return -found if order % 2 and sign == "-" else found

    found_rows = []
    for orders in ORDERS:
        bells, walls = 0.0, 0.0
        for order in orders:
            (x0, x1, x2, x3), (y0, y1, y2, y3), (z0, z1, z2, z3) = (
                along_axis(axis, order[axis]) for axis in range(3)
            )
            xy, xz, yz = x0 * y0, x0 * z0, y0 * z0
            skew = heats[0] * (x1 * (BEND * yz + cool * (y2 * z0 + y0 * z2)) + cool * x3 * yz)
            skew += heats[1] * (y1 * (BEND * xz + cool * (x2 * z0 + x0 * z2)) + cool * y3 * xz)
            skew += heats[2] * (z1 * (BEND * xy + cool * (x2 * y0 + x0 * y2)) + cool * z3 * xy)
            bells += xy * z0 + skew
            for face in range(FACES):
                terms = [
                    wall_half(order[axis], "+-"[face % 2])
                    if axis == face // 2
                    else wall_full(order[axis])
                    for axis in range(3)
                ]
                if all(term is not None for term in terms):
                    walls += returned[face : face + 1] * terms[0] * terms[1] * terms[2]
        found_rows.append(gain * bells + walls)
    found = WEIGHT * jnp.concatenate(found_rows, axis=0)
    out_ref[...] = found + keep * sums + TIME_STEP * gas


def halo_stream_kernel(face_ref, near_ref, *refs):
    halo_refs, (base_ref, from_y_ref, from_z_ref, values_ref) = refs[:-4], refs[-4:]
    rows, width = base_ref.shape
    count = rows // 2
    planes, upward = planes_y(2 * width)
    cell_start = lax.axis_index("space") * rows
    low = face_hits(face_ref, rows)[0]
    low_flipped, low = low.T.astype(BF16), low.astype(BF16)
    row = lax.broadcasted_iota(jnp.int32, (rows, rows), 0)
    steps = []
    for face in range(2, FACES):
        hits = jnp.where(row == near_ref[face : face + 1, :] - cell_start, 1.0, 0.0)
        from_rows = dot(low_flipped, hits.T.astype(BF16)).astype(BF16)
        steps.append(dot(from_rows, low))
    along_y = jnp.where(upward, steps[0], steps[1])
    picks_all = jnp.concatenate([along_y, steps[2], steps[3]], axis=0).astype(BF16)
    picks_all = jnp.concatenate([picks_all, picks_all], axis=1)
    for side in range(2):
        block = slice(side * count, (side + 1) * count)
        values_ref[block, :] = halo_rows(halo_refs, side)
        for start in range(0, width, COLUMN_TILE):
            lanes = slice(start, start + COLUMN_TILE)
            vel_x, vel_z = lane_points((1 - side) * HALF + start % HALF, COLUMN_TILE)
            vel_y = planes[start // HALF]
            values = values_ref[block, lanes]
            moved = dot(picks_all, jnp.concatenate(split(values, 2), axis=0))
            speed_x, speed_y, speed_z = jnp.abs(vel_x), jnp.abs(vel_y), jnp.abs(vel_z)
            from_z = jnp.where(vel_z > 0, moved[count : 2 * count], moved[2 * count :])
            from_y_ref[block, lanes] = (TIME_STEP * speed_y) * moved[:count]
            from_z_ref[block, lanes] = (TIME_STEP * speed_z) * from_z
            base_ref[block, lanes] = -TIME_STEP * (speed_x + speed_y + speed_z) * values


def halo_relax_kernel(base_ref, from_y_ref, from_z_ref, values_ref, *refs):
    shared_refs, (out_ref, open_ref, columns_ref) = refs[:-3], refs[-3:]
    rows, width = values_ref.shape
    _, upward = planes_y(2 * width)
    sums = shared_rows(shared_refs, 0, SUMS)
    notes = shared_rows(shared_refs, SUMS, SUMS + NOTES)
    back = jnp.where(notes[:FACES] == 1.0, notes[6:7], 0.0)
    passing = jnp.where(notes[:FACES] != 1.0, 1.0, 0.0)
    lane = lax.broadcasted_iota(jnp.int32, (1, rows), 1)
    more = [
        jnp.where(upward, passing[2:3], passing[3:4]),
        passing[4:6],
        notes[7:8],
        TIME_STEP * jnp.where(lane < rows // 2, passing[0:1], passing[1:2]),
    ]
    columns = columns_of(sums, back, 2 * width, TIME_STEP, 1.0, more)
    columns_ref[...] = columns
    open_ref[...] = jnp.broadcast_to(columns[:, 18:19], (rows, LANES))
    relax(columns_ref, base_ref, values_ref, None, out_ref, (from_y_ref, from_z_ref))


def second_kernel(
    face_ref, near_ref, mask_ref, sums_ref, back_ref, side_ref, dist_ref, stream_ref, shape_ref, *refs
):
    halo_refs, refs = refs[:-8], refs[-8:]
    middle_ref, part_ref, *plane_refs, columns_ref, base_ref = refs
    middle_kernel(
        sums_ref,
        back_ref,
        side_ref,
        dist_ref,
        stream_ref,
        shape_ref,
        *halo_refs,
        middle_ref,
        columns_ref,
        base_ref,
    )
    stream_last_kernel(near_ref, mask_ref, dist_ref, middle_ref, part_ref)
    halo_stream_kernel(face_ref, near_ref, *halo_refs, *plane_refs)


def third_kernel(face_ref, near_ref, mask_ref, sums_ref, back_ref, shape_ref, *refs):
    middle_ref, part_ref, *plane_refs = refs[:6]
    shared_refs, (out_ref, plane_ref, open_ref, next_ref, columns_ref) = refs[6:-5], refs[-5:]
    advance_kernel(face_ref, near_ref, mask_ref, sums_ref, back_ref, *shared_refs, next_ref)
    relax_kernel(next_ref, back_ref, middle_ref, part_ref, shape_ref, out_ref, columns_ref)
    halo_relax_kernel(*plane_refs, *shared_refs, plane_ref, open_ref, columns_ref)


def last_kernel(side_ref, part_ref, plane_ref, open_ref, *refs):
    refs, (out_ref, result_ref, sems) = refs[:-3], refs[-3:]
    cells, width = part_ref.shape
    count = cells // 2
    copies = []
    for part, (start, stop) in enumerate(far_parts(width // 2)):
        halo_refs = refs[part * len(refs) // 2 : (part + 1) * len(refs) // 2]
        for side, tiles in enumerate(half_tiles(start, stop, COLUMN_TILE)):
            pick = side_ref[side * cells : (side + 1) * cells, :]
            block = slice((1 - side) * count, (2 - side) * count)
            for source, target, size in tiles:
                lanes = slice(source, source + size)
                gate = jnp.concatenate([open_ref[block]] * (size // LANES), axis=1)
                speed_x = jnp.abs(lane_points(source, size)[0])
                rows = halo_rows(halo_refs, 1 - side)[:, target - start : target - start + size]
                rows = plane_ref[block, target : target + size] + gate * speed_x * rows
                halo = dot(pick, jnp.concatenate(split(rows, 2), axis=0))
                result_ref[:, lanes] = part_ref[:, lanes] + (0.5 * TIME_STEP * speed_x) * halo
                copy = pltpu.make_async_copy(
                    result_ref.at[:, lanes], out_ref.at[:, lanes], sems.at[len(copies)]
                )
                copy.start()
                copies.append(copy)
    for copy in copies:
        copy.wait()


def call(kernel, outs, arrays, scratch=(), scalars=0, far_outs=False, unread=(), aliases=None):
    spaces = [
        pltpu.SMEM if at < scalars else pl.ANY if at in unread else pltpu.VMEM
        for at in range(len(arrays))
    ]
    name = kernel.__name__
    size = sum(math.prod(array.shape) * 4 for array in arrays)
    return pl.pallas_call(
        kernel,
        out_shape=[jax.ShapeDtypeStruct(shape, dtype) for shape, dtype in outs],
        in_specs=[pl.BlockSpec(memory_space=space) for space in spaces],
        out_specs=[pl.BlockSpec(memory_space=pl.ANY if far_outs else pltpu.VMEM)] * len(outs),
        scratch_shapes=list(scratch),
        input_output_aliases=aliases or {},
        name=name,
        compiler_params=pltpu.CompilerParams(vmem_limit_bytes=40 * 2**20),
        cost_estimate=pl.CostEstimate(
            flops=COST.get(name, 0), bytes_accessed=size, transcendentals=0
        ),
    )(*arrays)


COST = {"third_kernel": 2 * 10**9, "second_kernel": 10**9}


def passed(value, after):
    return call(
        pass_kernel,
        [(value.shape, value.dtype)],
        [value, after],
        far_outs=True,
        unread=(0, 1),
        aliases={0: 0},
    )[0]


def total(value):
    count = lax.axis_size("vel")
    step = 1
    while step < count:
        value = value + lax.ppermute(value, "vel", [(i, i ^ step) for i in range(count)])
        step *= 2
    return value


def exchange(send):
    count = lax.axis_size("space")
    forward = [(i, (i + 1) % count) for i in range(count)]
    backward = [(target, source) for source, target in forward]
    if count == 2:
        return [lax.ppermute(send, "space", forward)]
    half = send.shape[0] // 2
    return [
        lax.ppermute(send[:half], "space", forward),
        lax.ppermute(send[half:], "space", backward),
    ]


def on_device(dist, wall_temp, neighbours, wall_mask, face_rows):
    cells, width = dist.shape
    count, half = cells // 2, width // 2
    temp = wall_temp[None, :]
    whole, plane = ((cells, width), F32), ((cells, half), F32)
    every = flux_start(FACES)
    columns = pltpu.VMEM((cells, LANES), F32)

    dist, sent = call(
        near_plane_kernel,
        [whole, plane],
        [
            pltpu.with_memory_space_constraint(face_rows, pltpu.HBM),
            pltpu.with_memory_space_constraint(dist, pltpu.HBM),
        ],
        [
            pltpu.SMEM(face_rows.shape, jnp.int32),
            pltpu.SemaphoreType.DMA(()),
            pltpu.SemaphoreType.DMA((width // HALF,)),
        ],
        unread=(0, 1),
    )
    near = exchange(sent)
    (sums,) = call(sums_kernel, [((every, cells), F32)], [dist])
    shape, back, side, notes = call(
        wall_kernel,
        [whole, ((8, cells), F32), ((2 * cells, cells), BF16), ((NOTES, cells), F32)],
        [face_rows, temp, wall_mask],
    )
    (stream,) = call(stream_kernel, [whole], [neighbours, wall_mask, dist])
    sums = total(sums)
    (sent,) = call(
        share_kernel,
        [((2 * (2 * SUMS + NOTES), count), F32)],
        [face_rows, sums, notes],
    )
    shared = exchange(sent)
    far_shapes = [((cells, stop - start), F32) for start, stop in far_parts(half)]
    far_rows = call(far_plane_kernel, far_shapes, [face_rows, dist], scalars=1)
    far = [exchange(far_rows[0]), exchange(passed(far_rows[1], sent))]
    middle, part, *planes = call(
        second_kernel,
        [whole, whole, plane, plane, plane, plane],
        [face_rows, neighbours, wall_mask, sums, back, side, dist, stream, shape, *near],
        [columns, pltpu.VMEM((cells, width), F32)],
    )
    part, plane_one, gate = call(
        third_kernel,
        [whole, plane, ((cells, LANES), F32)],
        [face_rows, neighbours, wall_mask, sums, back, shape, middle, part, *planes, *shared],
        [pltpu.VMEM((SUMS, cells), F32), columns],
    )
    (result,) = call(
        last_kernel,
        [whole],
        [side, part, plane_one, gate, *far[0], *far[1]],
        [pltpu.VMEM((cells, width), F32), pltpu.SemaphoreType.DMA((width // LANES,))],
        far_outs=True,
    )
    return result


def solution(mesh):
    return jax.shard_map(
        on_device,
        mesh=mesh,
        in_specs=(
            P("space", "vel"),
            P("space"),
            P(None, "space"),
            P(None, "space"),
            P("space", None, None),
        ),
        out_specs=P("space", "vel"),
        check_vma=False,
    )
```

```python
import functools
import math

import jax
import jax.numpy as jnp
from jax import lax
from jax.experimental import pallas as pl
from jax.experimental.pallas import tpu as pltpu
from jax.sharding import PartitionSpec as P

NV = 32
LIMIT = 4.5
SPACING = 2.0 * LIMIT / NV
WEIGHT = SPACING**3 * (2.0 * math.pi) ** (-1.5)
TIME_STEP = 0.05
BASELINE_SHEAR = 0.1
SHEAR_EXPONENT = 0.66
MOMENTUM_RATIO = 2.0 / 3.0
PLANE = NV * NV
HALF = PLANE // 2
ROWS = 8
LANES = 128
COLUMN_TILE = 256
SUMS = 16
FACES = 6
NOTES = 8
PARTS = 2
BEND = 2.5 * math.log2(math.e)
LOG2E = math.log2(math.e)
F32 = jnp.float32
BF16 = jnp.bfloat16


def point(slot):
    return -LIMIT + (slot.astype(F32) + 0.5) * SPACING


def lane_points(start, width):
    lane = lax.broadcasted_iota(jnp.int32, (1, width), 1) + start
    return point((lane >> 5) & (NV - 1)), point(lane & (NV - 1))


def planes_y(width):
    planes = width // PLANE
    first = lax.axis_index("vel") * planes
    return [point(first + at) for at in range(planes)], first >= NV // 2


def split(value, count):
    pieces = []
    for _ in range(count - 1):
        piece = value.astype(BF16)
        pieces.append(piece)
        value = value - piece.astype(F32)
    pieces.append(value.astype(BF16))
    return pieces


def dot(left, right, dims=((1,), (0,))):
    return lax.dot_general(left, right, (dims, ((), ())), preferred_element_type=F32)


def kept(face):
    other = face ^ 1
    return [*range(1, 10)] + [
        10 + out for out in range(FACES) if out == other or out // 2 > other // 2
    ]


def flux_start(face):
    return SUMS + sum(len(kept(before)) for before in range(face))


def flux_rows(base, packed, face):
    other = face ^ 1
    mine = packed[face]
    rows = [base[10 + other : 11 + other], mine[:9]]
    for out in range(FACES):
        if out == face:
            rows.append(jnp.zeros_like(mine[:1]))
            continue
        holder, row = (face, 10 + out) if 10 + out in kept(face) else (out ^ 1, 10 + other)
        at = kept(holder).index(row)
        rows.append(packed[holder][at : at + 1])
    return jnp.concatenate(rows, axis=0)


def exact(left, right, dims=((1,), (0,))):
    rows = left.shape[0]
    found = dot(jnp.concatenate(split(left, 3), axis=0), right, dims)
    return found[:rows] + found[rows : 2 * rows] + found[2 * rows :]


def inward(vel_x, vel_y, vel_z):
    return [
        jnp.maximum(sign * vel, 0.0) for vel in (vel_x, vel_y, vel_z) for sign in (1.0, -1.0)
    ]


def weights(vel_x, vel_y, vel_z):
    speed_sq = vel_x * vel_x + vel_y * vel_y + vel_z * vel_z
    into = inward(vel_x, vel_y, vel_z)
    rows = [
        jnp.ones_like(vel_x),
        vel_x * vel_x,
        vel_y * vel_y,
        vel_z * vel_z,
        vel_x * vel_y,
        vel_x * vel_z,
        vel_y * vel_z,
        vel_x * speed_sq,
        vel_y * speed_sq,
        vel_z * speed_sq,
        into[1],
        into[0],
        into[3],
        into[2],
        into[5],
        into[4],
    ]
    return WEIGHT * jnp.concatenate(rows, axis=0), into


def face_hits(face_ref, cells):
    row = lax.broadcasted_iota(jnp.int32, (cells, face_ref.shape[2]), 0)
    return [jnp.where(row == face_ref[0, side : side + 1, :], 1.0, 0.0) for side in range(2)]


def sums_kernel(dist_ref, sums_ref):
    width = dist_ref.shape[1]
    planes, _ = planes_y(width)
    total = None
    for start in range(0, width, HALF):
        lanes = slice(start, start + HALF)
        vel_x, vel_z = lane_points(start, HALF)
        vel_y = jnp.full((1, HALF), planes[start // PLANE])
        base, into = weights(vel_x, vel_y, vel_z)
        table = [base]
        for face, speed in enumerate(into):
            fluxes = base * speed
            table.append(fluxes[1:10])
            table += [fluxes[row : row + 1] for row in kept(face)[9:]]
        table = jnp.concatenate(table, axis=0)
        coarse, fine = split(table, 2)
        finest = split(base, 3)[2]
        pieces = split(dist_ref[:, lanes], 3)
        across = ((1,), (1,))
        one = dot(jnp.concatenate([coarse, fine, finest], axis=0), pieces[0], across)
        two = dot(jnp.concatenate([coarse, fine], axis=0), pieces[1], across)
        three = dot(coarse, pieces[2], across)
        rows = table.shape[0]
        part = one[:rows] + one[rows : 2 * rows] + two[:rows] + two[rows:] + three
        part = jnp.concatenate([part[:SUMS] + one[2 * rows :], part[SUMS:]], axis=0)
        total = part if total is None else total + part
    sums_ref[...] = total


def share_kernel(face_ref, sums_ref, notes_ref, _, send_ref):
    low, high = face_hits(face_ref, sums_ref.shape[1])
    for side, hits in ((0, high), (1, low)):
        rows = [sums_ref[:SUMS], notes_ref[...], sums_ref[flux_start(side) : flux_start(side + 1)]]
        rows = exact(jnp.concatenate(rows, axis=0), hits.astype(BF16))
        first = side * (send_ref.shape[0] // 2)
        send_ref[first : first + rows.shape[0], :] = rows


def halo_rows(refs, side, rows=slice(None)):
    if len(refs) == 2:
        return refs[side][rows]
    half = refs[0].shape[0] // 2
    start, stop, _ = rows.indices(half)
    return refs[0][side * half + start : side * half + stop]


def shared_rows(refs, start, stop):
    rows = slice(start, stop)
    return jnp.concatenate([halo_rows(refs, 0, rows), halo_rows(refs, 1, rows)], axis=1)


def half_tiles(width, part=0, parts=1):
    half = width // 2
    lanes = range(part * half // parts, (part + 1) * half // parts, COLUMN_TILE)
    low = [(lane // HALF * PLANE + lane % HALF, lane) for lane in lanes]
    return low, [(source + HALF, target) for source, target in low]


def gathered(rows_ref, plane, group, value_ref, source, size):
    below = lax.broadcasted_iota(jnp.int32, (ROWS, size), 0)
    found = None
    for at in range(ROWS):
        row = value_ref[pl.ds(rows_ref[0, plane, group + at], 1), source : source + size]
        row = jnp.broadcast_to(row, (ROWS, size))
        found = row if found is None else jnp.where(below == at, row, found)
    return found


def move_rows(rows_ref, value_ref, send_ref, part):
    cells, width = value_ref.shape
    count = cells // 2
    low, high = half_tiles(width, part, PARTS)
    begin = low[0][1]
    piece = min(HALF, send_ref.shape[1])
    step = piece // COLUMN_TILE

    for first, tiles, plane in ((0, high, 0), (count, low, 1)):
        for source, target in tiles[::step]:
            for group in range(0, count, ROWS):
                rows = slice(first + group, first + group + ROWS)
                send_ref[rows, target - begin : target - begin + piece] = gathered(
                    rows_ref, plane, group, value_ref, source, piece
                )


def wall_rows(temp_ref):
    cooling = (-0.5 * LOG2E) / temp_ref[...]
    axis_point = point(lax.broadcasted_iota(jnp.int32, (NV, 1), 0))
    profile = jnp.exp2(axis_point * axis_point * cooling)
    mass = jnp.sum(profile, axis=0, keepdims=True)
    flux = jnp.sum(jnp.maximum(axis_point, 0.0) * profile, axis=0, keepdims=True)
    return 1.0 / (WEIGHT * flux * mass * mass), cooling


def near_plane_kernel(face_ref, dist_ref, own_ref, send_ref, rows_ref, row_sem, sems):
    cells, width = dist_ref.shape
    count = cells // 2
    rows_copy = pltpu.make_async_copy(face_ref, rows_ref, row_sem)
    rows_copy.start()
    copies = []
    for start in range(0, width, HALF):
        lanes = slice(start, start + HALF)
        copy = pltpu.make_async_copy(
            dist_ref.at[:, lanes], own_ref.at[:, lanes], sems.at[len(copies)]
        )
        copy.start()
        copies.append(copy)
    rows_copy.wait()
    for at, copy in enumerate(copies):
        copy.wait()
        side = at % 2
        source, target, first = at * HALF, at // 2 * HALF, (1 - side) * count

        for group in range(0, count, ROWS):
            send_ref[first + group : first + group + ROWS, target : target + HALF] = gathered(
                rows_ref, side, group, own_ref, source, HALF
            )


def far_plane_kernel(rows_ref, dist_ref, *send_refs):
    for part, send_ref in enumerate(send_refs):
        move_rows(rows_ref, dist_ref, send_ref, part)


def pass_kernel(value_ref, after_ref, out_ref):
    pass


def picks(near_ref, mask_ref, face, cell_start, cells):
    index = near_ref[face : face + 1, :] - cell_start
    hit = lax.broadcasted_iota(jnp.int32, (cells, cells), 0) == index
    open_face = mask_ref[face : face + 1, :] != 1
    return jnp.where(hit & open_face, 1.0, 0.0).astype(F32)


def along(near_ref, mask_ref, upward):
    cells = near_ref.shape[1]
    cell_start = lax.axis_index("space") * cells
    faces = [picks(near_ref, mask_ref, face, cell_start, cells) for face in range(6)]
    return [faces[0], faces[1], jnp.where(upward, faces[2], faces[3]), faces[4], faces[5]]


def stream_tiles(near_ref, mask_ref, value_ref, store):
    cells, width = value_ref.shape
    planes, upward = planes_y(width)
    chosen = []
    for face in along(near_ref, mask_ref, upward):
        flipped = face.T.astype(BF16)
        chosen.append(jnp.concatenate([flipped, flipped], axis=1))
    rest = jnp.concatenate(chosen[2:], axis=0)
    for start in range(0, width, COLUMN_TILE):
        side = chosen[0] if start % PLANE >= HALF else chosen[1]
        vel_x, vel_z = lane_points(start, COLUMN_TILE)
        values = value_ref[:, start : start + COLUMN_TILE]
        pieces = jnp.concatenate(split(values, 2), axis=0)
        moved = dot(jnp.concatenate([side, rest], axis=0), pieces)
        speed_x, speed_z = jnp.abs(vel_x), jnp.abs(vel_z)
        speed_y = jnp.abs(planes[start // PLANE])
        from_z = jnp.where(vel_z > 0, moved[2 * cells : 3 * cells], moved[3 * cells :])
        stream = (
            speed_x * moved[:cells]
            + speed_y * moved[cells : 2 * cells]
            + speed_z * from_z
            - (speed_x + speed_y + speed_z) * values
        )
        store(slice(start, start + COLUMN_TILE), values, stream)


def stream_kernel(near_ref, mask_ref, value_ref, out_ref):
    def store(lanes, values, stream):
        out_ref[:, lanes] = TIME_STEP * stream

    stream_tiles(near_ref, mask_ref, value_ref, store)


def stream_last_kernel(near_ref, mask_ref, dist_ref, middle_ref, out_ref):
    def store(lanes, values, stream):
        out_ref[:, lanes] = 0.5 * (dist_ref[:, lanes] + values) + (0.5 * TIME_STEP) * stream

    stream_tiles(near_ref, mask_ref, middle_ref, store)


def wall_kernel(face_ref, temp_ref, mask_ref, shape_ref, back_ref, side_ref, notes_ref):
    cells, width = shape_ref.shape
    count = cells // 2
    planes, _ = planes_y(width)
    inv_norm, cooling = wall_rows(temp_ref)
    mask = mask_ref[...]
    notes_ref[...] = jnp.concatenate([mask.astype(F32), inv_norm, cooling], axis=0)
    back_ref[...] = jnp.concatenate(
        [jnp.where(mask == 1, inv_norm, 0.0), cooling, jnp.zeros((1, cells), F32)],
        axis=0,
    )
    rows = [mask[:2].astype(F32), cooling, jnp.zeros((LANES - 3, cells), F32)]
    columns = jnp.concatenate(rows, axis=0).T
    row = lax.broadcasted_iota(jnp.int32, (cells, count), 0)
    for side, face in enumerate((1, 0)):
        hit = (row == face_ref[0, face : face + 1, :]) & (columns[:, face : face + 1] != 1.0)
        picked = jnp.where(hit, 1.0, 0.0).astype(BF16)
        side_ref[side * cells : (side + 1) * cells, :] = jnp.concatenate([picked, picked], axis=1)
    cooling = jnp.broadcast_to(columns[:, 2:3], (cells, LANES))
    for start in range(0, PLANE, LANES):
        vel_x, vel_z = lane_points(start, LANES)
        flat = vel_x * vel_x + vel_z * vel_z
        for at, vel_y in enumerate(planes):
            lanes = slice(at * PLANE + start, at * PLANE + start + LANES)
            shape_ref[:, lanes] = jnp.exp2((flat + vel_y * vel_y) * cooling)


def coefficients(sums, back, step, keep):
    count = sums[0:1]
    inv_count = 1.0 / count
    flow_x = (sums[11:12] - sums[10:11]) * inv_count
    flow_y = (sums[13:14] - sums[12:13]) * inv_count
    flow_z = (sums[15:16] - sums[14:15]) * inv_count
    p_xx, p_yy, p_zz, p_xy, p_xz, p_yz = (sums[at : at + 1] for at in range(1, 7))
    energy = p_xx + p_yy + p_zz
    flow_sq = flow_x * flow_x + flow_y * flow_y + flow_z * flow_z
    temp = (energy * inv_count - flow_sq) / 3.0
    inv_temp = 1.0 / temp

    def heat(third, flow, press):
        return 0.5 * (
            third
            - 2.0 * (press[0] * flow_x + press[1] * flow_y + press[2] * flow_z)
            - flow * energy
            + 2.0 * count * flow * flow_sq
        )

    scale = ((1.0 - MOMENTUM_RATIO) / 5.0) * inv_count * inv_temp * inv_temp * (-2.0 / LOG2E)
    rate = (count * jnp.exp((1.0 - SHEAR_EXPONENT) * jnp.log(temp))) * (step / BASELINE_SHEAR)
    returned = (back[0:6] * step) * sums[10:16]
    rows = [
        flow_x,
        flow_y,
        flow_z,
        (-0.5 * LOG2E) * inv_temp,
        scale * heat(sums[7:8], flow_x, (p_xx, p_xy, p_xz)),
        scale * heat(sums[8:9], flow_y, (p_xy, p_yy, p_yz)),
        scale * heat(sums[9:10], flow_z, (p_xz, p_yz, p_zz)),
        count * inv_temp * lax.rsqrt(temp) * rate,
        keep - rate,
    ]
    return rows, returned


def columns_of(sums, back, width, step, keep, more=()):
    _, upward = planes_y(width)
    rows, returned = coefficients(sums, back, step, keep)
    rows += [
        jnp.where(upward, returned[2:3], returned[3:4]),
        returned[0:2],
        returned[4:6],
        *more,
        jnp.zeros((LANES - 14 - sum(row.shape[0] for row in more), sums.shape[1]), F32),
    ]
    return jnp.concatenate(rows, axis=0).T


def relax(columns_ref, base_ref, value_ref, shape_ref, out_ref, planes_refs=None):
    cells, width = value_ref.shape
    half = planes_refs is not None
    planes, _ = planes_y(2 * width if half else width)
    lane = lax.broadcasted_iota(jnp.int32, (ROWS, LANES), 1)
    first_x, vel_z = point((lane >> 5) & (NV - 1)), point(lane & (NV - 1))
    z_plus, z_minus = jnp.maximum(vel_z, 0.0), jnp.maximum(-vel_z, 0.0)

    def group(at, _, tiles=range(PLANE // LANES), stride=PLANE):
        rows = pl.ds(pl.multiple_of(at * ROWS, ROWS), ROWS)
        columns = columns_ref[rows, :]
        flow_x, flow_y, flow_z, cool, heat_x, heat_y, heat_z, gain, keep, back_y, *back = (
            jnp.broadcast_to(columns[:, column : column + 1], (ROWS, LANES))
            for column in range(18 if half else 14)
        )
        if half:
            open_y, open_low, open_high, cooling = back[4:]
            open_z = jnp.where(vel_z > 0, open_low, open_high)
        rel_z = vel_z - flow_z
        square_z = rel_z * rel_z * cool
        heat_of_z = rel_z * heat_z
        back_z = z_plus * back[2] + z_minus * back[3]
        of_y = []
        for vel_y in planes:
            rel_y = vel_y - flow_y
            of_y.append((rel_y * rel_y * cool, rel_y * heat_y, jnp.abs(vel_y) * back_y))
        for tile in tiles:
            vel_x = first_x + (tile * (LANES // NV)) * SPACING
            rel_x = vel_x - flow_x
            square_xz = rel_x * rel_x * cool + square_z
            heat_xz = rel_x * heat_x + heat_of_z
            upper = tile * LANES >= HALF
            back_xz = jnp.abs(vel_x) * (back[0] if upper else back[1]) + back_z
            for plane, (square_y, heat_of_y, back_of_y) in enumerate(of_y):
                start = plane * stride + (tile - tiles[0]) * LANES
                lanes = slice(start, start + LANES)
                square = square_xz + square_y
                skew = (heat_xz + heat_of_y) * (square + 2.5 * LOG2E) + 1.0
                base = base_ref[rows, lanes]
                if half:
                    from_y_ref, from_z_ref = planes_refs
                    base += open_y * from_y_ref[rows, lanes] + open_z * from_z_ref[rows, lanes]
                    speed_sq = vel_x * vel_x + vel_z * vel_z + planes[plane] * planes[plane]
                    shape = jnp.exp2(speed_sq * cooling)
                else:
                    shape = shape_ref[rows, lanes]
                out_ref[rows, lanes] = (
                    base
                    + keep * value_ref[rows, lanes]
                    + gain * jnp.exp2(square) * skew
                    + shape * (back_xz + back_of_y)
                )
        return 0

    groups = cells // ROWS
    if half:
        low, high = range(HALF // LANES), range(HALF // LANES, PLANE // LANES)
        lax.fori_loop(
            0, groups // 2, functools.partial(group, tiles=high, stride=HALF), 0, unroll=True
        )
        lax.fori_loop(
            groups // 2, groups, functools.partial(group, tiles=low, stride=HALF), 0, unroll=True
        )
    else:
        lax.fori_loop(0, groups, group, 0, unroll=True)


def middle_kernel(sums_ref, back_ref, side_ref, own_ref, stream_ref, shape_ref, *refs):
    halo_refs, (out_ref, columns_ref, base_ref) = refs[:-3], refs[-3:]
    cells, width = own_ref.shape
    columns_ref[...] = columns_of(sums_ref[:SUMS], back_ref[...], width, TIME_STEP, 1.0)
    for side, tiles in enumerate(half_tiles(width)):
        pick = side_ref[side * cells : (side + 1) * cells, :]
        for source, target in tiles:
            lanes = slice(source, source + COLUMN_TILE)
            vel_x, _ = lane_points(source, COLUMN_TILE)
            rows = halo_rows(halo_refs, 1 - side)[:, target : target + COLUMN_TILE]
            halo = dot(pick, jnp.concatenate(split(rows, 2), axis=0))
            base_ref[:, lanes] = stream_ref[:, lanes] + (TIME_STEP * jnp.abs(vel_x)) * halo
    relax(columns_ref, base_ref, own_ref, shape_ref, out_ref)


def relax_kernel(sums_ref, back_ref, middle_ref, part_ref, shape_ref, out_ref, columns_ref):
    width = middle_ref.shape[1]
    step = 0.5 * TIME_STEP
    columns_ref[...] = columns_of(sums_ref[...], back_ref[...], width, step, 0.0)
    relax(columns_ref, part_ref, middle_ref, shape_ref, out_ref)


ORDERS = (
    [(0, 0, 0)],
    [(2, 0, 0)],
    [(0, 2, 0)],
    [(0, 0, 2)],
    [(1, 1, 0)],
    [(1, 0, 1)],
    [(0, 1, 1)],
    [(3, 0, 0), (1, 2, 0), (1, 0, 2)],
    [(0, 3, 0), (2, 1, 0), (0, 1, 2)],
    [(0, 0, 3), (2, 0, 1), (0, 2, 1)],
    [("-", 0, 0)],
    [("+", 0, 0)],
    [(0, "-", 0)],
    [(0, "+", 0)],
    [(0, 0, "-")],
    [(0, 0, "+")],
)


def power(value, order):
    if order == "+":
        return jnp.maximum(value, 0.0)
    if order == "-":
        return jnp.maximum(-value, 0.0)
    result = None
    for _ in range(order):
        result = value if result is None else result * value
    return result


def advance_kernel(face_ref, near_ref, _, __, mask_ref, sums_ref, back_ref, *refs):
    shared_refs, out_ref = refs[:-1], refs[-1]
    cells = near_ref.shape[1]
    cell_start = lax.axis_index("space") * cells
    sums = sums_ref[:SUMS]
    packed = [sums_ref[flux_start(face) : flux_start(face + 1)] for face in range(FACES)]
    flux = [flux_rows(sums, packed, face) for face in range(FACES)]
    gas = 0.0
    for face in range(FACES):
        hits = picks(near_ref, mask_ref, face, cell_start, cells).astype(BF16)
        gas += exact(flux[face], hits) - flux[face]
    for face, hits in enumerate(face_hits(face_ref, cells)):
        base = halo_rows(shared_refs, face, slice(0, SUMS))
        count = len(kept(face))
        own = halo_rows(shared_refs, face, slice(SUMS + NOTES, SUMS + NOTES + count))
        arrived = flux_rows(base, {face: own}, face)
        found = exact(arrived, hits.astype(BF16), ((1,), (1,)))
        gas += jnp.where(mask_ref[face : face + 1, :] != 1, found, 0.0)

    rows, returned = coefficients(sums, back_ref[...], TIME_STEP, 1.0)
    flows, cool, heats, gain, keep = rows[0:3], rows[3], rows[4:7], rows[7], rows[8]
    points = jnp.broadcast_to(point(lax.broadcasted_iota(jnp.int32, (NV, cells), 0)), (NV, cells))
    axes = []
    for flow in flows:
        off = points - flow
        bell = jnp.exp2(off * off * cool)
        axes.append([bell, bell * off, bell * off * off, bell * off * off * off])
    known = {}

    def along_axis(axis, order):
        if (axis, order) not in known:
            factor = power(points, order)
            known[axis, order] = [
                jnp.sum(term if factor is None else factor * term, axis=0, keepdims=True)
                for term in axes[axis]
            ]
        return known[axis, order]

    wall_bell = jnp.exp2(points * points * back_ref[6:7])
    above = jnp.maximum(points, 0.0)
    wall_sums = [jnp.sum(jnp.where(points > 0, wall_bell, 0.0), axis=0, keepdims=True)]
    for _ in range(4):
        wall_bell = wall_bell * above
        wall_sums.append(jnp.sum(wall_bell, axis=0, keepdims=True))

    def wall_full(order):
        if order in ("+", "-"):
            return wall_sums[1]
        return None if order % 2 else 2.0 * wall_sums[order]

    def wall_half(order, sign):
        if order in ("+", "-"):
            return wall_sums[2] if order == sign else None
        found = wall_sums[order + 1]
        return -found if order % 2 and sign == "-" else found

    found_rows = []
    for orders in ORDERS:
        bells, walls = 0.0, 0.0
        for order in orders:
            (x0, x1, x2, x3), (y0, y1, y2, y3), (z0, z1, z2, z3) = (
                along_axis(axis, order[axis]) for axis in range(3)
            )
            xy, xz, yz = x0 * y0, x0 * z0, y0 * z0
            skew = heats[0] * (x1 * (BEND * yz + cool * (y2 * z0 + y0 * z2)) + cool * x3 * yz)
            skew += heats[1] * (y1 * (BEND * xz + cool * (x2 * z0 + x0 * z2)) + cool * y3 * xz)
            skew += heats[2] * (z1 * (BEND * xy + cool * (x2 * y0 + x0 * y2)) + cool * z3 * xy)
            bells += xy * z0 + skew
            for face in range(FACES):
                terms = [
                    wall_half(order[axis], "+-"[face % 2])
                    if axis == face // 2
                    else wall_full(order[axis])
                    for axis in range(3)
                ]
                if all(term is not None for term in terms):
                    walls += returned[face : face + 1] * terms[0] * terms[1] * terms[2]
        found_rows.append(gain * bells + walls)
    found = WEIGHT * jnp.concatenate(found_rows, axis=0)
    out_ref[...] = found + keep * sums + TIME_STEP * gas


def halo_stream_kernel(face_ref, near_ref, *refs):
    halo_refs, (base_ref, from_y_ref, from_z_ref, values_ref) = refs[:-4], refs[-4:]
    rows, width = base_ref.shape
    count = rows // 2
    planes, upward = planes_y(2 * width)
    cell_start = lax.axis_index("space") * rows
    low = face_hits(face_ref, rows)[0]
    low_flipped, low = low.T.astype(BF16), low.astype(BF16)
    row = lax.broadcasted_iota(jnp.int32, (rows, rows), 0)
    steps = []
    for face in range(2, FACES):
        hits = jnp.where(row == near_ref[face : face + 1, :] - cell_start, 1.0, 0.0)
        from_rows = dot(low_flipped, hits.T.astype(BF16)).astype(BF16)
        steps.append(dot(from_rows, low))
    along_y = jnp.where(upward, steps[0], steps[1])
    picks_all = jnp.concatenate([along_y, steps[2], steps[3]], axis=0).astype(BF16)
    picks_all = jnp.concatenate([picks_all, picks_all], axis=1)
    for side in range(2):
        block = slice(side * count, (side + 1) * count)
        values_ref[block, :] = halo_rows(halo_refs, side)
        for start in range(0, width, COLUMN_TILE):
            lanes = slice(start, start + COLUMN_TILE)
            vel_x, vel_z = lane_points((1 - side) * HALF + start % HALF, COLUMN_TILE)
            vel_y = planes[start // HALF]
            values = values_ref[block, lanes]
            moved = dot(picks_all, jnp.concatenate(split(values, 2), axis=0))
            speed_x, speed_y, speed_z = jnp.abs(vel_x), jnp.abs(vel_y), jnp.abs(vel_z)
            from_z = jnp.where(vel_z > 0, moved[count : 2 * count], moved[2 * count :])
            from_y_ref[block, lanes] = (TIME_STEP * speed_y) * moved[:count]
            from_z_ref[block, lanes] = (TIME_STEP * speed_z) * from_z
            base_ref[block, lanes] = -TIME_STEP * (speed_x + speed_y + speed_z) * values


def halo_relax_kernel(base_ref, from_y_ref, from_z_ref, values_ref, *refs):
    shared_refs, (out_ref, open_ref, columns_ref) = refs[:-3], refs[-3:]
    rows, width = values_ref.shape
    _, upward = planes_y(2 * width)
    sums = shared_rows(shared_refs, 0, SUMS)
    notes = shared_rows(shared_refs, SUMS, SUMS + NOTES)
    back = jnp.where(notes[:FACES] == 1.0, notes[6:7], 0.0)
    passing = jnp.where(notes[:FACES] != 1.0, 1.0, 0.0)
    lane = lax.broadcasted_iota(jnp.int32, (1, rows), 1)
    more = [
        jnp.where(upward, passing[2:3], passing[3:4]),
        passing[4:6],
        notes[7:8],
        TIME_STEP * jnp.where(lane < rows // 2, passing[0:1], passing[1:2]),
    ]
    columns = columns_of(sums, back, 2 * width, TIME_STEP, 1.0, more)
    columns_ref[...] = columns
    open_ref[...] = jnp.broadcast_to(columns[:, 18:19], (rows, LANES))
    relax(columns_ref, base_ref, values_ref, None, out_ref, (from_y_ref, from_z_ref))


def last_kernel(part, side_ref, part_ref, plane_ref, open_ref, *refs):
    refs, (out_ref, result_ref, sems) = refs[:-3], refs[-3:]
    halo_refs = refs[part > 0 :]
    cells, width = part_ref.shape
    count = cells // 2
    copies = []
    for side, tiles in enumerate(half_tiles(width, part, PARTS)):
        pick = side_ref[side * cells : (side + 1) * cells, :]
        block = slice((1 - side) * count, (2 - side) * count)
        gate = jnp.concatenate([open_ref[block]] * (COLUMN_TILE // LANES), axis=1)
        begin = tiles[0][1]
        for source, target in tiles:
            lanes = slice(source, source + COLUMN_TILE)
            speed_x = jnp.abs(lane_points(source, COLUMN_TILE)[0])
            rows = halo_rows(halo_refs, 1 - side)[:, target - begin : target - begin + COLUMN_TILE]
            rows = plane_ref[block, target : target + COLUMN_TILE] + gate * speed_x * rows
            halo = dot(pick, jnp.concatenate(split(rows, 2), axis=0))
            result_ref[:, lanes] = part_ref[:, lanes] + (0.5 * TIME_STEP * speed_x) * halo
            copy = pltpu.make_async_copy(
                result_ref.at[:, lanes], out_ref.at[:, lanes], sems.at[len(copies)]
            )
            copy.start()
            copies.append(copy)
    for copy in copies:
        copy.wait()


def call(kernel, outs, arrays, scratch=(), scalars=0, far_outs=False, unread=(), aliases=None):
    spaces = [
        pltpu.SMEM if at < scalars else pl.ANY if at in unread else pltpu.VMEM
        for at in range(len(arrays))
    ]
    if isinstance(kernel, functools.partial):
        name = f"{kernel.func.__name__}_{kernel.args[0]}"
    else:
        name = kernel.__name__
    size = sum(math.prod(array.shape) * 4 for array in arrays)
    return pl.pallas_call(
        kernel,
        out_shape=[jax.ShapeDtypeStruct(shape, dtype) for shape, dtype in outs],
        in_specs=[pl.BlockSpec(memory_space=space) for space in spaces],
        out_specs=[pl.BlockSpec(memory_space=pl.ANY if far_outs else pltpu.VMEM)] * len(outs),
        scratch_shapes=list(scratch),
        input_output_aliases=aliases or {},
        name=name,
        compiler_params=pltpu.CompilerParams(vmem_limit_bytes=40 * 2**20),
        cost_estimate=pl.CostEstimate(
            flops=COST.get(name, 0), bytes_accessed=size, transcendentals=0
        ),
    )(*arrays)


COST = {"advance_kernel": 14 * 10**8, "last_kernel_0": 4 * 10**9}


def total(value):
    count = lax.axis_size("vel")
    step = 1
    while step < count:
        value = value + lax.ppermute(value, "vel", [(i, i ^ step) for i in range(count)])
        step *= 2
    return value


def exchange(send):
    count = lax.axis_size("space")
    forward = [(i, (i + 1) % count) for i in range(count)]
    backward = [(target, source) for source, target in forward]
    if count == 2:
        return [lax.ppermute(send, "space", forward)]
    half = send.shape[0] // 2
    return [
        lax.ppermute(send[:half], "space", forward),
        lax.ppermute(send[half:], "space", backward),
    ]


def on_device(dist, wall_temp, neighbours, wall_mask, face_rows):
    cells, width = dist.shape
    count, half = cells // 2, width // 2
    temp = wall_temp[None, :]
    whole, plane = ((cells, width), F32), ((cells, half), F32)
    every = flux_start(FACES)
    columns = pltpu.VMEM((cells, LANES), F32)

    dist, sent = call(
        near_plane_kernel,
        [whole, plane],
        [
            pltpu.with_memory_space_constraint(face_rows, pltpu.HBM),
            pltpu.with_memory_space_constraint(dist, pltpu.HBM),
        ],
        [
            pltpu.SMEM(face_rows.shape, jnp.int32),
            pltpu.SemaphoreType.DMA(()),
            pltpu.SemaphoreType.DMA((width // HALF,)),
        ],
        unread=(0, 1),
    )
    near = exchange(sent)
    (sums,) = call(sums_kernel, [((every, cells), F32)], [dist])
    sums = total(sums)
    shape, back, side, notes = call(
        wall_kernel,
        [whole, ((8, cells), F32), ((2 * cells, cells), BF16), ((NOTES, cells), F32)],
        [face_rows, temp, wall_mask],
    )
    (stream,) = call(stream_kernel, [whole], [neighbours, wall_mask, dist])
    (sent,) = call(
        share_kernel,
        [((2 * (2 * SUMS + NOTES), count), F32)],
        [face_rows, sums, notes, stream],
        unread=(3,),
    )
    shared = exchange(sent)
    part_shape = ((cells, half // PARTS), F32)
    far_rows = call(far_plane_kernel, [part_shape] * PARTS, [face_rows, dist], scalars=1)
    far = []
    for part in range(PARTS):
        rows = far_rows[part]
        if part:
            (rows,) = call(
                pass_kernel,
                [part_shape],
                [rows, sent],
                far_outs=True,
                unread=(0, 1),
                aliases={0: 0},
            )
        far.append(exchange(rows))
    (middle,) = call(
        middle_kernel,
        [whole],
        [sums, back, side, dist, stream, shape, *near],
        [columns, pltpu.VMEM((cells, width), F32)],
    )
    (part_sum,) = call(stream_last_kernel, [whole], [neighbours, wall_mask, dist, middle])
    halo_parts = call(halo_stream_kernel, [plane] * 4, [face_rows, neighbours, *near])
    (sums_two,) = call(
        advance_kernel,
        [((SUMS, cells), F32)],
        [face_rows, neighbours, part_sum, halo_parts[0], wall_mask, sums, back, *shared],
        unread=(2, 3),
    )
    (part_sum,) = call(relax_kernel, [whole], [sums_two, back, middle, part_sum, shape], [columns])
    plane_one, gate = call(
        halo_relax_kernel, [plane, ((cells, LANES), F32)], [*halo_parts, *shared], [columns]
    )
    result = []
    for part in range(PARTS):
        result = call(
            functools.partial(last_kernel, part),
            [whole],
            [side, part_sum, plane_one, gate, *result, *far[part]],
            [
                pltpu.VMEM((cells, width), F32),
                pltpu.SemaphoreType.DMA((width // COLUMN_TILE // PARTS,)),
            ],
            far_outs=True,
            unread=(4,) if part else (),
            aliases={4: 0} if part else None,
        )
    return result[0]


def solution(mesh):
    return jax.shard_map(
        on_device,
        mesh=mesh,
        in_specs=(
            P("space", "vel"),
            P("space"),
            P(None, "space"),
            P(None, "space"),
            P("space", None, None),
        ),
        out_specs=P("space", "vel"),
        check_vma=False,
    )
```
